32 devices in a mesh: groups: 2 (over y), tm: 4 (over z), band: 2 (over x), pol: 2 (over core).
Axes of the slice: x: 2, y: 2, z: 4, core: 2. Of those that a mesh axis runs over, the one named last changes fastest.
Arguments:
- signal: float32 [16, 2, 2, 16384], P(('groups', 'band'), 'pol', None, 'tm'), parts along dimension 0, may hold values from -3 to 3
- cotangent: float32 [16, 2, 2, 16384], P(('groups', 'band'), 'pol', None, 'tm'), parts along dimension 0, may hold values from -6 to 6
- taps: float32 [2, 8, 2, 128], P(None, 'band'), may hold values from -0.375 to 0.375
- gains: float32 [2, 8], P(None, 'band'), may hold values from 0.005 to 0.02
- walk_off: int32 [2, 8], P(None, 'band'), may hold values from 0 to 2048, as said below
- tap_shift: int32 [2, 8], P(None, 'band'), may hold values from -64 to 64, as said below
Outputs:
- grad_signal: float32 [16, 2, 2, 16384], P(('groups', 'band'), 'pol', None, 'tm'), parts along dimension 0
- grad_taps: float32 [4, 8, 2, 128], P('groups', 'band'), parts along dimension 0
The draws below stay inside these ranges and needn't reach their ends.
There are 2 independent parts, one for each index of `groups`. The reference program is written for one: setup_inputs(seed, part) draws one part's arguments, and reference() takes and returns one part's arrays. A program takes and returns all parts, laid end to end along the dimension named above; an argument that names none is the same for every part. Nothing has to cross between parts.
Inputs may be any that keep to these rules, and one draw needn't show every extreme that they name: `walk_off`: in every step the delay is 0 at one end subband and 2048 at the other, and rises or falls roughly evenly with the subband index. `tap_shift`: in every step some subband has 64 and another has minus 64.
All inputs are finite; a program needn't handle non-finite values.
Results may differ from the reference program's by a relative error of at most 0.00011.
Values sent between devices are 32-bit elements; how exact they have to be, the bound alone decides.
No kernel may reach another device: no remote copies, remote signals or barrier semaphores. Data moves between devices by JAX's collectives and lax.ppermute only.
A program may use at most 64 MiB of HBM per device.

```python
import math
import jax
import jax.numpy as jnp
from jax import lax

POLS = 2
TAPS = 128
STEPS = 2
DMAX = 2048
OFF = 64
BANDS = 8
TIME = 16384


def draw_walk_off(key, part):
    first, second = jax.random.split(jax.random.fold_in(key, 11))
    index = jnp.arange(BANDS, dtype=jnp.int32)[None, :]
    base = index * DMAX // (BANDS - 1)
    spread = max(DMAX // (4 * (BANDS - 1)), 1)
    jitter = jax.random.randint(first, (STEPS, BANDS), -spread, spread + 1)
    delays = jnp.clip(base + jitter, 0, DMAX)
    delays = jnp.where(index == 0, 0, jnp.where(index == BANDS - 1, DMAX, delays))
    flip = jax.random.randint(second, (STEPS, 1), 0, 2)
    return jnp.where(flip == 1, DMAX - delays, delays).astype(jnp.int32)


def draw_tap_shift(key, part):
    first, second = jax.random.split(jax.random.fold_in(key, 23))
    values = jax.random.randint(first, (STEPS, BANDS), -OFF, OFF + 1)
    orders = jax.vmap(lambda k: jax.random.permutation(k, BANDS))(jax.random.split(second, STEPS))
    index = jnp.arange(BANDS, dtype=jnp.int32)[None, :]
    values = jnp.where(index == orders[:, 0:1], OFF, values)
    values = jnp.where(index == orders[:, 1:2], -OFF, values)
    return values.astype(jnp.int32)


def level_of(key, dims, shards, low, high):
    def one(axis_at, shards_of):
        draws = jax.random.uniform(jax.random.fold_in(jax.random.fold_in(key, 6), axis_at), (shards_of,), jnp.float32, low / len(shards), high / len(shards))
        return jnp.repeat(jnp.exp(draws), dims[axis_at] // shards_of).reshape((-1,) + (1,) * (len(dims) - axis_at - 1))

    factor_of = one(*shards[0])
    for cut in shards[1:]:
        factor_of = factor_of * one(*cut)
    return factor_of


def normal_values(key, shape, scale, most, pieces=(), kind=jnp.bfloat16):
    array = jax.random.normal(key, shape, jnp.float32) * scale
    if len(pieces) > 0:
        array = level_of(key, shape, pieces, -0.22, 0.18) * array
    return jnp.clip(array, min=-most, max=most).astype(kind)


def setup_inputs(seed: int = 0, part: int = 0) -> dict:
    key_of = jax.random.split(jax.random.key(seed), 7)
    part_keys = jax.random.split(jax.random.fold_in(key_of[6], part), 7)
    return {
        "signal": normal_values(part_keys[0], (BANDS, POLS, 2, TIME), 0.5, 3.0, ((0, 2), (1, 2), (3, 4)), jnp.float32),
        "cotangent": normal_values(part_keys[1], (BANDS, POLS, 2, TIME), 1.0, 6.0, ((0, 2), (1, 2), (3, 4)), jnp.float32),
        "taps": normal_values(key_of[2], (STEPS, BANDS, 2, TAPS), (2 * TAPS) ** -0.5, 0.375, ((1, 2),), jnp.float32),
        "gains": jnp.clip(jnp.exp(math.log(0.02) - 1.3862944 * jax.random.uniform(key_of[3], (STEPS, BANDS), jnp.float32) ** level_of(key_of[3], (STEPS, BANDS), ((1, 2),), -0.2, 0.2)), 0.005, 0.02),
        "walk_off": draw_walk_off(jax.random.fold_in(key_of[6], 71), part),
        "tap_shift": draw_tap_shift(jax.random.fold_in(key_of[6], 71), part),
    }


highest = lax.Precision.HIGHEST

def toeplitz(vector):
    width = vector.shape[-1]
    rows = width // 3
    lead = vector.shape[:-1]
    padded = jnp.concatenate([vector, jnp.zeros(lead + (1,), vector.dtype)], -1)
    tiled = jnp.broadcast_to(padded[..., None, :], lead + (rows, width + 1)).reshape(lead + (rows * (width + 1),))
    return tiled[..., :rows * width].reshape(lead + (rows, width))

def complex_matrix(table):
    real_part = table[:, 0]
    imag_part = table[:, 1]
    return jnp.stack([jnp.stack([real_part, imag_part], 1), jnp.stack([-imag_part, real_part], 1)], 1)

def selector(offset, count, dtype):
    places = jnp.arange(2 * count, dtype=jnp.int32)[None, :, None]
    index = jnp.arange(count, dtype=jnp.int32)[None, None, :]
    return (places == index + count // 2 + offset[:, None, None]).astype(dtype)

def fir(field, weights, offset):
    count = weights.shape[-1]
    effective = jnp.einsum('bmk,bck->bcm', selector(offset, count, weights.dtype), weights, precision=highest)
    ahead = jnp.concatenate([effective, jnp.zeros((effective.shape[0], 2, count), weights.dtype)], -1)
    matrix = complex_matrix(toeplitz(ahead))
    padded = jnp.pad(field, ((0, 0), (0, 0), (0, 0), (count, count)))
    blocks = TIME // count

    def one_band(pair):
        rows, table = pair
        parts = [rows[..., s * count:s * count + TIME].reshape(POLS, 2, blocks, count) for s in range(3)]
        windows = jnp.concatenate(parts, -1)
        result = jnp.einsum('pcnj,cdij->pdni', windows, table, precision=highest)
        return result.reshape(POLS, 2, TIME)
    return lax.map(one_band, (padded, matrix))

def nonlinear(linear, gain, delay):
    power = lax.optimization_barrier(jnp.sum(linear[:, :, 0] ** 2 + linear[:, :, 1] ** 2, 1))
    padded = jnp.pad(power, ((0, 0), (DMAX, 0)))
    shifted = jax.vmap(lambda row, d: lax.dynamic_slice_in_dim(row, DMAX - d, TIME))(padded, delay)
    spread = lax.optimization_barrier(jnp.sum(shifted, 0))
    extended = jnp.pad(spread, (0, DMAX))
    read = jax.vmap(lambda d: lax.dynamic_slice_in_dim(extended, d, TIME))(delay)
    phase = gain[:, None] * read
    cosine = jnp.cos(phase)[:, None]
    sine = jnp.sin(phase)[:, None]
    real_part = linear[:, :, 0]
    imag_part = linear[:, :, 1]
    return jnp.stack([real_part * cosine - imag_part * sine, real_part * sine + imag_part * cosine], 2)

def reference(signal, cotangent, taps, gains, walk_off, tap_shift):

    def forward(field, weights):
        for step in range(STEPS):
            field = nonlinear(fir(field, weights[step], tap_shift[step]), gains[step], walk_off[step])
        return field
    output, pullback = jax.vjp(forward, signal, taps)
    grad_signal, grad_taps = pullback(cotangent)
    return (grad_signal, grad_taps / math.sqrt(2.0 * TIME))
```

```python
import functools
import math

import jax
import jax.numpy as jnp
from jax import lax
from jax.experimental import pallas as pl
from jax.experimental.pallas import tpu as pltpu
from jax.sharding import PartitionSpec as P

LANES = 128
REACH = 2048 // LANES
EDGE = 4
PAD = 8
F32 = jnp.float32
BF16 = jnp.bfloat16

TWO_OVER_PI = 2.0 / math.pi
HALF_PI_1 = 1.5625
HALF_PI_2 = 67.0 / 8192.0
HALF_PI_3 = 123.0 / 1048576.0
HALF_PI_4 = math.pi / 2.0 - HALF_PI_1 - HALF_PI_2 - HALF_PI_3


def split(x):
    high = x.astype(BF16)
    return high, (x - high.astype(F32)).astype(BF16)


def sine_cosine(x):
    turns = jnp.floor(x * TWO_OVER_PI + 0.5)
    quadrant = turns.astype(jnp.int32)
    r = x - turns * HALF_PI_1
    r = r - turns * HALF_PI_2
    r = r - turns * HALF_PI_3
    r = r - turns * HALF_PI_4
    r2 = r * r
    s = r + r * r2 * (-1.6666654611e-1 + r2 * (8.3321608736e-3 + r2 * -1.9515295891e-4))
    c = 1.0 - 0.5 * r2 + r2 * r2 * (
        4.166664568298827e-2 + r2 * (-1.388731625493765e-3 + r2 * 2.443315711809948e-5)
    )
    odd = (quadrant & 1) == 1
    sine = jnp.where(odd, c, s)
    cosine = jnp.where(odd, s, c)
    sine = jnp.where((quadrant & 2) == 2, -sine, sine)
    cosine = jnp.where(((quadrant + 1) & 2) == 2, -cosine, cosine)
    return sine, cosine


def lanes_of(shape):
    return lax.broadcasted_iota(jnp.int32, shape, len(shape) - 1)


def later(x, amount):
    rolled = pltpu.roll(x, amount & (LANES - 1), 1)
    return jnp.where(lanes_of(x.shape) >= amount, rolled, pltpu.roll(rolled, 1, 0))


def earlier(x, amount):
    rows = x.shape[0]
    rolled = pltpu.roll(x, (LANES - amount) & (LANES - 1), 1)
    follow = pltpu.roll(rolled, rows - 1, 0)
    return jnp.where(lanes_of(x.shape) + amount < LANES, rolled, follow)


def is_even():
    return lax.rem(lax.axis_index("tm"), 2) == 0


def keep_inside(values, rows):
    z = lax.axis_index("tm")
    row = lax.broadcasted_iota(jnp.int32, values.shape, 0)
    low = jnp.where(z == 0, PAD, 0)
    high = jnp.where(z == lax.axis_size("tm") - 1, PAD + rows, 2 * PAD + rows)
    return jnp.where((row >= low) & (row < high), values, 0.0)


def extend(out, own, even_in, odd_in, first):
    bands, _, rows, _ = own.shape
    even = is_even()
    for b in range(bands):
        for c in range(2):
            e = even_in[b, c, first : first + EDGE, :]
            o = odd_in[b, c, first : first + EDGE, :]
            out[b, c, 0:PAD, :] = jnp.zeros((PAD, LANES), F32)
            out[b, c, PAD - EDGE : PAD, :] = jnp.where(even, o, e)
            out[b, c, PAD : PAD + rows, :] = own[b, c]
            out[b, c, PAD + rows :, :] = jnp.zeros((PAD, LANES), F32)
            out[b, c, PAD + rows : PAD + rows + EDGE, :] = jnp.where(even, e, o)


def fir(real, imag, high, low):
    rows = real.shape[0]
    x = jnp.concatenate(
        [real, pltpu.roll(real, rows - 1, 0), imag, pltpu.roll(imag, rows - 1, 0)], 1
    )
    xh, xl = split(x)
    contract = (((1,), (1,)), ((), ()))
    both = lax.dot_general(jnp.concatenate([xh, xl], 0), high, contract, preferred_element_type=F32)
    rest = lax.dot_general(xh, low, contract, preferred_element_type=F32)
    y = both[:rows] + both[rows:] + rest
    return y[:, :LANES], y[:, LANES:]


def fir_adjoint(real, imag, high, low):
    rows = real.shape[0]
    xh, xl = split(jnp.concatenate([real, imag], 1))
    both = jnp.dot(jnp.concatenate([xh, xl], 0), high, preferred_element_type=F32)
    rest = jnp.dot(xh, low, preferred_element_type=F32)
    g = both[:rows] + both[rows:] + rest
    out_real = g[:, :LANES] + pltpu.roll(g[:, LANES : 2 * LANES], 1, 0)
    out_imag = g[:, 2 * LANES : 3 * LANES] + pltpu.roll(g[:, 3 * LANES :], 1, 0)
    return out_real, out_imag


def scatter_delayed(values, delays, step, held, out):
    bands = len(values)
    rows = values[0].shape[0]
    total = rows + REACH
    base = REACH + 8
    lane = lanes_of((total, LANES))
    acc = None
    for b in range(bands):
        delay = delays[step, b]
        q = lax.shift_right_logical(delay, 7)
        s = delay & (LANES - 1)
        held[b, 0:base, :] = jnp.zeros((base, LANES), F32)
        held[b, base : base + rows, :] = pltpu.roll(values[b], s, 1)
        held[b, base + rows :, :] = jnp.zeros((held.shape[1] - base - rows, LANES), F32)
        near = held[b, pl.ds(base - q, total), :]
        far = held[b, pl.ds(base - q - 1, total), :]
        part = jnp.where(lane >= s, near, far)
        acc = part if acc is None else acc + part
    out[...] = acc


def gather_spread(own, even_in, odd_in, spread, rows):
    even = is_even()
    e, o = even_in[...], odd_in[...]
    before = jnp.where(even, o, e)
    after = jnp.where(even, e, o)
    width = REACH + PAD
    total = rows + REACH + 2 * PAD
    spread[0:PAD, :] = before[rows - PAD : rows]
    spread[PAD:total - PAD, :] = own[...]
    spread[total - PAD : total, :] = after[REACH : REACH + PAD]
    spread[PAD : PAD + REACH, :] += before[rows : rows + REACH]
    spread[PAD + rows : PAD + rows + REACH, :] += after[0:REACH]
    values = spread[...]
    row = lax.broadcasted_iota(jnp.int32, values.shape, 0)
    last = lax.axis_index("tm") == lax.axis_size("tm") - 1
    return jnp.where(row < jnp.where(last, PAD + rows, total), values, 0.0)


def read_spread(values, delay, held, b, rows):
    total = values.shape[0]
    q = lax.shift_right_logical(delay, 7)
    s = delay & (LANES - 1)
    held[b, 0:total, :] = pltpu.roll(values, (LANES - s) & (LANES - 1), 1)
    held[b, total:, :] = jnp.zeros((held.shape[1] - total, LANES), F32)
    count = rows + 2 * PAD
    near = held[b, pl.ds(q, count), :]
    far = held[b, pl.ds(q + 1, count), :]
    return jnp.where(lanes_of((count, LANES)) + s < LANES, near, far)


def k_rows(signal, cotangent, sig_rows, cot_rows, even_out, odd_out):
    bands = signal.shape[0]
    rows = sig_rows.shape[2]
    even = is_even()
    for source, target, first in ((signal, sig_rows, 0), (cotangent, cot_rows, EDGE)):
        for b in range(bands):
            for r in range(rows):
                pair = source[b, 0, :, r * LANES : (r + 1) * LANES]
                target[b, 0, r : r + 1, :] = pair[0:1]
                target[b, 1, r : r + 1, :] = pair[1:2]
            for c in range(2):
                left = target[b, c, 0:EDGE, :]
                right = target[b, c, rows - EDGE : rows, :]
                even_out[b, c, first : first + EDGE, :] = jnp.where(even, right, left)
                odd_out[b, c, first : first + EDGE, :] = jnp.where(even, left, right)


def k_tables(taps, *tables):
    steps, bands = taps.shape[:2]
    shape = (LANES, LANES)
    diagonal = lanes_of(shape) >= lax.broadcasted_iota(jnp.int32, shape, 0)
    for step in range(steps):
        high, low = tables[2 * step : 2 * step + 2]
        for b in range(bands):
            for c in range(2):
                row = jnp.broadcast_to(taps[step, b, c : c + 1, :], shape)
                ring = pltpu.roll(row, 0, 1, stride=1, stride_axis=0)
                first = jnp.where(diagonal, ring, 0.0)
                for place, half in ((0, first), (1, ring - first)):
                    for target, value in zip((high, low), split(half)):
                        a = place * LANES
                        d = (2 + place) * LANES
                        if c == 0:
                            target[b, 0:LANES, a : a + LANES] = value
                            target[b, LANES:, d : d + LANES] = value
                        else:
                            target[b, LANES:, a : a + LANES] = value
                            target[b, 0:LANES, d : d + LANES] = -value


def k_first(delays, shifts, sig_rows, even_in, odd_in, high, low, shifted, linear, out, ext, held):
    bands, _, rows, _ = sig_rows.shape
    extend(ext, sig_rows, even_in, odd_in, 0)
    powers = []
    for b in range(bands):
        amount = LANES // 2 - shifts[0, b]
        real = later(ext[b, 0], amount)
        imag = later(ext[b, 1], amount)
        shifted[b, 0] = real
        shifted[b, 1] = imag
        lr, li = fir(real, imag, high[b], low[b])
        linear[b, 0] = lr
        linear[b, 1] = li
        lr, li = lr[PAD : PAD + rows], li[PAD : PAD + rows]
        powers.append(lr * lr + li * li)
    scatter_delayed(powers, delays, 0, held, out)


def k_second(
    delays, shifts, gains, linear0, own, even_in, odd_in, high, low,
    cosine0, sine0, field1, shifted, linear1, out, spread, held, held_out,
):
    bands = linear0.shape[0]
    rows = linear0.shape[2] - 2 * PAD
    values = gather_spread(own, even_in, odd_in, spread, rows)
    powers = []
    for b in range(bands):
        phase = gains[0, b] * read_spread(values, delays[0, b], held, b, rows)
        sine, cosine = sine_cosine(phase)
        cosine0[b] = cosine
        sine0[b] = sine
        lr, li = linear0[b, 0], linear0[b, 1]
        fr = keep_inside(lr * cosine - li * sine, rows)
        fi = keep_inside(lr * sine + li * cosine, rows)
        field1[b, 0] = fr
        field1[b, 1] = fi
        amount = LANES // 2 - shifts[1, b]
        real = later(fr, amount)
        imag = later(fi, amount)
        shifted[b, 0] = real
        shifted[b, 1] = imag
        lr, li = fir(real, imag, high[b], low[b])
        linear1[b, 0] = lr
        linear1[b, 1] = li
        lr, li = lr[PAD : PAD + rows], li[PAD : PAD + rows]
        powers.append(lr * lr + li * li)
    scatter_delayed(powers, delays, 1, held_out, out)


def k_third(
    delays, gains, linear1, own, even_in, odd_in, cot_rows, even_edge, odd_edge,
    turned1, out, ext, spread, held, held_out,
):
    bands = linear1.shape[0]
    rows = linear1.shape[2] - 2 * PAD
    extend(ext, cot_rows, even_edge, odd_edge, EDGE)
    values = gather_spread(own, even_in, odd_in, spread, rows)
    terms = []
    for b in range(bands):
        phase = gains[1, b] * read_spread(values, delays[1, b], held, b, rows)
        sine, cosine = sine_cosine(phase)
        gr, gi = ext[b, 0], ext[b, 1]
        er = gr * cosine + gi * sine
        ei = gi * cosine - gr * sine
        turned1[b, 0] = er
        turned1[b, 1] = ei
        term = ei * linear1[b, 0] - er * linear1[b, 1]
        terms.append(gains[1, b] * term[PAD : PAD + rows])
    scatter_delayed(terms, delays, 1, held_out, out)


def k_fourth(
    delays, shifts, gains, turned1, linear1, own, even_in, odd_in, high, low, cosine0, sine0, field1,
    grad1, turned0, out, spread, held, held_out,
):
    bands = linear1.shape[0]
    rows = linear1.shape[2] - 2 * PAD
    values = gather_spread(own, even_in, odd_in, spread, rows)
    terms = []
    for b in range(bands):
        twice = 2.0 * read_spread(values, delays[1, b], held, b, rows)
        gr = keep_inside(turned1[b, 0] + linear1[b, 0] * twice, rows)
        gi = keep_inside(turned1[b, 1] + linear1[b, 1] * twice, rows)
        grad1[b, 0] = gr
        grad1[b, 1] = gi
        gr, gi = fir_adjoint(gr, gi, high[b], low[b])
        amount = LANES // 2 - shifts[1, b]
        gr = earlier(gr, amount)
        gi = earlier(gi, amount)
        cosine, sine = cosine0[b], sine0[b]
        turned0[b, 0] = gr * cosine + gi * sine
        turned0[b, 1] = gi * cosine - gr * sine
        term = gi * field1[b, 0] - gr * field1[b, 1]
        terms.append(gains[0, b] * term[PAD : PAD + rows])
    scatter_delayed(terms, delays, 0, held_out, out)


def correlate(real, imag, grad_real, grad_imag, rows):
    inside = slice(PAD, PAD + rows)
    following = slice(PAD + 1, PAD + rows + 1)
    a = jnp.concatenate(
        [
            jnp.concatenate([real[inside], real[following]], 1),
            jnp.concatenate([imag[inside], imag[following]], 1),
        ],
        0,
    )
    gr, gi = grad_real[inside], grad_imag[inside]
    d = jnp.concatenate([jnp.concatenate([gr, gi], 1), jnp.concatenate([gi, -gr], 1)], 0)
    ah, al = split(a)
    dh, dl = split(d)
    table = lax.dot_general(
        jnp.concatenate([dh, dh, dl], 0),
        jnp.concatenate([ah, al, ah], 0),
        (((0,), (0,)), ((), ())),
        preferred_element_type=F32,
    )
    width = 2 * LANES
    results = []
    for c in range(2):
        acc = table[c * LANES : c * LANES + 8]
        for g in range(1, LANES // 8):
            first = c * LANES + 8 * g
            acc = acc + pltpu.roll(table[first : first + 8], width - 8 * g, 1)
        total = acc[0:1]
        for s in range(1, 8):
            total = total + pltpu.roll(acc, width - s, 1)[s : s + 1]
        results.append(total[:, :LANES])
    return results


def k_taps(shifted, grad, out):
    bands = grad.shape[0]
    rows = grad.shape[2] - 2 * PAD
    for b in range(bands):
        parts = correlate(shifted[b, 0], shifted[b, 1], grad[b, 0], grad[b, 1], rows)
        for c in range(2):
            out[2 * b + c : 2 * b + c + 1, :] = parts[c]


def k_fifth(
    scale, delays, turned0, linear0, own, even_in, odd_in, shifted, taps1,
    grad0, out, spread, held,
):
    bands = linear0.shape[0]
    rows = linear0.shape[2] - 2 * PAD
    values = gather_spread(own, even_in, odd_in, spread, rows)
    for b in range(bands):
        twice = 2.0 * read_spread(values, delays[0, b], held, b, rows)
        gr = keep_inside(turned0[b, 0] + linear0[b, 0] * twice, rows)
        gi = keep_inside(turned0[b, 1] + linear0[b, 1] * twice, rows)
        grad0[b, 0] = gr
        grad0[b, 1] = gi
        parts = correlate(shifted[b, 0], shifted[b, 1], gr, gi, rows)
        for c in range(2):
            out[2 * b + c : 2 * b + c + 1, :] = parts[c] * scale
    out[2 * bands :, :] = taps1[...] * scale


def k_last(shifts, grad0, high, low, result):
    bands = grad0.shape[0]
    rows = grad0.shape[2] - 2 * PAD
    for b in range(bands):
        gr, gi = fir_adjoint(grad0[b, 0], grad0[b, 1], high[b], low[b])
        amount = LANES // 2 - shifts[0, b]
        gr = earlier(gr, amount)[PAD : PAD + rows]
        gi = earlier(gi, amount)[PAD : PAD + rows]
        for r in range(rows):
            result[b, 0, 0:1, r * LANES : (r + 1) * LANES] = gr[r : r + 1]
            result[b, 0, 1:2, r * LANES : (r + 1) * LANES] = gi[r : r + 1]


def call(kernel, scalars, arrays, shapes, scratch=(), micros=2.0):
    smem = pl.BlockSpec(memory_space=pltpu.SMEM)
    vmem = pl.BlockSpec(memory_space=pltpu.VMEM)
    return pl.pallas_call(
        kernel,
        out_shape=shapes,
        in_specs=[smem] * len(scalars) + [vmem] * len(arrays),
        out_specs=[vmem] * len(shapes),
        scratch_shapes=[pltpu.VMEM(s, F32) for s in scratch],
        compiler_params=pltpu.CompilerParams(vmem_limit_bytes=24 * 1024 * 1024),
        cost_estimate=pl.CostEstimate(
            flops=int(micros * 1e8), bytes_accessed=int(micros * 3e6), transcendentals=0
        ),
    )(*scalars, *arrays)


def swapped(x, axis, distance):
    size = lax.axis_size(axis)
    return lax.ppermute(x, axis, [(i, i ^ distance) for i in range(size)])


def summed(x, axis):
    size = lax.axis_size(axis)
    if size & (size - 1):
        return lax.psum(x, axis)
    distance = 1
    while distance < size:
        x = x + swapped(x, axis, distance)
        distance *= 2
    return x


def neighbours(even_out, odd_out):
    size = lax.axis_size("tm")
    evens = [(i, i ^ 1) for i in range(size) if (i ^ 1) < size]
    odds = [(i, ((i + 1) ^ 1) - 1) for i in range(size)]
    odds = [(i, j) for i, j in odds if 0 <= j < size]
    return lax.ppermute(even_out, "tm", evens), lax.ppermute(odd_out, "tm", odds)


def exchanged(part):
    part = summed(part, "pol")
    part = summed(part, "band")
    return (part,) + neighbours(part, part)


def on_device(signal, cotangent, taps, gains, walk_off, tap_shift):
    bands, _, _, length = signal.shape
    steps = taps.shape[0]
    rows = length // LANES
    held_rows = rows + 2 * PAD

    def shape(*dims, dtype=F32):
        return jax.ShapeDtypeStruct(dims, dtype)

    own = shape(bands, 2, rows, LANES)
    field = shape(bands, 2, held_rows, LANES)
    angle = shape(bands, held_rows, LANES)
    edge = shape(bands, 2, 2 * EDGE, LANES)
    part = shape(rows + REACH, LANES)
    table = shape(bands, 2 * LANES, 4 * LANES, dtype=BF16)
    ext = (bands, 2, held_rows, LANES)
    spread = (rows + REACH + 2 * PAD, LANES)
    held_in = (bands, rows + REACH + 3 * PAD, LANES)
    held_out = (bands, rows + 3 * REACH, LANES)

    sig_rows, cot_rows, even_out, odd_out = call(
        k_rows, (), (signal, cotangent), [own, own, edge, edge]
    )
    even_edge, odd_edge = neighbours(even_out, odd_out)
    taps, even_out = lax.optimization_barrier((taps, even_out))
    high0, low0, high1, low1 = call(k_tables, (), (taps,), [table] * (2 * steps))
    shifted0, linear0, sent = call(
        k_first, (walk_off, tap_shift), (sig_rows, even_edge, odd_edge, high0, low0),
        [field, field, part], (ext, held_out),
    )
    cosine0, sine0, field1, shifted1, linear1, sent = call(
        k_second, (walk_off, tap_shift, gains), (linear0, *exchanged(sent), high1, low1),
        [angle, angle, field, field, field, part], (spread, held_in, held_out),
    )
    turned1, sent = call(
        k_third, (walk_off, gains),
        (linear1, *exchanged(sent), cot_rows, even_edge, odd_edge),
        [field, part], (ext, spread, held_in, held_out),
    )
    grad1, turned0, sent = call(
        k_fourth, (walk_off, tap_shift, gains),
        (turned1, linear1, *exchanged(sent), high1, low1, cosine0, sine0, field1),
        [field, field, part], (spread, held_in, held_out),
    )
    (taps1,) = call(k_taps, (), (shifted1, grad1), [shape(2 * bands, LANES)])
    scale = 1.0 / math.sqrt(2.0 * length * lax.axis_size("tm"))
    grad0, grad_taps = call(
        functools.partial(k_fifth, scale),
        (walk_off,), (turned0, linear0, *exchanged(sent), shifted0, taps1),
        [field, shape(steps * 2 * bands, LANES)], (spread, held_in),
    )
    (grad_signal,) = call(
        k_last, (tap_shift,), (grad0, high0, low0), [shape(bands, 1, 2, length)]
    )
    grad_taps = summed(summed(grad_taps, "pol"), "tm")
    return grad_signal, grad_taps.reshape(steps, bands, 2, LANES)


def solution(mesh):
    return jax.shard_map(
        on_device,
        mesh=mesh,
        in_specs=(
            P(("groups", "band"), "pol", None, "tm"),
            P(("groups", "band"), "pol", None, "tm"),
            P(None, "band", None, None),
            P(None, "band"),
            P(None, "band"),
            P(None, "band"),
        ),
        out_specs=(P(("groups", "band"), "pol", None, "tm"), P("groups", "band", None, None)),
        check_vma=False,
    )
```

```python
import functools
import math

import jax
import jax.numpy as jnp
from jax import lax
from jax.experimental import pallas as pl
from jax.experimental.pallas import tpu as pltpu
from jax.sharding import PartitionSpec as P

LANES = 128
REACH = 2048 // LANES
EDGE = 4
PAD = 8
F32 = jnp.float32
BF16 = jnp.bfloat16

TWO_OVER_PI = 2.0 / math.pi
HALF_PI_1 = 1.5625
HALF_PI_2 = 67.0 / 8192.0
HALF_PI_3 = 123.0 / 1048576.0
HALF_PI_4 = math.pi / 2.0 - HALF_PI_1 - HALF_PI_2 - HALF_PI_3


def split(x):
    high = x.astype(BF16)
    return high, (x - high.astype(F32)).astype(BF16)


def sine_cosine(x):
    turns = jnp.floor(x * TWO_OVER_PI + 0.5)
    quadrant = turns.astype(jnp.int32)
    r = x - turns * HALF_PI_1
    r = r - turns * HALF_PI_2
    r = r - turns * HALF_PI_3
    r = r - turns * HALF_PI_4
    r2 = r * r
    s = r + r * r2 * (-1.6666654611e-1 + r2 * (8.3321608736e-3 + r2 * -1.9515295891e-4))
    c = 1.0 - 0.5 * r2 + r2 * r2 * (
        4.166664568298827e-2 + r2 * (-1.388731625493765e-3 + r2 * 2.443315711809948e-5)
    )
    odd = (quadrant & 1) == 1
    sine = jnp.where(odd, c, s)
    cosine = jnp.where(odd, s, c)
    sine = jnp.where((quadrant & 2) == 2, -sine, sine)
    cosine = jnp.where(((quadrant + 1) & 2) == 2, -cosine, cosine)
    return sine, cosine


def lanes_of(shape):
    return lax.broadcasted_iota(jnp.int32, shape, len(shape) - 1)


def later(x, amount):
    rolled = pltpu.roll(x, amount & (LANES - 1), 1)
    return jnp.where(lanes_of(x.shape) >= amount, rolled, pltpu.roll(rolled, 1, 0))


def earlier(x, amount):
    rows = x.shape[0]
    rolled = pltpu.roll(x, (LANES - amount) & (LANES - 1), 1)
    follow = pltpu.roll(rolled, rows - 1, 0)
    return jnp.where(lanes_of(x.shape) + amount < LANES, rolled, follow)


def is_even():
    return lax.rem(lax.axis_index("tm"), 2) == 0


def keep_inside(values, rows):
    z = lax.axis_index("tm")
    row = lax.broadcasted_iota(jnp.int32, values.shape, 0)
    low = jnp.where(z == 0, PAD, 0)
    high = jnp.where(z == lax.axis_size("tm") - 1, PAD + rows, 2 * PAD + rows)
    return jnp.where((row >= low) & (row < high), values, 0.0)


def from_sides(even_value, odd_value):
    z = lax.axis_index("tm")
    even = is_even()
    before = jnp.where(even, odd_value, even_value)
    after = jnp.where(even, even_value, odd_value)
    before = jnp.where(z == 0, 0.0, before)
    after = jnp.where(z == lax.axis_size("tm") - 1, 0.0, after)
    return before, after


def extend(out, own, even_in, odd_in, first):
    bands, _, rows, _ = own.shape
    for b in range(bands):
        for c in range(2):
            before, after = from_sides(
                even_in[b, c, first : first + EDGE, :], odd_in[b, c, first : first + EDGE, :]
            )
            out[b, c, 0:PAD, :] = jnp.zeros((PAD, LANES), F32)
            out[b, c, PAD - EDGE : PAD, :] = before
            out[b, c, PAD : PAD + rows, :] = own[b, c]
            out[b, c, PAD + rows :, :] = jnp.zeros((PAD, LANES), F32)
            out[b, c, PAD + rows : PAD + rows + EDGE, :] = after


def fir(real, imag, high, low):
    rows = real.shape[0]
    x = jnp.concatenate(
        [real, pltpu.roll(real, rows - 1, 0), imag, pltpu.roll(imag, rows - 1, 0)], 1
    )
    xh, xl = split(x)
    contract = (((1,), (1,)), ((), ()))
    both = lax.dot_general(jnp.concatenate([xh, xl], 0), high, contract, preferred_element_type=F32)
    rest = lax.dot_general(xh, low, contract, preferred_element_type=F32)
    y = both[:rows] + both[rows:] + rest
    return y[:, :LANES], y[:, LANES:]


def fir_adjoint(real, imag, high, low):
    rows = real.shape[0]
    xh, xl = split(jnp.concatenate([real, imag], 1))
    both = jnp.dot(jnp.concatenate([xh, xl], 0), high, preferred_element_type=F32)
    rest = jnp.dot(xh, low, preferred_element_type=F32)
    g = both[:rows] + both[rows:] + rest
    out_real = g[:, :LANES] + pltpu.roll(g[:, LANES : 2 * LANES], 1, 0)
    out_imag = g[:, 2 * LANES : 3 * LANES] + pltpu.roll(g[:, 3 * LANES :], 1, 0)
    return out_real, out_imag


def scatter_delayed(values, delays, step, held, out):
    bands = len(values)
    rows = values[0].shape[0]
    total = rows + REACH
    base = REACH + 8
    lane = lanes_of((total, LANES))
    acc = None
    for b in range(bands):
        delay = delays[step, b]
        q = lax.shift_right_logical(delay, 7)
        s = delay & (LANES - 1)
        held[b, 0:base, :] = jnp.zeros((base, LANES), F32)
        held[b, base : base + rows, :] = pltpu.roll(values[b], s, 1)
        held[b, base + rows :, :] = jnp.zeros((held.shape[1] - base - rows, LANES), F32)
        near = held[b, pl.ds(base - q, total), :]
        far = held[b, pl.ds(base - q - 1, total), :]
        part = jnp.where(lane >= s, near, far)
        acc = part if acc is None else acc + part
    out[...] = acc


def gather_spread(own, even_in, odd_in, spread, rows):
    before, after = from_sides(even_in[...], odd_in[...])
    total = rows + REACH + 2 * PAD
    spread[0:PAD, :] = before[rows - PAD : rows]
    spread[PAD:total - PAD, :] = own[...]
    spread[total - PAD : total, :] = after[REACH : REACH + PAD]
    spread[PAD : PAD + REACH, :] += before[rows : rows + REACH]
    spread[PAD + rows : PAD + rows + REACH, :] += after[0:REACH]
    values = spread[...]
    row = lax.broadcasted_iota(jnp.int32, values.shape, 0)
    last = lax.axis_index("tm") == lax.axis_size("tm") - 1
    return jnp.where(row < jnp.where(last, PAD + rows, total), values, 0.0)


def read_spread(values, delay, held, b, rows):
    total = values.shape[0]
    q = lax.shift_right_logical(delay, 7)
    s = delay & (LANES - 1)
    held[b, 0:total, :] = pltpu.roll(values, (LANES - s) & (LANES - 1), 1)
    held[b, total:, :] = jnp.zeros((held.shape[1] - total, LANES), F32)
    count = rows + 2 * PAD
    near = held[b, pl.ds(q, count), :]
    far = held[b, pl.ds(q + 1, count), :]
    return jnp.where(lanes_of((count, LANES)) + s < LANES, near, far)


def k_rows(signal, cotangent, sig_rows, cot_rows, even_out, odd_out, sig_held, cot_held, done):
    bands = signal.shape[0]
    rows = sig_rows.shape[2]
    even = is_even()
    copies = (
        pltpu.make_async_copy(signal, sig_held, done.at[0]),
        pltpu.make_async_copy(cotangent, cot_held, done.at[1]),
    )
    for copy in copies:
        copy.start()
    for copy, source, target, first in (
        (copies[0], sig_held, sig_rows, 0),
        (copies[1], cot_held, cot_rows, EDGE),
    ):
        copy.wait()
        for b in range(bands):
            for r in range(rows):
                pair = source[b, 0, :, r * LANES : (r + 1) * LANES]
                target[b, 0, r : r + 1, :] = pair[0:1]
                target[b, 1, r : r + 1, :] = pair[1:2]
            for c in range(2):
                left = target[b, c, 0:EDGE, :]
                right = target[b, c, rows - EDGE : rows, :]
                even_out[b, c, first : first + EDGE, :] = jnp.where(even, right, left)
                odd_out[b, c, first : first + EDGE, :] = jnp.where(even, left, right)


def k_tables(taps, delays, shifts, gains, delays_out, shifts_out, gains_out, *tables):
    steps, bands = taps.shape[:2]
    delays_out[...] = delays[...]
    shifts_out[...] = shifts[...]
    gains_out[...] = gains[...]
    shape = (LANES, LANES)
    diagonal = lanes_of(shape) >= lax.broadcasted_iota(jnp.int32, shape, 0)
    for step in range(steps):
        high, low = tables[2 * step : 2 * step + 2]
        for b in range(bands):
            for c in range(2):
                row = jnp.broadcast_to(taps[step, b, c : c + 1, :], shape)
                ring = pltpu.roll(row, 0, 1, stride=1, stride_axis=0)
                first = jnp.where(diagonal, ring, 0.0)
                for place, half in ((0, first), (1, ring - first)):
                    for target, value in zip((high, low), split(half)):
                        a = place * LANES
                        d = (2 + place) * LANES
                        if c == 0:
                            target[b, 0:LANES, a : a + LANES] = value
                            target[b, LANES:, d : d + LANES] = value
                        else:
                            target[b, LANES:, a : a + LANES] = value
                            target[b, 0:LANES, d : d + LANES] = -value


def k_first(delays, shifts, sig_rows, even_in, odd_in, high, low, shifted, linear, out, ext, held):
    bands, _, rows, _ = sig_rows.shape
    extend(ext, sig_rows, even_in, odd_in, 0)
    powers = []
    for b in range(bands):
        amount = LANES // 2 - shifts[0, b]
        real = later(ext[b, 0], amount)
        imag = later(ext[b, 1], amount)
        shifted[b, 0] = real
        shifted[b, 1] = imag
        lr, li = fir(real, imag, high[b], low[b])
        linear[b, 0] = lr
        linear[b, 1] = li
        lr, li = lr[PAD : PAD + rows], li[PAD : PAD + rows]
        powers.append(lr * lr + li * li)
    scatter_delayed(powers, delays, 0, held, out)


def k_second(
    delays, shifts, gains, linear0, own, even_in, odd_in, high, low,
    cosine0, sine0, field1, shifted, linear1, out, spread, held, held_out,
):
    bands = linear0.shape[0]
    rows = linear0.shape[2] - 2 * PAD
    values = gather_spread(own, even_in, odd_in, spread, rows)
    powers = []
    for b in range(bands):
        phase = gains[0, b] * read_spread(values, delays[0, b], held, b, rows)
        sine, cosine = sine_cosine(phase)
        cosine0[b] = cosine
        sine0[b] = sine
        lr, li = linear0[b, 0], linear0[b, 1]
        fr = keep_inside(lr * cosine - li * sine, rows)
        fi = keep_inside(lr * sine + li * cosine, rows)
        field1[b, 0] = fr
        field1[b, 1] = fi
        amount = LANES // 2 - shifts[1, b]
        real = later(fr, amount)
        imag = later(fi, amount)
        shifted[b, 0] = real
        shifted[b, 1] = imag
        lr, li = fir(real, imag, high[b], low[b])
        linear1[b, 0] = lr
        linear1[b, 1] = li
        lr, li = lr[PAD : PAD + rows], li[PAD : PAD + rows]
        powers.append(lr * lr + li * li)
    scatter_delayed(powers, delays, 1, held_out, out)


def k_third(
    delays, gains, linear1, own, even_in, odd_in, cot_rows, even_edge, odd_edge,
    turned1, out, ext, spread, held, held_out,
):
    bands = linear1.shape[0]
    rows = linear1.shape[2] - 2 * PAD
    extend(ext, cot_rows, even_edge, odd_edge, EDGE)
    values = gather_spread(own, even_in, odd_in, spread, rows)
    terms = []
    for b in range(bands):
        phase = gains[1, b] * read_spread(values, delays[1, b], held, b, rows)
        sine, cosine = sine_cosine(phase)
        gr, gi = ext[b, 0], ext[b, 1]
        er = gr * cosine + gi * sine
        ei = gi * cosine - gr * sine
        turned1[b, 0] = er
        turned1[b, 1] = ei
        term = ei * linear1[b, 0] - er * linear1[b, 1]
        terms.append(gains[1, b] * term[PAD : PAD + rows])
    scatter_delayed(terms, delays, 1, held_out, out)


def k_fourth(
    delays, shifts, gains, turned1, linear1, own, even_in, odd_in, high, low, cosine0, sine0, field1,
    grad1, turned0, out, spread, held, held_out,
):
    bands = linear1.shape[0]
    rows = linear1.shape[2] - 2 * PAD
    values = gather_spread(own, even_in, odd_in, spread, rows)
    terms = []
    for b in range(bands):
        twice = 2.0 * read_spread(values, delays[1, b], held, b, rows)
        gr = keep_inside(turned1[b, 0] + linear1[b, 0] * twice, rows)
        gi = keep_inside(turned1[b, 1] + linear1[b, 1] * twice, rows)
        grad1[b, 0] = gr
        grad1[b, 1] = gi
        gr, gi = fir_adjoint(gr, gi, high[b], low[b])
        amount = LANES // 2 - shifts[1, b]
        gr = earlier(gr, amount)
        gi = earlier(gi, amount)
        cosine, sine = cosine0[b], sine0[b]
        turned0[b, 0] = gr * cosine + gi * sine
        turned0[b, 1] = gi * cosine - gr * sine
        term = gi * field1[b, 0] - gr * field1[b, 1]
        terms.append(gains[0, b] * term[PAD : PAD + rows])
    scatter_delayed(terms, delays, 0, held_out, out)


def correlate(real, imag, grad_real, grad_imag, rows):
    inside = slice(PAD, PAD + rows)
    following = slice(PAD + 1, PAD + rows + 1)
    a = jnp.concatenate(
        [
            jnp.concatenate([real[inside], real[following]], 1),
            jnp.concatenate([imag[inside], imag[following]], 1),
        ],
        0,
    )
    gr, gi = grad_real[inside], grad_imag[inside]
    d = jnp.concatenate([jnp.concatenate([gr, gi], 1), jnp.concatenate([gi, -gr], 1)], 0)
    ah, al = split(a)
    dh, dl = split(d)
    table = lax.dot_general(
        jnp.concatenate([dh, dh, dl], 0),
        jnp.concatenate([ah, al, ah], 0),
        (((0,), (0,)), ((), ())),
        preferred_element_type=F32,
    )
    width = 2 * LANES
    results = []
    for c in range(2):
        acc = table[c * LANES : c * LANES + 8]
        for g in range(1, LANES // 8):
            first = c * LANES + 8 * g
            acc = acc + pltpu.roll(table[first : first + 8], width - 8 * g, 1)
        total = acc[0:1]
        for s in range(1, 8):
            total = total + pltpu.roll(acc, width - s, 1)[s : s + 1]
        results.append(total[:, :LANES])
    return results


def k_taps(shifted, grad, out):
    bands = grad.shape[0]
    rows = grad.shape[2] - 2 * PAD
    for b in range(bands):
        parts = correlate(shifted[b, 0], shifted[b, 1], grad[b, 0], grad[b, 1], rows)
        for c in range(2):
            out[2 * b + c : 2 * b + c + 1, :] = parts[c]


def k_fifth(
    scale, delays, turned0, linear0, own, even_in, odd_in, shifted, taps1,
    grad0, out, spread, held,
):
    bands = linear0.shape[0]
    rows = linear0.shape[2] - 2 * PAD
    values = gather_spread(own, even_in, odd_in, spread, rows)
    for b in range(bands):
        twice = 2.0 * read_spread(values, delays[0, b], held, b, rows)
        gr = keep_inside(turned0[b, 0] + linear0[b, 0] * twice, rows)
        gi = keep_inside(turned0[b, 1] + linear0[b, 1] * twice, rows)
        grad0[b, 0] = gr
        grad0[b, 1] = gi
        parts = correlate(shifted[b, 0], shifted[b, 1], gr, gi, rows)
        for c in range(2):
            out[2 * b + c : 2 * b + c + 1, :] = parts[c] * scale
    out[2 * bands :, :] = taps1[...] * scale


def k_last(shifts, grad0, high, low, result):
    bands = grad0.shape[0]
    rows = grad0.shape[2] - 2 * PAD
    for b in range(bands):
        gr, gi = fir_adjoint(grad0[b, 0], grad0[b, 1], high[b], low[b])
        amount = LANES // 2 - shifts[0, b]
        gr = earlier(gr, amount)[PAD : PAD + rows]
        gi = earlier(gi, amount)[PAD : PAD + rows]
        for r in range(rows):
            result[b, 0, 0:1, r * LANES : (r + 1) * LANES] = gr[r : r + 1]
            result[b, 0, 1:2, r * LANES : (r + 1) * LANES] = gi[r : r + 1]


def call(kernel, scalars, arrays, shapes, scratch=(), micros=2.0):
    smem = pl.BlockSpec(memory_space=pltpu.SMEM)
    vmem = pl.BlockSpec(memory_space=pltpu.VMEM)
    return pl.pallas_call(
        kernel,
        out_shape=shapes,
        in_specs=[smem] * len(scalars) + [vmem] * len(arrays),
        out_specs=[vmem] * len(shapes),
        scratch_shapes=[pltpu.VMEM(s, F32) for s in scratch],
        compiler_params=pltpu.CompilerParams(vmem_limit_bytes=24 * 1024 * 1024),
        cost_estimate=pl.CostEstimate(
            flops=int(micros * 1e8), bytes_accessed=int(micros * 3e6), transcendentals=0
        ),
    )(*scalars, *arrays)


def swapped(x, axis, partner, cross):
    size, cores = lax.axis_size(axis), lax.axis_size("pol")
    pairs = []
    for i in range(size):
        for p in range(cores):
            j, q = partner(i), cores - 1 - p
            if 0 <= j < size:
                pairs.append((i * cores + p, j * cores + (q if cross else p)))
            else:
                pairs.append((i * cores + p, i * cores + q))
    return lax.ppermute(x, (axis, "pol"), pairs)


def summed(x, axis, cross=True):
    size = lax.axis_size(axis)
    if size & (size - 1):
        return lax.psum(x, axis)
    distance = 1
    while distance < size:
        x = x + swapped(x, axis, lambda i, d=distance: i ^ d, cross)
        distance *= 2
    return x


def over_cores(x):
    cores = lax.axis_size("pol")
    return x + lax.ppermute(x, "pol", [(p, cores - 1 - p) for p in range(cores)])


def neighbours(even_out, odd_out, cross):
    odd_in = swapped(odd_out, "tm", lambda i: ((i + 1) ^ 1) - 1, cross)
    even_in = swapped(even_out, "tm", lambda i: i ^ 1, cross)
    return even_in, odd_in


def exchanged(part):
    part = summed(over_cores(part), "band")
    return (part,) + neighbours(part, part, True)


def on_device(signal, cotangent, taps, gains, walk_off, tap_shift):
    bands, _, _, length = signal.shape
    steps = taps.shape[0]
    rows = length // LANES
    held_rows = rows + 2 * PAD

    def shape(*dims, dtype=F32):
        return jax.ShapeDtypeStruct(dims, dtype)

    own = shape(bands, 2, rows, LANES)
    field = shape(bands, 2, held_rows, LANES)
    angle = shape(bands, held_rows, LANES)
    edge = shape(bands, 2, 2 * EDGE, LANES)
    part = shape(rows + REACH, LANES)
    table = shape(bands, 2 * LANES, 4 * LANES, dtype=BF16)
    ext = (bands, 2, held_rows, LANES)
    spread = (rows + REACH + 2 * PAD, LANES)
    held_in = (bands, rows + REACH + 3 * PAD, LANES)
    held_out = (bands, rows + 3 * REACH, LANES)

    whole = pltpu.VMEM((bands, 1, 2, length), F32)
    vmem = pl.BlockSpec(memory_space=pltpu.VMEM)
    sig_rows, cot_rows, even_out, odd_out = pl.pallas_call(
        k_rows,
        out_shape=[own, own, edge, edge],
        in_specs=[pl.BlockSpec(memory_space=pltpu.HBM)] * 2,
        out_specs=[vmem] * 4,
        scratch_shapes=[whole, whole, pltpu.SemaphoreType.DMA((2,))],
        compiler_params=pltpu.CompilerParams(vmem_limit_bytes=24 * 1024 * 1024),
    )(signal, cotangent)
    even_edge, odd_edge = neighbours(even_out, odd_out, False)
    taps, even_out = lax.optimization_barrier((taps, even_out))
    small = [shape(*a.shape, dtype=a.dtype) for a in (walk_off, tap_shift, gains)]
    walk_off, tap_shift, gains, high0, low0, high1, low1 = call(
        k_tables, (), (taps, walk_off, tap_shift, gains), small + [table] * (2 * steps)
    )
    shifted0, linear0, sent = call(
        k_first, (walk_off, tap_shift), (sig_rows, even_edge, odd_edge, high0, low0),
        [field, field, part], (ext, held_out),
    )
    cosine0, sine0, field1, shifted1, linear1, sent = call(
        k_second, (walk_off, tap_shift, gains), (linear0, *exchanged(sent), high1, low1),
        [angle, angle, field, field, field, part], (spread, held_in, held_out),
    )
    turned1, sent = call(
        k_third, (walk_off, gains),
        (linear1, *exchanged(sent), cot_rows, even_edge, odd_edge),
        [field, part], (ext, spread, held_in, held_out),
    )
    grad1, turned0, sent = call(
        k_fourth, (walk_off, tap_shift, gains),
        (turned1, linear1, *exchanged(sent), high1, low1, cosine0, sine0, field1),
        [field, field, part], (spread, held_in, held_out),
    )
    (taps1,) = call(k_taps, (), (shifted1, grad1), [shape(2 * bands, LANES)])
    scale = 1.0 / math.sqrt(2.0 * length * lax.axis_size("tm"))
    grad0, grad_taps = call(
        functools.partial(k_fifth, scale),
        (walk_off,), (turned0, linear0, *exchanged(sent), shifted0, taps1),
        [field, shape(steps * 2 * bands, LANES)], (spread, held_in),
    )
    (grad_signal,) = call(
        k_last, (tap_shift,), (grad0, high0, low0), [shape(bands, 1, 2, length)]
    )
    grad_taps = summed(over_cores(grad_taps), "tm")
    return grad_signal, grad_taps.reshape(steps, bands, 2, LANES)


def solution(mesh):
    return jax.shard_map(
        on_device,
        mesh=mesh,
        in_specs=(
            P(("groups", "band"), "pol", None, "tm"),
            P(("groups", "band"), "pol", None, "tm"),
            P(None, "band", None, None),
            P(None, "band"),
            P(None, "band"),
            P(None, "band"),
        ),
        out_specs=(P(("groups", "band"), "pol", None, "tm"), P("groups", "band", None, None)),
        check_vma=False,
    )
```

```python
import functools
import math

import jax
import jax.numpy as jnp
from jax import lax
from jax.experimental import pallas as pl
from jax.experimental.pallas import tpu as pltpu
from jax.sharding import PartitionSpec as P

LANES = 128
REACH = 2048 // LANES
EDGE = 4
WIDE = REACH + 4
PAD = 8
WIDE_PAD = REACH + PAD
F32 = jnp.float32
BF16 = jnp.bfloat16

TWO_OVER_PI = 2.0 / math.pi
HALF_PI_1 = 1.5625
HALF_PI_2 = 67.0 / 8192.0
HALF_PI_3 = 123.0 / 1048576.0
HALF_PI_4 = math.pi / 2.0 - HALF_PI_1 - HALF_PI_2 - HALF_PI_3


def split(x):
    high = x.astype(BF16)
    return high, (x - high.astype(F32)).astype(BF16)


def sine_cosine(x):
    turns = jnp.floor(x * TWO_OVER_PI + 0.5)
    quadrant = turns.astype(jnp.int32)
    r = x - turns * HALF_PI_1
    r = r - turns * HALF_PI_2
    r = r - turns * HALF_PI_3
    r = r - turns * HALF_PI_4
    r2 = r * r
    s = r + r * r2 * (-1.6666654611e-1 + r2 * (8.3321608736e-3 + r2 * -1.9515295891e-4))
    c = 1.0 - 0.5 * r2 + r2 * r2 * (
        4.166664568298827e-2 + r2 * (-1.388731625493765e-3 + r2 * 2.443315711809948e-5)
    )
    odd = (quadrant & 1) == 1
    sine = jnp.where(odd, c, s)
    cosine = jnp.where(odd, s, c)
    sine = jnp.where((quadrant & 2) == 2, -sine, sine)
    cosine = jnp.where(((quadrant + 1) & 2) == 2, -cosine, cosine)
    return sine, cosine


def lanes_of(shape):
    return lax.broadcasted_iota(jnp.int32, shape, len(shape) - 1)


def later(x, amount):
    rolled = pltpu.roll(x, amount & (LANES - 1), 1)
    return jnp.where(lanes_of(x.shape) >= amount, rolled, pltpu.roll(rolled, 1, 0))


def earlier(x, amount):
    rows = x.shape[0]
    rolled = pltpu.roll(x, (LANES - amount) & (LANES - 1), 1)
    follow = pltpu.roll(rolled, rows - 1, 0)
    return jnp.where(lanes_of(x.shape) + amount < LANES, rolled, follow)


def is_even():
    return lax.rem(lax.axis_index("tm"), 2) == 0


def keep_inside(values, rows, pad=PAD):
    z = lax.axis_index("tm")
    row = lax.broadcasted_iota(jnp.int32, values.shape, 0)
    low = jnp.where(z == 0, pad, 0)
    high = jnp.where(z == lax.axis_size("tm") - 1, pad + rows, 2 * pad + rows)
    return jnp.where((row >= low) & (row < high), values, 0.0)


def from_sides(even_value, odd_value):
    z = lax.axis_index("tm")
    even = is_even()
    before = jnp.where(even, odd_value, even_value)
    after = jnp.where(even, even_value, odd_value)
    before = jnp.where(z == 0, 0.0, before)
    after = jnp.where(z == lax.axis_size("tm") - 1, 0.0, after)
    return before, after


def extend(out, own, even_in, odd_in, first, edge):
    bands, _, rows, _ = own.shape
    pad = (out.shape[2] - rows) // 2
    for b in range(bands):
        for c in range(2):
            out[b, c, 0:pad, :] = jnp.zeros((pad, LANES), F32)
            out[b, c, pad : pad + rows, :] = own[b, c]
            out[b, c, pad + rows :, :] = jnp.zeros((pad, LANES), F32)
        for r in range(edge):
            lanes = slice((first + r) * LANES, (first + r + 1) * LANES)
            before, after = from_sides(even_in[b, :, lanes], odd_in[b, :, lanes])
            for c in range(2):
                above = pad - edge + r
                below = pad + rows + r
                out[b, c, above : above + 1, :] = before[c : c + 1]
                out[b, c, below : below + 1, :] = after[c : c + 1]


def fir(real, imag, high, low):
    rows = real.shape[0]
    x = jnp.concatenate(
        [real, pltpu.roll(real, rows - 1, 0), imag, pltpu.roll(imag, rows - 1, 0)], 1
    )
    xh, xl = split(x)
    contract = (((1,), (1,)), ((), ()))
    both = lax.dot_general(jnp.concatenate([xh, xl], 0), high, contract, preferred_element_type=F32)
    rest = lax.dot_general(xh, low, contract, preferred_element_type=F32)
    y = both[:rows] + both[rows:] + rest
    return y[:, :LANES], y[:, LANES:]


def fir_adjoint(real, imag, high, low):
    rows = real.shape[0]
    xh, xl = split(jnp.concatenate([real, imag], 1))
    both = jnp.dot(jnp.concatenate([xh, xl], 0), high, preferred_element_type=F32)
    rest = jnp.dot(xh, low, preferred_element_type=F32)
    g = both[:rows] + both[rows:] + rest
    out_real = g[:, :LANES] + pltpu.roll(g[:, LANES : 2 * LANES], 1, 0)
    out_imag = g[:, 2 * LANES : 3 * LANES] + pltpu.roll(g[:, 3 * LANES :], 1, 0)
    return out_real, out_imag


def scatter_delayed(values, delays, step, held, out):
    bands = len(values)
    rows = values[0].shape[0]
    total = rows + REACH
    base = REACH + 8
    lane = lanes_of((total, LANES))
    acc = None
    for b in range(bands):
        delay = delays[step, b]
        q = lax.shift_right_logical(delay, 7)
        s = delay & (LANES - 1)
        held[b, 0:base, :] = jnp.zeros((base, LANES), F32)
        held[b, base : base + rows, :] = pltpu.roll(values[b], s, 1)
        held[b, base + rows :, :] = jnp.zeros((held.shape[1] - base - rows, LANES), F32)
        near = held[b, pl.ds(base - q, total), :]
        far = held[b, pl.ds(base - q - 1, total), :]
        part = jnp.where(lane >= s, near, far)
        acc = part if acc is None else acc + part
    out[...] = acc


def delayed_sum(values, delays, step, held, out):
    bands = len(values)
    count, total = values[0].shape[0], out.shape[0]
    lane = lanes_of((total, LANES))
    acc = None
    for b in range(bands):
        delay = delays[step, b]
        q = lax.shift_right_logical(delay, 7)
        s = delay & (LANES - 1)
        held[b, 0:8, :] = jnp.zeros((8, LANES), F32)
        held[b, 8 : 8 + count, :] = pltpu.roll(values[b], s, 1)
        near = held[b, pl.ds(8 + REACH - q, total), :]
        far = held[b, pl.ds(8 + REACH - q - 1, total), :]
        part = jnp.where(lane >= s, near, far)
        acc = part if acc is None else acc + part
    out[...] = acc


def end_at_last(values, rows):
    row = lax.broadcasted_iota(jnp.int32, values.shape, 0)
    last = lax.axis_index("tm") == lax.axis_size("tm") - 1
    return jnp.where(row < jnp.where(last, PAD + rows, values.shape[0]), values, 0.0)


def gather_spread(own, even_in, odd_in, spread, rows):
    before, after = from_sides(even_in[...], odd_in[...])
    total = rows + REACH + 2 * PAD
    spread[0:PAD, :] = before[rows - PAD : rows]
    spread[PAD:total - PAD, :] = own[...]
    spread[total - PAD : total, :] = after[REACH : REACH + PAD]
    spread[PAD : PAD + REACH, :] += before[rows : rows + REACH]
    spread[PAD + rows : PAD + rows + REACH, :] += after[0:REACH]
    return end_at_last(spread[...], rows)


def read_spread(values, delay, held, b, rows):
    total = values.shape[0]
    q = lax.shift_right_logical(delay, 7)
    s = delay & (LANES - 1)
    held[b, 0:total, :] = pltpu.roll(values, (LANES - s) & (LANES - 1), 1)
    held[b, total:, :] = jnp.zeros((held.shape[1] - total, LANES), F32)
    count = rows + 2 * PAD
    near = held[b, pl.ds(q, count), :]
    far = held[b, pl.ds(q + 1, count), :]
    return jnp.where(lanes_of((count, LANES)) + s < LANES, near, far)


def k_setup(
    signal, cotangent, taps, delays, shifts, gains,
    sig_rows, cot_rows, delays_out, shifts_out, gains_out, *tables,
):
    steps, bands = taps.shape[:2]
    rows = sig_rows.shape[2]
    for source, target in ((signal, sig_rows), (cotangent, cot_rows)):
        for b in range(bands):
            for r in range(rows):
                pair = source[b, 0, :, r * LANES : (r + 1) * LANES]
                target[b, 0, r : r + 1, :] = pair[0:1]
                target[b, 1, r : r + 1, :] = pair[1:2]
    delays_out[...] = delays[...]
    shifts_out[...] = shifts[...]
    gains_out[...] = gains[...]
    shape = (LANES, LANES)
    diagonal = lanes_of(shape) >= lax.broadcasted_iota(jnp.int32, shape, 0)
    for step in range(steps):
        high, low = tables[2 * step : 2 * step + 2]
        for b in range(bands):
            for c in range(2):
                row = jnp.broadcast_to(taps[step, b, c : c + 1, :], shape)
                ring = pltpu.roll(row, 0, 1, stride=1, stride_axis=0)
                first = jnp.where(diagonal, ring, 0.0)
                for place, half in ((0, first), (1, ring - first)):
                    for target, value in zip((high, low), split(half)):
                        a = place * LANES
                        d = (2 + place) * LANES
                        if c == 0:
                            target[b, 0:LANES, a : a + LANES] = value
                            target[b, LANES:, d : d + LANES] = value
                        else:
                            target[b, LANES:, a : a + LANES] = value
                            target[b, 0:LANES, d : d + LANES] = -value


def k_first(delays, shifts, sig_rows, even_in, odd_in, high, low, shifted, linear, out, ext, held):
    bands, _, rows, _ = sig_rows.shape
    extend(ext, sig_rows, even_in, odd_in, 0, WIDE)
    middle = slice(WIDE_PAD - PAD, WIDE_PAD + rows + PAD)
    powers = []
    for b in range(bands):
        amount = LANES // 2 - shifts[0, b]
        real = later(ext[b, 0], amount)
        imag = later(ext[b, 1], amount)
        shifted[b, 0] = real[middle]
        shifted[b, 1] = imag[middle]
        lr, li = fir(real, imag, high[b], low[b])
        linear[b, 0] = lr[middle]
        linear[b, 1] = li[middle]
        powers.append(keep_inside(lr * lr + li * li, rows, WIDE_PAD))
    delayed_sum(powers, delays, 0, held, out)


def k_second(
    delays, shifts, gains, linear0, own, high, low,
    cosine0, sine0, field1, shifted, linear1, out, held, held_out,
):
    bands = linear0.shape[0]
    rows = linear0.shape[2] - 2 * PAD
    values = end_at_last(own[...], rows)
    powers = []
    for b in range(bands):
        phase = gains[0, b] * read_spread(values, delays[0, b], held, b, rows)
        sine, cosine = sine_cosine(phase)
        cosine0[b] = cosine
        sine0[b] = sine
        lr, li = linear0[b, 0], linear0[b, 1]
        fr = keep_inside(lr * cosine - li * sine, rows)
        fi = keep_inside(lr * sine + li * cosine, rows)
        field1[b, 0] = fr
        field1[b, 1] = fi
        amount = LANES // 2 - shifts[1, b]
        real = later(fr, amount)
        imag = later(fi, amount)
        shifted[b, 0] = real
        shifted[b, 1] = imag
        lr, li = fir(real, imag, high[b], low[b])
        linear1[b, 0] = lr
        linear1[b, 1] = li
        lr, li = lr[PAD : PAD + rows], li[PAD : PAD + rows]
        powers.append(lr * lr + li * li)
    scatter_delayed(powers, delays, 1, held_out, out)


def k_third(
    delays, gains, linear1, own, even_in, odd_in, cot_rows, even_edge, odd_edge,
    turned1, out, ext, spread, held, held_out,
):
    bands = linear1.shape[0]
    rows = linear1.shape[2] - 2 * PAD
    extend(ext, cot_rows, even_edge, odd_edge, WIDE, EDGE)
    values = gather_spread(own, even_in, odd_in, spread, rows)
    terms = []
    for b in range(bands):
        phase = gains[1, b] * read_spread(values, delays[1, b], held, b, rows)
        sine, cosine = sine_cosine(phase)
        gr, gi = ext[b, 0], ext[b, 1]
        er = gr * cosine + gi * sine
        ei = gi * cosine - gr * sine
        turned1[b, 0] = er
        turned1[b, 1] = ei
        term = ei * linear1[b, 0] - er * linear1[b, 1]
        terms.append(gains[1, b] * term[PAD : PAD + rows])
    scatter_delayed(terms, delays, 1, held_out, out)


def k_fourth(
    delays, shifts, gains, turned1, linear1, own, even_in, odd_in, high, low, cosine0, sine0, field1,
    grad1, turned0, out, spread, held, held_out,
):
    bands = linear1.shape[0]
    rows = linear1.shape[2] - 2 * PAD
    values = gather_spread(own, even_in, odd_in, spread, rows)
    terms = []
    for b in range(bands):
        twice = 2.0 * read_spread(values, delays[1, b], held, b, rows)
        gr = keep_inside(turned1[b, 0] + linear1[b, 0] * twice, rows)
        gi = keep_inside(turned1[b, 1] + linear1[b, 1] * twice, rows)
        grad1[b, 0] = gr
        grad1[b, 1] = gi
        gr, gi = fir_adjoint(gr, gi, high[b], low[b])
        amount = LANES // 2 - shifts[1, b]
        gr = earlier(gr, amount)
        gi = earlier(gi, amount)
        cosine, sine = cosine0[b], sine0[b]
        turned0[b, 0] = gr * cosine + gi * sine
        turned0[b, 1] = gi * cosine - gr * sine
        term = gi * field1[b, 0] - gr * field1[b, 1]
        terms.append(gains[0, b] * term[PAD : PAD + rows])
    scatter_delayed(terms, delays, 0, held_out, out)


def correlate(real, imag, grad_real, grad_imag, rows):
    inside = slice(PAD, PAD + rows)
    following = slice(PAD + 1, PAD + rows + 1)
    a = jnp.concatenate(
        [
            jnp.concatenate([real[inside], real[following]], 1),
            jnp.concatenate([imag[inside], imag[following]], 1),
        ],
        0,
    )
    gr, gi = grad_real[inside], grad_imag[inside]
    d = jnp.concatenate([jnp.concatenate([gr, gi], 1), jnp.concatenate([gi, -gr], 1)], 0)
    ah, al = split(a)
    dh, dl = split(d)
    table = lax.dot_general(
        jnp.concatenate([dh, dh, dl], 0),
        jnp.concatenate([ah, al, ah], 0),
        (((0,), (0,)), ((), ())),
        preferred_element_type=F32,
    )
    width = 2 * LANES
    results = []
    for c in range(2):
        acc = table[c * LANES : c * LANES + 8]
        for g in range(1, LANES // 8):
            first = c * LANES + 8 * g
            acc = acc + pltpu.roll(table[first : first + 8], width - 8 * g, 1)
        total = acc[0:1]
        for s in range(1, 8):
            total = total + pltpu.roll(acc, width - s, 1)[s : s + 1]
        results.append(total[:, :LANES])
    return results


def k_taps(shifted, grad, out):
    bands = grad.shape[0]
    rows = grad.shape[2] - 2 * PAD
    for b in range(bands):
        parts = correlate(shifted[b, 0], shifted[b, 1], grad[b, 0], grad[b, 1], rows)
        for c in range(2):
            out[2 * b + c : 2 * b + c + 1, :] = parts[c]


def k_fifth(
    scale, delays, turned0, linear0, own, even_in, odd_in, shifted, taps1,
    grad0, out, spread, held,
):
    bands = linear0.shape[0]
    rows = linear0.shape[2] - 2 * PAD
    values = gather_spread(own, even_in, odd_in, spread, rows)
    for b in range(bands):
        twice = 2.0 * read_spread(values, delays[0, b], held, b, rows)
        gr = keep_inside(turned0[b, 0] + linear0[b, 0] * twice, rows)
        gi = keep_inside(turned0[b, 1] + linear0[b, 1] * twice, rows)
        grad0[b, 0] = gr
        grad0[b, 1] = gi
        parts = correlate(shifted[b, 0], shifted[b, 1], gr, gi, rows)
        for c in range(2):
            out[2 * b + c : 2 * b + c + 1, :] = parts[c] * scale
    out[2 * bands :, :] = taps1[...] * scale


def k_last(shifts, grad0, high, low, result):
    bands = grad0.shape[0]
    rows = grad0.shape[2] - 2 * PAD
    for b in range(bands):
        gr, gi = fir_adjoint(grad0[b, 0], grad0[b, 1], high[b], low[b])
        amount = LANES // 2 - shifts[0, b]
        gr = earlier(gr, amount)[PAD : PAD + rows]
        gi = earlier(gi, amount)[PAD : PAD + rows]
        for r in range(rows):
            result[b, 0, 0:1, r * LANES : (r + 1) * LANES] = gr[r : r + 1]
            result[b, 0, 1:2, r * LANES : (r + 1) * LANES] = gi[r : r + 1]


def call(kernel, scalars, arrays, shapes, scratch=(), micros=2.0):
    vmem = pl.BlockSpec(memory_space=pltpu.VMEM)
    return pl.pallas_call(
        kernel,
        out_shape=shapes,
        in_specs=[vmem] * (len(scalars) + len(arrays)),
        out_specs=[vmem] * len(shapes),
        scratch_shapes=[pltpu.VMEM(s, F32) for s in scratch],
        compiler_params=pltpu.CompilerParams(vmem_limit_bytes=24 * 1024 * 1024),
        cost_estimate=pl.CostEstimate(
            flops=int(micros * 1e8), bytes_accessed=int(micros * 3e6), transcendentals=0
        ),
    )(*scalars, *arrays)


def swapped(x, axis, partner, cross):
    size, cores = lax.axis_size(axis), lax.axis_size("pol")
    pairs = []
    for i in range(size):
        for p in range(cores):
            j, q = partner(i), cores - 1 - p
            if 0 <= j < size:
                pairs.append((i * cores + p, j * cores + (q if cross else p)))
            else:
                pairs.append((i * cores + p, i * cores + q))
    return lax.ppermute(x, (axis, "pol"), pairs)


def summed(x, axis, cross=True):
    size = lax.axis_size(axis)
    if size & (size - 1):
        return lax.psum(x, axis)
    distance = 1
    while distance < size:
        x = x + swapped(x, axis, lambda i, d=distance: i ^ d, cross)
        distance *= 2
    return x


def over_cores(x):
    cores = lax.axis_size("pol")
    return x + lax.ppermute(x, "pol", [(p, cores - 1 - p) for p in range(cores)])


def neighbours(even_out, odd_out, cross):
    odd_in = swapped(odd_out, "tm", lambda i: ((i + 1) ^ 1) - 1, cross)
    even_in = swapped(even_out, "tm", lambda i: i ^ 1, cross)
    return even_in, odd_in


def over_tm(x):
    if lax.axis_size("tm") != 4:
        return summed(x, "tm")
    others = [swapped(x, "tm", lambda i, d=d: i ^ d, True) for d in (1, 2, 3)]
    return (x + others[0]) + (others[1] + others[2])


def over_powers(part):
    return summed(over_cores(part), "band")


def exchanged(part):
    part = over_powers(part)
    return (part,) + neighbours(part, part, True)


def edges(signal, cotangent):
    wide, edge = WIDE * LANES, EDGE * LANES
    left = jnp.concatenate([signal[..., :wide], cotangent[..., :edge]], -1)
    right = jnp.concatenate([signal[..., -wide:], cotangent[..., -edge:]], -1)
    even = is_even()
    return jnp.where(even, right, left), jnp.where(even, left, right)


def on_device(signal, cotangent, taps, gains, walk_off, tap_shift):
    bands, _, _, length = signal.shape
    steps = taps.shape[0]
    rows = length // LANES
    held_rows = rows + 2 * PAD

    def shape(*dims, dtype=F32):
        return jax.ShapeDtypeStruct(dims, dtype)

    own = shape(bands, 2, rows, LANES)
    field = shape(bands, 2, held_rows, LANES)
    angle = shape(bands, held_rows, LANES)
    wide_part = shape(rows + REACH + 2 * PAD, LANES)
    part = shape(rows + REACH, LANES)
    table = shape(bands, 2 * LANES, 4 * LANES, dtype=BF16)
    ext = (bands, 2, held_rows, LANES)
    ext_wide = (bands, 2, rows + 2 * WIDE_PAD, LANES)
    held_wide = (bands, rows + 2 * WIDE_PAD + 8, LANES)
    spread = (rows + REACH + 2 * PAD, LANES)
    held_in = (bands, rows + REACH + 3 * PAD, LANES)
    held_out = (bands, rows + 3 * REACH, LANES)

    even_out, odd_out = edges(signal[:, 0], cotangent[:, 0])
    even_edge, odd_edge = neighbours(even_out, odd_out, False)
    taps, even_out = lax.optimization_barrier((taps, even_out))
    small = [shape(*a.shape, dtype=a.dtype) for a in (walk_off, tap_shift, gains)]
    sig_rows, cot_rows, walk_off, tap_shift, gains, high0, low0, high1, low1 = call(
        k_setup, (), (signal, cotangent, taps, walk_off, tap_shift, gains),
        [own, own] + small + [table] * (2 * steps),
    )
    shifted0, linear0, sent = call(
        k_first, (walk_off, tap_shift), (sig_rows, even_edge, odd_edge, high0, low0),
        [field, field, wide_part], (ext_wide, held_wide),
    )
    cosine0, sine0, field1, shifted1, linear1, sent = call(
        k_second, (walk_off, tap_shift, gains), (linear0, over_powers(sent), high1, low1),
        [angle, angle, field, field, field, part], (held_in, held_out),
    )
    turned1, sent = call(
        k_third, (walk_off, gains),
        (linear1, *exchanged(sent), cot_rows, even_edge, odd_edge),
        [field, part], (ext, spread, held_in, held_out),
    )
    grad1, turned0, sent = call(
        k_fourth, (walk_off, tap_shift, gains),
        (turned1, linear1, *exchanged(sent), high1, low1, cosine0, sine0, field1),
        [field, field, part], (spread, held_in, held_out),
    )
    (taps1,) = call(k_taps, (), (shifted1, grad1), [shape(2 * bands, LANES)])
    scale = 1.0 / math.sqrt(2.0 * length * lax.axis_size("tm"))
    grad0, grad_taps = call(
        functools.partial(k_fifth, scale),
        (walk_off,), (turned0, linear0, *exchanged(sent), shifted0, taps1),
        [field, shape(steps * 2 * bands, LANES)], (spread, held_in),
    )
    (grad_signal,) = call(
        k_last, (tap_shift,), (grad0, high0, low0), [shape(bands, 1, 2, length)]
    )
    grad_taps = over_tm(over_cores(grad_taps))
    return grad_signal, grad_taps.reshape(steps, bands, 2, LANES)


def solution(mesh):
    return jax.shard_map(
        on_device,
        mesh=mesh,
        in_specs=(
            P(("groups", "band"), "pol", None, "tm"),
            P(("groups", "band"), "pol", None, "tm"),
            P(None, "band", None, None),
            P(None, "band"),
            P(None, "band"),
            P(None, "band"),
        ),
        out_specs=(P(("groups", "band"), "pol", None, "tm"), P("groups", "band", None, None)),
        check_vma=False,
    )
```

```python
import functools
import math

import jax
import jax.numpy as jnp
from jax import lax
from jax.experimental import pallas as pl
from jax.experimental.pallas import tpu as pltpu
from jax.sharding import PartitionSpec as P

LANES = 128
REACH = 2048 // LANES
EDGE = 4
WIDE = REACH + 4
PAD = 8
WIDE_PAD = REACH + PAD
F32 = jnp.float32
BF16 = jnp.bfloat16

TWO_OVER_PI = 2.0 / math.pi
HALF_PI_1 = 1.5625
HALF_PI_2 = 67.0 / 8192.0
HALF_PI_3 = 123.0 / 1048576.0
HALF_PI_4 = math.pi / 2.0 - HALF_PI_1 - HALF_PI_2 - HALF_PI_3


def split(x):
    high = x.astype(BF16)
    return high, (x - high.astype(F32)).astype(BF16)


def sine_cosine(x):
    turns = jnp.floor(x * TWO_OVER_PI + 0.5)
    quadrant = turns.astype(jnp.int32)
    r = x - turns * HALF_PI_1
    r = r - turns * HALF_PI_2
    r = r - turns * HALF_PI_3
    r = r - turns * HALF_PI_4
    r2 = r * r
    s = r + r * r2 * (-1.6666654611e-1 + r2 * (8.3321608736e-3 + r2 * -1.9515295891e-4))
    c = 1.0 - 0.5 * r2 + r2 * r2 * (
        4.166664568298827e-2 + r2 * (-1.388731625493765e-3 + r2 * 2.443315711809948e-5)
    )
    odd = (quadrant & 1) == 1
    sine = jnp.where(odd, c, s)
    cosine = jnp.where(odd, s, c)
    sine = jnp.where((quadrant & 2) == 2, -sine, sine)
    cosine = jnp.where(((quadrant + 1) & 2) == 2, -cosine, cosine)
    return sine, cosine


def lanes_of(shape):
    return lax.broadcasted_iota(jnp.int32, shape, len(shape) - 1)


def later(x, amount):
    rolled = pltpu.roll(x, amount & (LANES - 1), 1)
    return jnp.where(lanes_of(x.shape) >= amount, rolled, pltpu.roll(rolled, 1, 0))


def earlier(x, amount):
    rows = x.shape[0]
    rolled = pltpu.roll(x, (LANES - amount) & (LANES - 1), 1)
    follow = pltpu.roll(rolled, rows - 1, 0)
    return jnp.where(lanes_of(x.shape) + amount < LANES, rolled, follow)


def at(table, step, b):
    own = table.shape[2]
    return table[b // own, step, b % own]


def is_even():
    return lax.rem(lax.axis_index("tm"), 2) == 0


def keep_inside(values, rows, pad=PAD):
    z = lax.axis_index("tm")
    row = lax.broadcasted_iota(jnp.int32, values.shape, 0)
    low = jnp.where(z == 0, pad, 0)
    high = jnp.where(z == lax.axis_size("tm") - 1, pad + rows, 2 * pad + rows)
    return jnp.where((row >= low) & (row < high), values, 0.0)


def from_sides(even_value, odd_value):
    z = lax.axis_index("tm")
    even = is_even()
    before = jnp.where(even, odd_value, even_value)
    after = jnp.where(even, even_value, odd_value)
    before = jnp.where(z == 0, 0.0, before)
    after = jnp.where(z == lax.axis_size("tm") - 1, 0.0, after)
    return before, after


def extend(out, b, even_in, odd_in, first, edge):
    own = even_in.shape[0]
    rows = out.shape[2]
    pad = edge + 4
    for c in range(2):
        out[b, c, 0:8, :] = jnp.zeros((8, LANES), F32)
        out[b, c, rows - 8 :, :] = jnp.zeros((8, LANES), F32)
    for r in range(edge):
        lanes = slice((first + r) * LANES, (first + r + 1) * LANES)
        before, after = from_sides(even_in[b % own, :, lanes], odd_in[b % own, :, lanes])
        for c in range(2):
            above = pad - edge + r
            below = rows - pad + r
            out[b, c, above : above + 1, :] = before[c : c + 1]
            out[b, c, below : below + 1, :] = after[c : c + 1]


def lay_rows(source, target, b, first, rows):
    own = source.shape[0]
    for r in range(rows):
        pair = source[b % own, 0, :, r * LANES : (r + 1) * LANES]
        for c in range(2):
            target[b, c, first + r : first + r + 1, :] = pair[c : c + 1]


def fir(real, imag, high, low):
    rows = real.shape[0]
    x = jnp.concatenate(
        [real, pltpu.roll(real, rows - 1, 0), imag, pltpu.roll(imag, rows - 1, 0)], 1
    )
    xh, xl = split(x)
    contract = (((1,), (1,)), ((), ()))
    both = lax.dot_general(jnp.concatenate([xh, xl], 0), high, contract, preferred_element_type=F32)
    rest = lax.dot_general(xh, low, contract, preferred_element_type=F32)
    y = both[:rows] + both[rows:] + rest
    return y[:, :LANES], y[:, LANES:]


def fir_adjoint(real, imag, high, low):
    rows = real.shape[0]
    xh, xl = split(jnp.concatenate([real, imag], 1))
    both = jnp.dot(jnp.concatenate([xh, xl], 0), high, preferred_element_type=F32)
    rest = jnp.dot(xh, low, preferred_element_type=F32)
    g = both[:rows] + both[rows:] + rest
    out_real = g[:, :LANES] + pltpu.roll(g[:, LANES : 2 * LANES], 1, 0)
    out_imag = g[:, 2 * LANES : 3 * LANES] + pltpu.roll(g[:, 3 * LANES :], 1, 0)
    return out_real, out_imag


def scatter_delayed(values, delays, step, held, out):
    bands = len(values)
    rows = values[0].shape[0]
    total = rows + REACH
    base = REACH + 8
    lane = lanes_of((total, LANES))
    acc = None
    for b in range(bands):
        delay = at(delays, step, b)
        q = lax.shift_right_logical(delay, 7)
        s = delay & (LANES - 1)
        held[b, 0:base, :] = jnp.zeros((base, LANES), F32)
        held[b, base : base + rows, :] = pltpu.roll(values[b], s, 1)
        held[b, base + rows :, :] = jnp.zeros((held.shape[1] - base - rows, LANES), F32)
        near = held[b, pl.ds(base - q, total), :]
        far = held[b, pl.ds(base - q - 1, total), :]
        part = jnp.where(lane >= s, near, far)
        acc = part if acc is None else acc + part
    out[...] = acc


def delayed_sum(values, delays, step, held, out):
    bands = len(values)
    count, total = values[0].shape[0], out.shape[0]
    lane = lanes_of((total, LANES))
    acc = None
    for b in range(bands):
        delay = at(delays, step, b)
        q = lax.shift_right_logical(delay, 7)
        s = delay & (LANES - 1)
        held[b, 0:8, :] = jnp.zeros((8, LANES), F32)
        held[b, 8 : 8 + count, :] = pltpu.roll(values[b], s, 1)
        near = held[b, pl.ds(8 + REACH - q, total), :]
        far = held[b, pl.ds(8 + REACH - q - 1, total), :]
        part = jnp.where(lane >= s, near, far)
        acc = part if acc is None else acc + part
    out[...] = acc


def end_at_last(values, rows):
    row = lax.broadcasted_iota(jnp.int32, values.shape, 0)
    last = lax.axis_index("tm") == lax.axis_size("tm") - 1
    return jnp.where(row < jnp.where(last, PAD + rows, values.shape[0]), values, 0.0)


def gather_spread(own, even_in, odd_in, spread, rows):
    before, after = from_sides(even_in[...], odd_in[...])
    total = rows + REACH + 2 * PAD
    spread[0:PAD, :] = before[rows - PAD : rows]
    spread[PAD:total - PAD, :] = own[...]
    spread[total - PAD : total, :] = after[REACH : REACH + PAD]
    spread[PAD : PAD + REACH, :] += before[rows : rows + REACH]
    spread[PAD + rows : PAD + rows + REACH, :] += after[0:REACH]
    return end_at_last(spread[...], rows)


def read_spread(values, delay, held, b, rows):
    total = values.shape[0]
    q = lax.shift_right_logical(delay, 7)
    s = delay & (LANES - 1)
    held[b, 0:total, :] = pltpu.roll(values, (LANES - s) & (LANES - 1), 1)
    held[b, total:, :] = jnp.zeros((held.shape[1] - total, LANES), F32)
    count = rows + 2 * PAD
    near = held[b, pl.ds(q, count), :]
    far = held[b, pl.ds(q + 1, count), :]
    return jnp.where(lanes_of((count, LANES)) + s < LANES, near, far)


def k_setup(groups, steps, *refs):
    signals, packs = refs[:groups], refs[groups : 2 * groups]
    sig_rows, delays, shifts, gains = refs[2 * groups : 2 * groups + 4]
    tables = refs[2 * groups + 4 :]
    rows = sig_rows.shape[2]
    own = delays.shape[2]
    shape = (LANES, LANES)
    diagonal = lanes_of(shape) >= lax.broadcasted_iota(jnp.int32, shape, 0)
    first = 2 * steps * own
    for k, pack in enumerate(packs):
        for n, target in enumerate((delays, shifts, gains)):
            row = first + n * steps
            target[k] = pack[row : row + steps, 0:own].astype(target.dtype)
    for b in range(groups * own):
        lay_rows(signals[b // own], sig_rows, b, 0, rows)
        pack = packs[b // own]
        for step in range(steps):
            high, low = tables[2 * step : 2 * step + 2]
            for c in range(2):
                tap = 2 * (step * own + b % own) + c
                row = jnp.broadcast_to(pack[tap : tap + 1, :], shape)
                ring = pltpu.roll(row, 0, 1, stride=1, stride_axis=0)
                near = jnp.where(diagonal, ring, 0.0)
                for place, half in ((0, near), (1, ring - near)):
                    for target, value in zip((high, low), split(half)):
                        a = place * LANES
                        d = (2 + place) * LANES
                        if c == 0:
                            target[b, 0:LANES, a : a + LANES] = value
                            target[b, LANES:, d : d + LANES] = value
                        else:
                            target[b, LANES:, a : a + LANES] = value
                            target[b, 0:LANES, d : d + LANES] = -value


def k_cotangent(groups, *refs):
    out = refs[-1]
    own = refs[0].shape[0]
    rows = out.shape[2] - 2 * PAD
    for b in range(out.shape[0]):
        k = b // own
        extend(out, b, refs[groups + 2 * k], refs[groups + 2 * k + 1], WIDE, EDGE)
        lay_rows(refs[k], out, b, PAD, rows)


def k_first(groups, delays, shifts, sig_rows, *refs):
    sides = refs[: 2 * groups]
    high, low, shifted, linear, out, ext, held = refs[2 * groups :]
    bands, _, rows, _ = sig_rows.shape
    own = shifted.shape[0]
    middle = slice(WIDE_PAD - PAD, WIDE_PAD + rows + PAD)
    powers = []
    for b in range(bands):
        k = b // own
        extend(ext, b, sides[2 * k], sides[2 * k + 1], 0, WIDE)
        for c in range(2):
            ext[b, c, WIDE_PAD : WIDE_PAD + rows, :] = sig_rows[b, c]
        amount = LANES // 2 - at(shifts, 0, b)
        real = later(ext[b, 0], amount)
        imag = later(ext[b, 1], amount)
        if b < own:
            shifted[b, 0] = real[middle]
            shifted[b, 1] = imag[middle]
        lr, li = fir(real, imag, high[b], low[b])
        linear[b, 0] = lr[middle]
        linear[b, 1] = li[middle]
        powers.append(keep_inside(lr * lr + li * li, rows, WIDE_PAD))
    delayed_sum(powers, delays, 0, held, out)


def k_second(
    delays, shifts, gains, linear0, own, high, low,
    cosine0, sine0, field1, shifted, linear1, out, held, held_out,
):
    bands = linear0.shape[0]
    rows = linear0.shape[2] - 2 * PAD
    values = end_at_last(own[...], rows)
    powers = []
    for b in range(bands):
        spread = read_spread(values, at(delays, 0, b), held, b, rows)
        sine, cosine = sine_cosine(at(gains, 0, b) * spread)
        lr, li = linear0[b, 0], linear0[b, 1]
        fr = keep_inside(lr * cosine - li * sine, rows)
        fi = keep_inside(lr * sine + li * cosine, rows)
        field1[b, 0] = fr
        field1[b, 1] = fi
        amount = LANES // 2 - at(shifts, 1, b)
        real = later(fr, amount)
        imag = later(fi, amount)
        if b < shifted.shape[0]:
            cosine0[b] = cosine
            sine0[b] = sine
            shifted[b, 0] = real
            shifted[b, 1] = imag
        lr, li = fir(real, imag, high[b], low[b])
        linear1[b, 0] = lr
        linear1[b, 1] = li
        lr, li = lr[PAD : PAD + rows], li[PAD : PAD + rows]
        powers.append(lr * lr + li * li)
    scatter_delayed(powers, delays, 1, held_out, out)


def k_third(
    delays, gains, linear1, own, even_in, odd_in, cotangent, turned1, out, spread, held, held_out
):
    bands = linear1.shape[0]
    rows = linear1.shape[2] - 2 * PAD
    values = gather_spread(own, even_in, odd_in, spread, rows)
    terms = []
    for b in range(bands):
        gain = at(gains, 1, b)
        phase = gain * read_spread(values, at(delays, 1, b), held, b, rows)
        sine, cosine = sine_cosine(phase)
        gr, gi = cotangent[b, 0], cotangent[b, 1]
        er = gr * cosine + gi * sine
        ei = gi * cosine - gr * sine
        turned1[b, 0] = er
        turned1[b, 1] = ei
        term = ei * linear1[b, 0] - er * linear1[b, 1]
        terms.append(gain * term[PAD : PAD + rows])
    scatter_delayed(terms, delays, 1, held_out, out)


def k_fourth(
    delays, shifts, gains, turned1, linear1, own, even_in, odd_in, high, low, cosine0, sine0, field1,
    grad1, turned0, out, spread, held, held_out,
):
    bands = linear1.shape[0]
    rows = linear1.shape[2] - 2 * PAD
    values = gather_spread(own, even_in, odd_in, spread, rows)
    terms = []
    for b in range(bands):
        twice = 2.0 * read_spread(values, at(delays, 1, b), held, b, rows)
        gr = keep_inside(turned1[b, 0] + linear1[b, 0] * twice, rows)
        gi = keep_inside(turned1[b, 1] + linear1[b, 1] * twice, rows)
        if b < grad1.shape[0]:
            grad1[b, 0] = gr
            grad1[b, 1] = gi
        gr, gi = fir_adjoint(gr, gi, high[b], low[b])
        amount = LANES // 2 - at(shifts, 1, b)
        gr = earlier(gr, amount)
        gi = earlier(gi, amount)
        if b < grad1.shape[0]:
            cosine, sine = cosine0[b], sine0[b]
            turned0[b, 0] = gr * cosine + gi * sine
            turned0[b, 1] = gi * cosine - gr * sine
        term = gi * field1[b, 0] - gr * field1[b, 1]
        terms.append(at(gains, 0, b) * term[PAD : PAD + rows])
    scatter_delayed(terms, delays, 0, held_out, out)


def correlate(real, imag, grad_real, grad_imag, rows):
    inside = slice(PAD, PAD + rows)
    following = slice(PAD + 1, PAD + rows + 1)
    a = jnp.concatenate(
        [
            jnp.concatenate([real[inside], real[following]], 1),
            jnp.concatenate([imag[inside], imag[following]], 1),
        ],
        0,
    )
    gr, gi = grad_real[inside], grad_imag[inside]
    d = jnp.concatenate([jnp.concatenate([gr, gi], 1), jnp.concatenate([gi, -gr], 1)], 0)
    ah, al = split(a)
    dh, dl = split(d)
    table = lax.dot_general(
        jnp.concatenate([dh, dh, dl], 0),
        jnp.concatenate([ah, al, ah], 0),
        (((0,), (0,)), ((), ())),
        preferred_element_type=F32,
    )
    width = 2 * LANES
    results = []
    for c in range(2):
        acc = table[c * LANES : c * LANES + 8]
        for g in range(1, LANES // 8):
            first = c * LANES + 8 * g
            acc = acc + pltpu.roll(table[first : first + 8], width - 8 * g, 1)
        total = acc[0:1]
        for s in range(1, 8):
            total = total + pltpu.roll(acc, width - s, 1)[s : s + 1]
        results.append(total[:, :LANES])
    return results


def k_taps(shifted, grad, out):
    bands = grad.shape[0]
    rows = grad.shape[2] - 2 * PAD
    for b in range(bands):
        parts = correlate(shifted[b, 0], shifted[b, 1], grad[b, 0], grad[b, 1], rows)
        for c in range(2):
            out[2 * b + c : 2 * b + c + 1, :] = parts[c]


def k_fifth(
    scale, delays, turned0, linear0, own, even_in, odd_in, shifted, taps1,
    grad0, out, spread, held,
):
    bands = turned0.shape[0]
    rows = turned0.shape[2] - 2 * PAD
    values = gather_spread(own, even_in, odd_in, spread, rows)
    for b in range(bands):
        twice = 2.0 * read_spread(values, at(delays, 0, b), held, b, rows)
        gr = keep_inside(turned0[b, 0] + linear0[b, 0] * twice, rows)
        gi = keep_inside(turned0[b, 1] + linear0[b, 1] * twice, rows)
        grad0[b, 0] = gr
        grad0[b, 1] = gi
        parts = correlate(shifted[b, 0], shifted[b, 1], gr, gi, rows)
        for c in range(2):
            out[2 * b + c : 2 * b + c + 1, :] = parts[c] * scale
    out[2 * bands :, :] = taps1[...] * scale


def k_last(shifts, grad0, high, low, result):
    bands = grad0.shape[0]
    rows = grad0.shape[2] - 2 * PAD
    for b in range(bands):
        gr, gi = fir_adjoint(grad0[b, 0], grad0[b, 1], high[b], low[b])
        amount = LANES // 2 - at(shifts, 0, b)
        gr = earlier(gr, amount)[PAD : PAD + rows]
        gi = earlier(gi, amount)[PAD : PAD + rows]
        for r in range(rows):
            result[b, 0, 0:1, r * LANES : (r + 1) * LANES] = gr[r : r + 1]
            result[b, 0, 1:2, r * LANES : (r + 1) * LANES] = gi[r : r + 1]


def call(kernel, arrays, shapes, scratch=(), micros=2.0):
    vmem = pl.BlockSpec(memory_space=pltpu.VMEM)
    return pl.pallas_call(
        kernel,
        out_shape=shapes,
        in_specs=[vmem] * len(arrays),
        out_specs=[vmem] * len(shapes),
        scratch_shapes=[pltpu.VMEM(s, F32) for s in scratch],
        compiler_params=pltpu.CompilerParams(vmem_limit_bytes=24 * 1024 * 1024),
        cost_estimate=pl.CostEstimate(
            flops=int(micros * 1e8), bytes_accessed=int(micros * 3e6), transcendentals=0
        ),
    )(*arrays)


def swapped(x, axis, partner, cross):
    size, cores = lax.axis_size(axis), lax.axis_size("pol")
    pairs = []
    for i in range(size):
        for p in range(cores):
            j, q = partner(i), cores - 1 - p
            if 0 <= j < size:
                pairs.append((i * cores + p, j * cores + (q if cross else p)))
            else:
                pairs.append((i * cores + p, i * cores + q))
    return lax.ppermute(x, (axis, "pol"), pairs)


def summed(x, axis, cross=True):
    size = lax.axis_size(axis)
    if size & (size - 1):
        return lax.psum(x, axis)
    distance = 1
    while distance < size:
        x = x + swapped(x, axis, lambda i, d=distance: i ^ d, cross)
        distance *= 2
    return x


def over_cores(x):
    cores = lax.axis_size("pol")
    return x + lax.ppermute(x, "pol", [(p, cores - 1 - p) for p in range(cores)])


def evenly(i):
    return i ^ 1


def oddly(i):
    return ((i + 1) ^ 1) - 1


def neighbours(even_out, odd_out, cross):
    odd_in = swapped(odd_out, "tm", oddly, cross)
    even_in = swapped(even_out, "tm", evenly, cross)
    return even_in, odd_in


def aslant(x, partner):
    size, cores = lax.axis_size("tm"), lax.axis_size("pol")
    pairs = []
    for i in range(size):
        for b in range(2):
            for p in range(cores):
                here = (i * 2 + b) * cores
                j = partner(i)
                if 0 <= j < size:
                    pairs.append((here + p, (j * 2 + 1 - b) * cores + p))
                else:
                    pairs.append((here + p, here + cores - 1 - p))
    return lax.ppermute(x, ("tm", "band", "pol"), pairs)


def over_tm(x):
    if lax.axis_size("tm") != 4:
        return summed(x, "tm")
    others = [swapped(x, "tm", lambda i, d=d: i ^ d, True) for d in (1, 2, 3)]
    return (x + others[0]) + (others[1] + others[2])


def over_powers(part, doubled):
    part = over_cores(part)
    return part if doubled else summed(part, "band")


def exchanged(part, doubled):
    part = over_powers(part, doubled)
    return (part,) + neighbours(part, part, True)


def edges(signal, cotangent):
    wide, edge = WIDE * LANES, EDGE * LANES
    left = jnp.concatenate([signal[..., :wide], cotangent[..., :edge]], -1)
    right = jnp.concatenate([signal[..., -wide:], cotangent[..., -edge:]], -1)
    even = is_even()
    return jnp.where(even, right, left), jnp.where(even, left, right)


def on_device(signal, cotangent, taps, gains, walk_off, tap_shift):
    own, _, _, length = signal.shape
    steps = taps.shape[0]
    rows = length // LANES
    held_rows = rows + 2 * PAD
    doubled = lax.axis_size("band") == 2
    groups = 2 if doubled else 1
    bands = groups * own

    def shape(*dims, dtype=F32):
        return jax.ShapeDtypeStruct(dims, dtype)

    field = shape(bands, 2, held_rows, LANES)
    own_field = shape(own, 2, held_rows, LANES)
    angle = shape(own, held_rows, LANES)
    wide_part = shape(rows + REACH + 2 * PAD, LANES)
    part = shape(rows + REACH, LANES)
    table = shape(bands, 2 * LANES, 4 * LANES, dtype=BF16)
    ext_wide = (bands, 2, rows + 2 * WIDE_PAD, LANES)
    held_wide = (bands, rows + 2 * WIDE_PAD + 8, LANES)
    spread = (rows + REACH + 2 * PAD, LANES)
    held_in = (bands, rows + REACH + 3 * PAD, LANES)
    held_out = (bands, rows + 3 * REACH, LANES)

    signals, cotangents = [signal], [cotangent]
    small = jnp.concatenate([walk_off.astype(F32), tap_shift.astype(F32), gains])
    small = jnp.pad(small, ((0, -3 * steps % 8), (0, LANES - own)))
    small = jnp.concatenate([taps.reshape(2 * steps * own, LANES), small])
    even_out, odd_out = edges(signal[:, 0], cotangent[:, 0])
    small, _ = lax.optimization_barrier((small, even_out))
    packs = [small]
    sides = list(neighbours(even_out, odd_out, False))
    if doubled:
        signals.append(swapped(signal, "band", evenly, False))
        packs.append(swapped(packs[0], "band", evenly, False))
        sides += [aslant(even_out, evenly), aslant(odd_out, oddly)]
        cotangents.append(swapped(cotangent, "band", evenly, False))
    tiny = [shape(groups, steps, own, dtype=d) for d in (jnp.int32, jnp.int32, F32)]
    sig_rows, delays, shifts, gains, high0, low0, high1, low1 = call(
        functools.partial(k_setup, groups, steps), (*signals, *packs),
        [shape(bands, 2, rows, LANES)] + tiny + [table] * (2 * steps),
    )
    (cot_rows,) = call(
        functools.partial(k_cotangent, groups), (*cotangents, *sides), [field]
    )
    shifted0, linear0, sent = call(
        functools.partial(k_first, groups), (delays, shifts, sig_rows, *sides, high0, low0),
        [own_field, field, wide_part], (ext_wide, held_wide),
    )
    cosine0, sine0, field1, shifted1, linear1, sent = call(
        k_second, (delays, shifts, gains, linear0, over_powers(sent, doubled), high1, low1),
        [angle, angle, field, own_field, field, part], (held_in, held_out),
    )
    turned1, sent = call(
        k_third, (delays, gains, linear1, *exchanged(sent, doubled), cot_rows),
        [field, part], (spread, held_in, held_out),
    )
    grad1, turned0, sent = call(
        k_fourth,
        (delays, shifts, gains, turned1, linear1, *exchanged(sent, doubled), high1, low1,
         cosine0, sine0, field1),
        [own_field, own_field, part], (spread, held_in, held_out),
    )
    (taps1,) = call(k_taps, (shifted1, grad1), [shape(2 * own, LANES)])
    scale = 1.0 / math.sqrt(2.0 * length * lax.axis_size("tm"))
    grad0, grad_taps = call(
        functools.partial(k_fifth, scale),
        (delays, turned0, linear0, *exchanged(sent, doubled), shifted0, taps1),
        [own_field, shape(steps * 2 * own, LANES)], (spread, held_in),
    )
    (grad_signal,) = call(
        k_last, (shifts, grad0, high0, low0), [shape(own, 1, 2, length)]
    )
    grad_taps = over_tm(over_cores(grad_taps))
    return grad_signal, grad_taps.reshape(steps, own, 2, LANES)


def solution(mesh):
    return jax.shard_map(
        on_device,
        mesh=mesh,
        in_specs=(
            P(("groups", "band"), "pol", None, "tm"),
            P(("groups", "band"), "pol", None, "tm"),
            P(None, "band", None, None),
            P(None, "band"),
            P(None, "band"),
            P(None, "band"),
        ),
        out_specs=(P(("groups", "band"), "pol", None, "tm"), P("groups", "band", None, None)),
        check_vma=False,
    )
```

```python
import functools
import math

import jax
import jax.numpy as jnp
from jax import lax
from jax.experimental import pallas as pl
from jax.experimental.pallas import tpu as pltpu
from jax.sharding import PartitionSpec as P

LANES = 128
REACH = 2048 // LANES
EDGE = 4
WIDE = REACH + 4
PAD = 8
WIDE_PAD = REACH + PAD
F32 = jnp.float32
BF16 = jnp.bfloat16

TWO_OVER_PI = 2.0 / math.pi
HALF_PI_1 = 1.5625
HALF_PI_2 = 67.0 / 8192.0
HALF_PI_3 = 123.0 / 1048576.0
HALF_PI_4 = math.pi / 2.0 - HALF_PI_1 - HALF_PI_2 - HALF_PI_3


def split(x):
    high = x.astype(BF16)
    return high, (x - high.astype(F32)).astype(BF16)


def sine_cosine(x):
    turns = jnp.floor(x * TWO_OVER_PI + 0.5)
    quadrant = turns.astype(jnp.int32)
    r = x - turns * HALF_PI_1
    r = r - turns * HALF_PI_2
    r = r - turns * HALF_PI_3
    r = r - turns * HALF_PI_4
    r2 = r * r
    s = r + r * r2 * (-1.6666654611e-1 + r2 * (8.3321608736e-3 + r2 * -1.9515295891e-4))
    c = 1.0 - 0.5 * r2 + r2 * r2 * (
        4.166664568298827e-2 + r2 * (-1.388731625493765e-3 + r2 * 2.443315711809948e-5)
    )
    odd = (quadrant & 1) == 1
    sine = jnp.where(odd, c, s)
    cosine = jnp.where(odd, s, c)
    sine = jnp.where((quadrant & 2) == 2, -sine, sine)
    cosine = jnp.where(((quadrant + 1) & 2) == 2, -cosine, cosine)
    return sine, cosine


def lanes_of(shape):
    return lax.broadcasted_iota(jnp.int32, shape, len(shape) - 1)


def later(x, amount):
    rolled = pltpu.roll(x, amount & (LANES - 1), 1)
    return jnp.where(lanes_of(x.shape) >= amount, rolled, pltpu.roll(rolled, 1, 0))


def earlier(x, amount):
    rows = x.shape[0]
    rolled = pltpu.roll(x, (LANES - amount) & (LANES - 1), 1)
    follow = pltpu.roll(rolled, rows - 1, 0)
    return jnp.where(lanes_of(x.shape) + amount < LANES, rolled, follow)


def at(table, step, b):
    own = table.shape[2]
    return table[b // own, step, b % own]


def is_even():
    return lax.rem(lax.axis_index("tm"), 2) == 0


def keep_inside(values, rows, pad=PAD):
    z = lax.axis_index("tm")
    row = lax.broadcasted_iota(jnp.int32, values.shape, 0)
    low = jnp.where(z == 0, pad, 0)
    high = jnp.where(z == lax.axis_size("tm") - 1, pad + rows, 2 * pad + rows)
    return jnp.where((row >= low) & (row < high), values, 0.0)


def from_sides(even_value, odd_value):
    z = lax.axis_index("tm")
    even = is_even()
    before = jnp.where(even, odd_value, even_value)
    after = jnp.where(even, even_value, odd_value)
    before = jnp.where(z == 0, 0.0, before)
    after = jnp.where(z == lax.axis_size("tm") - 1, 0.0, after)
    return before, after


def extend(out, b, even_in, odd_in, first, edge):
    own = even_in.shape[0]
    rows = out.shape[2]
    pad = edge + 4
    for c in range(2):
        out[b, c, 0:8, :] = jnp.zeros((8, LANES), F32)
        out[b, c, rows - 8 :, :] = jnp.zeros((8, LANES), F32)
    for r in range(edge):
        lanes = slice((first + r) * LANES, (first + r + 1) * LANES)
        before, after = from_sides(even_in[b % own, :, lanes], odd_in[b % own, :, lanes])
        for c in range(2):
            above = pad - edge + r
            below = rows - pad + r
            out[b, c, above : above + 1, :] = before[c : c + 1]
            out[b, c, below : below + 1, :] = after[c : c + 1]


def fir(real, imag, high, low):
    rows = real.shape[0]
    x = jnp.concatenate(
        [real, pltpu.roll(real, rows - 1, 0), imag, pltpu.roll(imag, rows - 1, 0)], 1
    )
    xh, xl = split(x)
    contract = (((1,), (1,)), ((), ()))
    both = lax.dot_general(jnp.concatenate([xh, xl], 0), high, contract, preferred_element_type=F32)
    rest = lax.dot_general(xh, low, contract, preferred_element_type=F32)
    y = both[:rows] + both[rows:] + rest
    return y[:, :LANES], y[:, LANES:]


def fir_adjoint(real, imag, high, low):
    rows = real.shape[0]
    xh, xl = split(jnp.concatenate([real, imag], 1))
    both = jnp.dot(jnp.concatenate([xh, xl], 0), high, preferred_element_type=F32)
    rest = jnp.dot(xh, low, preferred_element_type=F32)
    g = both[:rows] + both[rows:] + rest
    out_real = g[:, :LANES] + pltpu.roll(g[:, LANES : 2 * LANES], 1, 0)
    out_imag = g[:, 2 * LANES : 3 * LANES] + pltpu.roll(g[:, 3 * LANES :], 1, 0)
    return out_real, out_imag


def scatter_delayed(values, delays, step, held, out):
    bands = len(values)
    rows = values[0].shape[0]
    total = rows + REACH
    base = REACH + 8
    lane = lanes_of((total, LANES))
    acc = None
    for b in range(bands):
        delay = at(delays, step, b)
        q = lax.shift_right_logical(delay, 7)
        s = delay & (LANES - 1)
        held[b, 0:base, :] = jnp.zeros((base, LANES), F32)
        held[b, base : base + rows, :] = pltpu.roll(values[b], s, 1)
        held[b, base + rows :, :] = jnp.zeros((held.shape[1] - base - rows, LANES), F32)
        near = held[b, pl.ds(base - q, total), :]
        far = held[b, pl.ds(base - q - 1, total), :]
        part = jnp.where(lane >= s, near, far)
        acc = part if acc is None else acc + part
    out[...] = acc


def delayed_sum(values, delays, step, held, out):
    bands = len(values)
    count, total = values[0].shape[0], out.shape[0]
    lane = lanes_of((total, LANES))
    acc = None
    for b in range(bands):
        delay = at(delays, step, b)
        q = lax.shift_right_logical(delay, 7)
        s = delay & (LANES - 1)
        held[b, 0:8, :] = jnp.zeros((8, LANES), F32)
        held[b, 8 : 8 + count, :] = pltpu.roll(values[b], s, 1)
        near = held[b, pl.ds(8 + REACH - q, total), :]
        far = held[b, pl.ds(8 + REACH - q - 1, total), :]
        part = jnp.where(lane >= s, near, far)
        acc = part if acc is None else acc + part
    out[...] = acc


def end_at_last(values, rows):
    row = lax.broadcasted_iota(jnp.int32, values.shape, 0)
    last = lax.axis_index("tm") == lax.axis_size("tm") - 1
    return jnp.where(row < jnp.where(last, PAD + rows, values.shape[0]), values, 0.0)


def gather_spread(own, even_in, odd_in, spread, rows):
    before, after = from_sides(even_in[...], odd_in[...])
    total = rows + REACH + 2 * PAD
    spread[0:PAD, :] = before[rows - PAD : rows]
    spread[PAD:total - PAD, :] = own[...]
    spread[total - PAD : total, :] = after[REACH : REACH + PAD]
    spread[PAD : PAD + REACH, :] += before[rows : rows + REACH]
    spread[PAD + rows : PAD + rows + REACH, :] += after[0:REACH]
    return end_at_last(spread[...], rows)


def read_spread(values, delay, held, b, rows):
    total = values.shape[0]
    q = lax.shift_right_logical(delay, 7)
    s = delay & (LANES - 1)
    held[b, 0:total, :] = pltpu.roll(values, (LANES - s) & (LANES - 1), 1)
    held[b, total:, :] = jnp.zeros((held.shape[1] - total, LANES), F32)
    count = rows + 2 * PAD
    near = held[b, pl.ds(q, count), :]
    far = held[b, pl.ds(q + 1, count), :]
    return jnp.where(lanes_of((count, LANES)) + s < LANES, near, far)


def k_begin(
    signal, cotangent, taps, delays, shifts, gains, even_out, odd_out, sent, cot_rows,
    sig_held, cot_held, taps_held, delays_held, shifts_held, gains_held, done,
):
    steps, bands = taps.shape[:2]
    rows = cot_rows.shape[2]
    pairs = (
        (signal, sig_held), (cotangent, cot_held), (taps, taps_held),
        (delays, delays_held), (shifts, shifts_held), (gains, gains_held),
    )
    copies = [pltpu.make_async_copy(a, b, done.at[n]) for n, (a, b) in enumerate(pairs)]
    for copy in copies:
        copy.start()
    for copy in copies:
        copy.wait()
    even = is_even()
    length, wide, edge = rows * LANES, WIDE * LANES, EDGE * LANES
    for b in range(bands):
        for held, first, width in ((sig_held, 0, wide), (cot_held, wide, edge)):
            left = held[b, 0, :, 0:width]
            right = held[b, 0, :, length - width : length]
            even_out[b, :, first : first + width] = jnp.where(even, right, left)
            odd_out[b, :, first : first + width] = jnp.where(even, left, right)
        for r in range(rows):
            lanes = slice(r * LANES, (r + 1) * LANES)
            pair = sig_held[b, 0, :, lanes]
            other = cot_held[b, 0, :, lanes]
            for c in range(2):
                row = (2 * b + c) * rows + r
                sent[row : row + 1, :] = pair[c : c + 1]
                cot_rows[b, c, r : r + 1, :] = other[c : c + 1]
    first = 2 * bands * rows
    for step in range(steps):
        for b in range(bands):
            row = first + 2 * (step * bands + b)
            sent[row : row + 2, :] = taps_held[step, b]
    first = first + 2 * steps * bands
    sent[first:, :] = jnp.zeros((sent.shape[0] - first, LANES), F32)
    for k, held in enumerate((delays_held, shifts_held, gains_held)):
        row = first + k * steps
        sent[row : row + steps, 0:bands] = held[...].astype(F32)


def k_setup(groups, steps, rows, *refs):
    packs = refs[:groups]
    delays, shifts, gains = refs[groups : groups + 3]
    tables = refs[groups + 3 :]
    own = delays.shape[2]
    shape = (LANES, LANES)
    diagonal = lanes_of(shape) >= lax.broadcasted_iota(jnp.int32, shape, 0)
    base = 2 * own * rows
    first = base + 2 * steps * own
    for k, pack in enumerate(packs):
        for n, target in enumerate((delays, shifts, gains)):
            row = first + n * steps
            target[k] = pack[row : row + steps, 0:own].astype(target.dtype)
    for b in range(groups * own):
        pack = packs[b // own]
        for step in range(steps):
            high, low = tables[2 * step : 2 * step + 2]
            for c in range(2):
                tap = base + 2 * (step * own + b % own) + c
                row = jnp.broadcast_to(pack[tap : tap + 1, :], shape)
                ring = pltpu.roll(row, 0, 1, stride=1, stride_axis=0)
                near = jnp.where(diagonal, ring, 0.0)
                for place, half in ((0, near), (1, ring - near)):
                    for target, value in zip((high, low), split(half)):
                        a = place * LANES
                        d = (2 + place) * LANES
                        if c == 0:
                            target[b, 0:LANES, a : a + LANES] = value
                            target[b, LANES:, d : d + LANES] = value
                        else:
                            target[b, LANES:, a : a + LANES] = value
                            target[b, 0:LANES, d : d + LANES] = -value


def k_cotangent(groups, *refs):
    out = refs[-1]
    own = refs[0].shape[0]
    rows = out.shape[2] - 2 * PAD
    for b in range(out.shape[0]):
        k = b // own
        extend(out, b, refs[groups + 2 * k], refs[groups + 2 * k + 1], WIDE, EDGE)
        for c in range(2):
            out[b, c, PAD : PAD + rows, :] = refs[k][b % own, c]


def k_first(groups, delays, shifts, *refs):
    packs, sides = refs[:groups], refs[groups : 3 * groups]
    high, low, shifted, linear, out, ext, held = refs[3 * groups :]
    bands = linear.shape[0]
    rows = linear.shape[2] - 2 * PAD
    own = shifted.shape[0]
    middle = slice(WIDE_PAD - PAD, WIDE_PAD + rows + PAD)
    powers = []
    for b in range(bands):
        k = b // own
        extend(ext, b, sides[2 * k], sides[2 * k + 1], 0, WIDE)
        for c in range(2):
            row = (2 * (b % own) + c) * rows
            ext[b, c, WIDE_PAD : WIDE_PAD + rows, :] = packs[k][row : row + rows, :]
        amount = LANES // 2 - at(shifts, 0, b)
        real = later(ext[b, 0], amount)
        imag = later(ext[b, 1], amount)
        if b < own:
            shifted[b, 0] = real[middle]
            shifted[b, 1] = imag[middle]
        lr, li = fir(real, imag, high[b], low[b])
        linear[b, 0] = lr[middle]
        linear[b, 1] = li[middle]
        powers.append(keep_inside(lr * lr + li * li, rows, WIDE_PAD))
    delayed_sum(powers, delays, 0, held, out)


def k_second(
    delays, shifts, gains, linear0, own, high, low,
    cosine0, sine0, field1, shifted, linear1, out, held, held_out,
):
    bands = linear0.shape[0]
    rows = linear0.shape[2] - 2 * PAD
    values = end_at_last(own[...], rows)
    powers = []
    for b in range(bands):
        spread = read_spread(values, at(delays, 0, b), held, b, rows)
        sine, cosine = sine_cosine(at(gains, 0, b) * spread)
        lr, li = linear0[b, 0], linear0[b, 1]
        fr = keep_inside(lr * cosine - li * sine, rows)
        fi = keep_inside(lr * sine + li * cosine, rows)
        field1[b, 0] = fr
        field1[b, 1] = fi
        amount = LANES // 2 - at(shifts, 1, b)
        real = later(fr, amount)
        imag = later(fi, amount)
        if b < shifted.shape[0]:
            cosine0[b] = cosine
            sine0[b] = sine
            shifted[b, 0] = real
            shifted[b, 1] = imag
        lr, li = fir(real, imag, high[b], low[b])
        linear1[b, 0] = lr
        linear1[b, 1] = li
        lr, li = lr[PAD : PAD + rows], li[PAD : PAD + rows]
        powers.append(lr * lr + li * li)
    scatter_delayed(powers, delays, 1, held_out, out)


def k_third(
    delays, gains, linear1, own, even_in, odd_in, cotangent, turned1, out, spread, held, held_out
):
    bands = linear1.shape[0]
    rows = linear1.shape[2] - 2 * PAD
    values = gather_spread(own, even_in, odd_in, spread, rows)
    terms = []
    for b in range(bands):
        gain = at(gains, 1, b)
        phase = gain * read_spread(values, at(delays, 1, b), held, b, rows)
        sine, cosine = sine_cosine(phase)
        gr, gi = cotangent[b, 0], cotangent[b, 1]
        er = gr * cosine + gi * sine
        ei = gi * cosine - gr * sine
        turned1[b, 0] = er
        turned1[b, 1] = ei
        term = ei * linear1[b, 0] - er * linear1[b, 1]
        terms.append(gain * term[PAD : PAD + rows])
    scatter_delayed(terms, delays, 1, held_out, out)


def k_fourth(
    delays, shifts, gains, turned1, linear1, own, even_in, odd_in, high, low, cosine0, sine0, field1,
    grad1, turned0, out, spread, held, held_out,
):
    bands = linear1.shape[0]
    rows = linear1.shape[2] - 2 * PAD
    values = gather_spread(own, even_in, odd_in, spread, rows)
    terms = []
    for b in range(bands):
        twice = 2.0 * read_spread(values, at(delays, 1, b), held, b, rows)
        gr = keep_inside(turned1[b, 0] + linear1[b, 0] * twice, rows)
        gi = keep_inside(turned1[b, 1] + linear1[b, 1] * twice, rows)
        if b < grad1.shape[0]:
            grad1[b, 0] = gr
            grad1[b, 1] = gi
        gr, gi = fir_adjoint(gr, gi, high[b], low[b])
        amount = LANES // 2 - at(shifts, 1, b)
        gr = earlier(gr, amount)
        gi = earlier(gi, amount)
        if b < grad1.shape[0]:
            cosine, sine = cosine0[b], sine0[b]
            turned0[b, 0] = gr * cosine + gi * sine
            turned0[b, 1] = gi * cosine - gr * sine
        term = gi * field1[b, 0] - gr * field1[b, 1]
        terms.append(at(gains, 0, b) * term[PAD : PAD + rows])
    scatter_delayed(terms, delays, 0, held_out, out)


def correlate(real, imag, grad_real, grad_imag, rows):
    inside = slice(PAD, PAD + rows)
    following = slice(PAD + 1, PAD + rows + 1)
    a = jnp.concatenate(
        [
            jnp.concatenate([real[inside], real[following]], 1),
            jnp.concatenate([imag[inside], imag[following]], 1),
        ],
        0,
    )
    gr, gi = grad_real[inside], grad_imag[inside]
    d = jnp.concatenate([jnp.concatenate([gr, gi], 1), jnp.concatenate([gi, -gr], 1)], 0)
    ah, al = split(a)
    dh, dl = split(d)
    table = lax.dot_general(
        jnp.concatenate([dh, dh, dl], 0),
        jnp.concatenate([ah, al, ah], 0),
        (((0,), (0,)), ((), ())),
        preferred_element_type=F32,
    )
    width = 2 * LANES
    results = []
    for c in range(2):
        acc = table[c * LANES : c * LANES + 8]
        for g in range(1, LANES // 8):
            first = c * LANES + 8 * g
            acc = acc + pltpu.roll(table[first : first + 8], width - 8 * g, 1)
        total = acc[0:1]
        for s in range(1, 8):
            total = total + pltpu.roll(acc, width - s, 1)[s : s + 1]
        results.append(total[:, :LANES])
    return results


def k_taps(shifted, grad, out):
    bands = grad.shape[0]
    rows = grad.shape[2] - 2 * PAD
    for b in range(bands):
        parts = correlate(shifted[b, 0], shifted[b, 1], grad[b, 0], grad[b, 1], rows)
        for c in range(2):
            out[2 * b + c : 2 * b + c + 1, :] = parts[c]


def k_fifth(
    scale, delays, turned0, linear0, own, even_in, odd_in, shifted, taps1,
    grad0, out, spread, held,
):
    bands = turned0.shape[0]
    rows = turned0.shape[2] - 2 * PAD
    values = gather_spread(own, even_in, odd_in, spread, rows)
    for b in range(bands):
        twice = 2.0 * read_spread(values, at(delays, 0, b), held, b, rows)
        gr = keep_inside(turned0[b, 0] + linear0[b, 0] * twice, rows)
        gi = keep_inside(turned0[b, 1] + linear0[b, 1] * twice, rows)
        grad0[b, 0] = gr
        grad0[b, 1] = gi
        parts = correlate(shifted[b, 0], shifted[b, 1], gr, gi, rows)
        for c in range(2):
            out[2 * b + c : 2 * b + c + 1, :] = parts[c] * scale
    out[2 * bands :, :] = taps1[...] * scale


def k_last(shifts, grad0, high, low, result):
    bands = grad0.shape[0]
    rows = grad0.shape[2] - 2 * PAD
    for b in range(bands):
        gr, gi = fir_adjoint(grad0[b, 0], grad0[b, 1], high[b], low[b])
        amount = LANES // 2 - at(shifts, 0, b)
        gr = earlier(gr, amount)[PAD : PAD + rows]
        gi = earlier(gi, amount)[PAD : PAD + rows]
        for r in range(rows):
            result[b, 0, 0:1, r * LANES : (r + 1) * LANES] = gr[r : r + 1]
            result[b, 0, 1:2, r * LANES : (r + 1) * LANES] = gi[r : r + 1]


def call(kernel, arrays, shapes, scratch=(), micros=2.0):
    vmem = pl.BlockSpec(memory_space=pltpu.VMEM)
    return pl.pallas_call(
        kernel,
        out_shape=shapes,
        in_specs=[vmem] * len(arrays),
        out_specs=[vmem] * len(shapes),
        scratch_shapes=[pltpu.VMEM(s, F32) for s in scratch],
        compiler_params=pltpu.CompilerParams(vmem_limit_bytes=24 * 1024 * 1024),
        cost_estimate=pl.CostEstimate(
            flops=int(micros * 1e8), bytes_accessed=int(micros * 3e6), transcendentals=0
        ),
    )(*arrays)


def swapped(x, axis, partner, cross):
    size, cores = lax.axis_size(axis), lax.axis_size("pol")
    pairs = []
    for i in range(size):
        for p in range(cores):
            j, q = partner(i), cores - 1 - p
            if 0 <= j < size:
                pairs.append((i * cores + p, j * cores + (q if cross else p)))
            else:
                pairs.append((i * cores + p, i * cores + q))
    return lax.ppermute(x, (axis, "pol"), pairs)


def summed(x, axis, cross=True):
    size = lax.axis_size(axis)
    if size & (size - 1):
        return lax.psum(x, axis)
    distance = 1
    while distance < size:
        x = x + swapped(x, axis, lambda i, d=distance: i ^ d, cross)
        distance *= 2
    return x


def over_cores(x):
    cores = lax.axis_size("pol")
    return x + lax.ppermute(x, "pol", [(p, cores - 1 - p) for p in range(cores)])


def evenly(i):
    return i ^ 1


def oddly(i):
    return ((i + 1) ^ 1) - 1


def neighbours(even_out, odd_out, cross):
    odd_in = swapped(odd_out, "tm", oddly, cross)
    even_in = swapped(even_out, "tm", evenly, cross)
    return even_in, odd_in


def aslant(x, partner):
    size, cores = lax.axis_size("tm"), lax.axis_size("pol")
    pairs = []
    for i in range(size):
        for b in range(2):
            for p in range(cores):
                here = (i * 2 + b) * cores
                j = partner(i)
                if 0 <= j < size:
                    pairs.append((here + p, (j * 2 + 1 - b) * cores + p))
                else:
                    pairs.append((here + p, here + cores - 1 - p))
    return lax.ppermute(x, ("tm", "band", "pol"), pairs)


def over_tm(x):
    if lax.axis_size("tm") != 4:
        return summed(x, "tm")
    others = [swapped(x, "tm", lambda i, d=d: i ^ d, True) for d in (1, 2, 3)]
    return (x + others[0]) + (others[1] + others[2])


def over_powers(part, doubled):
    part = over_cores(part)
    return part if doubled else summed(part, "band")


def exchanged(part, doubled):
    part = over_powers(part, doubled)
    return (part,) + neighbours(part, part, True)


def on_device(signal, cotangent, taps, gains, walk_off, tap_shift):
    own, _, _, length = signal.shape
    steps = taps.shape[0]
    rows = length // LANES
    held_rows = rows + 2 * PAD
    doubled = lax.axis_size("band") == 2
    groups = 2 if doubled else 1
    bands = groups * own

    def shape(*dims, dtype=F32):
        return jax.ShapeDtypeStruct(dims, dtype)

    field = shape(bands, 2, held_rows, LANES)
    own_field = shape(own, 2, held_rows, LANES)
    angle = shape(own, held_rows, LANES)
    wide_part = shape(rows + REACH + 2 * PAD, LANES)
    part = shape(rows + REACH, LANES)
    table = shape(bands, 2 * LANES, 4 * LANES, dtype=BF16)
    ext_wide = (bands, 2, rows + 2 * WIDE_PAD, LANES)
    held_wide = (bands, rows + 2 * WIDE_PAD + 8, LANES)
    spread = (rows + REACH + 2 * PAD, LANES)
    held_in = (bands, rows + REACH + 3 * PAD, LANES)
    held_out = (bands, rows + 3 * REACH, LANES)

    inputs = (signal, cotangent, taps, walk_off, tap_shift, gains)
    hbm, vmem = (pl.BlockSpec(memory_space=m) for m in (pltpu.HBM, pltpu.VMEM))
    cut = shape(own, 2, (WIDE + EDGE) * LANES)
    pack_rows = 2 * own * rows + 2 * steps * own + 3 * steps
    pack = shape(pack_rows + -pack_rows % 8, LANES)
    even_out, odd_out, pack_out, cot_out = pl.pallas_call(
        k_begin,
        out_shape=[cut, cut, pack, shape(own, 2, rows, LANES)],
        in_specs=[hbm] * len(inputs),
        out_specs=[vmem] * 4,
        scratch_shapes=[pltpu.VMEM(a.shape, a.dtype) for a in inputs]
        + [pltpu.SemaphoreType.DMA((len(inputs),))],
        compiler_params=pltpu.CompilerParams(vmem_limit_bytes=24 * 1024 * 1024),
        cost_estimate=pl.CostEstimate(flops=10**9, bytes_accessed=0, transcendentals=0),
    )(*(pltpu.with_memory_space_constraint(a, pltpu.HBM) for a in inputs))
    packs, cots = [pack_out], [cot_out]
    if doubled:
        packs.append(swapped(pack_out, "band", evenly, False))
    sides = list(neighbours(even_out, odd_out, False))
    if doubled:
        sides += [aslant(even_out, evenly), aslant(odd_out, oddly)]
        cots.append(swapped(cot_out, "band", evenly, False))
    tiny = [shape(groups, steps, own, dtype=d) for d in (jnp.int32, jnp.int32, F32)]
    delays, shifts, gains, high0, low0, high1, low1 = call(
        functools.partial(k_setup, groups, steps, rows), tuple(packs),
        tiny + [table] * (2 * steps),
    )
    (cot_rows,) = call(functools.partial(k_cotangent, groups), (*cots, *sides), [field])
    shifted0, linear0, sent = call(
        functools.partial(k_first, groups), (delays, shifts, *packs, *sides, high0, low0),
        [own_field, field, wide_part], (ext_wide, held_wide),
    )
    cosine0, sine0, field1, shifted1, linear1, sent = call(
        k_second, (delays, shifts, gains, linear0, over_powers(sent, doubled), high1, low1),
        [angle, angle, field, own_field, field, part], (held_in, held_out),
    )
    turned1, sent = call(
        k_third, (delays, gains, linear1, *exchanged(sent, doubled), cot_rows),
        [field, part], (spread, held_in, held_out),
    )
    grad1, turned0, sent = call(
        k_fourth,
        (delays, shifts, gains, turned1, linear1, *exchanged(sent, doubled), high1, low1,
         cosine0, sine0, field1),
        [own_field, own_field, part], (spread, held_in, held_out),
    )
    (taps1,) = call(k_taps, (shifted1, grad1), [shape(2 * own, LANES)])
    scale = 1.0 / math.sqrt(2.0 * length * lax.axis_size("tm"))
    grad0, grad_taps = call(
        functools.partial(k_fifth, scale),
        (delays, turned0, linear0, *exchanged(sent, doubled), shifted0, taps1),
        [own_field, shape(steps * 2 * own, LANES)], (spread, held_in),
    )
    (grad_signal,) = call(
        k_last, (shifts, grad0, high0, low0), [shape(own, 1, 2, length)]
    )
    grad_taps = over_tm(over_cores(grad_taps))
    return grad_signal, grad_taps.reshape(steps, own, 2, LANES)


def solution(mesh):
    return jax.shard_map(
        on_device,
        mesh=mesh,
        in_specs=(
            P(("groups", "band"), "pol", None, "tm"),
            P(("groups", "band"), "pol", None, "tm"),
            P(None, "band", None, None),
            P(None, "band"),
            P(None, "band"),
            P(None, "band"),
        ),
        out_specs=(P(("groups", "band"), "pol", None, "tm"), P("groups", "band", None, None)),
        check_vma=False,
    )
```

```python
import functools
import math

import jax
import jax.numpy as jnp
from jax import lax
from jax.experimental import pallas as pl
from jax.experimental.pallas import tpu as pltpu
from jax.sharding import PartitionSpec as P

LANES = 128
REACH = 2048 // LANES
EDGE = 4
WIDE = REACH + 4
PAD = 8
WIDE_PAD = REACH + PAD
F32 = jnp.float32
BF16 = jnp.bfloat16

TWO_OVER_PI = 2.0 / math.pi
HALF_PI_1 = 1.5625
HALF_PI_2 = 67.0 / 8192.0
HALF_PI_3 = 123.0 / 1048576.0
HALF_PI_4 = math.pi / 2.0 - HALF_PI_1 - HALF_PI_2 - HALF_PI_3


def split(x):
    high = x.astype(BF16)
    return high, (x - high.astype(F32)).astype(BF16)


def sine_cosine(x):
    turns = jnp.floor(x * TWO_OVER_PI + 0.5)
    quadrant = turns.astype(jnp.int32)
    r = x - turns * HALF_PI_1
    r = r - turns * HALF_PI_2
    r = r - turns * HALF_PI_3
    r = r - turns * HALF_PI_4
    r2 = r * r
    s = r + r * r2 * (-1.6666654611e-1 + r2 * (8.3321608736e-3 + r2 * -1.9515295891e-4))
    c = 1.0 - 0.5 * r2 + r2 * r2 * (
        4.166664568298827e-2 + r2 * (-1.388731625493765e-3 + r2 * 2.443315711809948e-5)
    )
    odd = (quadrant & 1) == 1
    sine = jnp.where(odd, c, s)
    cosine = jnp.where(odd, s, c)
    sine = jnp.where((quadrant & 2) == 2, -sine, sine)
    cosine = jnp.where(((quadrant + 1) & 2) == 2, -cosine, cosine)
    return sine, cosine


def lanes_of(shape):
    return lax.broadcasted_iota(jnp.int32, shape, len(shape) - 1)


def later(x, amount):
    rolled = pltpu.roll(x, amount & (LANES - 1), 1)
    return jnp.where(lanes_of(x.shape) >= amount, rolled, pltpu.roll(rolled, 1, 0))


def earlier(x, amount):
    rows = x.shape[0]
    rolled = pltpu.roll(x, (LANES - amount) & (LANES - 1), 1)
    follow = pltpu.roll(rolled, rows - 1, 0)
    return jnp.where(lanes_of(x.shape) + amount < LANES, rolled, follow)


def at(table, step, b):
    own = table[0].shape[1]
    return table[b // own][step, b % own]


def of(groups, b):
    own = groups[0].shape[0]
    return groups[b // own].at[b % own]


def is_even():
    return lax.rem(lax.axis_index("tm"), 2) == 0


def keep_inside(values, rows, pad=PAD):
    z = lax.axis_index("tm")
    row = lax.broadcasted_iota(jnp.int32, values.shape, 0)
    low = jnp.where(z == 0, pad, 0)
    high = jnp.where(z == lax.axis_size("tm") - 1, pad + rows, 2 * pad + rows)
    return jnp.where((row >= low) & (row < high), values, 0.0)


def from_sides(even_value, odd_value):
    z = lax.axis_index("tm")
    even = is_even()
    before = jnp.where(even, odd_value, even_value)
    after = jnp.where(even, even_value, odd_value)
    before = jnp.where(z == 0, 0.0, before)
    after = jnp.where(z == lax.axis_size("tm") - 1, 0.0, after)
    return before, after


def extend(out, b, even_in, odd_in, first, edge):
    own = even_in.shape[0]
    rows = out.shape[2]
    pad = edge + 4
    for c in range(2):
        out[b, c, 0:8, :] = jnp.zeros((8, LANES), F32)
        out[b, c, rows - 8 :, :] = jnp.zeros((8, LANES), F32)
    for r in range(edge):
        lanes = slice((first + r) * LANES, (first + r + 1) * LANES)
        before, after = from_sides(even_in[b % own, :, lanes], odd_in[b % own, :, lanes])
        for c in range(2):
            above = pad - edge + r
            below = rows - pad + r
            out[b, c, above : above + 1, :] = before[c : c + 1]
            out[b, c, below : below + 1, :] = after[c : c + 1]


def fir(real, imag, high, low):
    rows = real.shape[0]
    x = jnp.concatenate(
        [real, pltpu.roll(real, rows - 1, 0), imag, pltpu.roll(imag, rows - 1, 0)], 1
    )
    xh, xl = split(x)
    contract = (((1,), (1,)), ((), ()))
    both = lax.dot_general(jnp.concatenate([xh, xl], 0), high, contract, preferred_element_type=F32)
    rest = lax.dot_general(xh, low, contract, preferred_element_type=F32)
    y = both[:rows] + both[rows:] + rest
    return y[:, :LANES], y[:, LANES:]


def fir_adjoint(real, imag, high, low):
    rows = real.shape[0]
    xh, xl = split(jnp.concatenate([real, imag], 1))
    both = jnp.dot(jnp.concatenate([xh, xl], 0), high, preferred_element_type=F32)
    rest = jnp.dot(xh, low, preferred_element_type=F32)
    g = both[:rows] + both[rows:] + rest
    out_real = g[:, :LANES] + pltpu.roll(g[:, LANES : 2 * LANES], 1, 0)
    out_imag = g[:, 2 * LANES : 3 * LANES] + pltpu.roll(g[:, 3 * LANES :], 1, 0)
    return out_real, out_imag


def scatter_delayed(values, delays, step, held, out):
    bands = len(values)
    rows = values[0].shape[0]
    total = rows + REACH
    base = REACH + 8
    lane = lanes_of((total, LANES))
    acc = None
    for b in range(bands):
        delay = at(delays, step, b)
        q = lax.shift_right_logical(delay, 7)
        s = delay & (LANES - 1)
        held[b, 0:base, :] = jnp.zeros((base, LANES), F32)
        held[b, base : base + rows, :] = pltpu.roll(values[b], s, 1)
        held[b, base + rows :, :] = jnp.zeros((held.shape[1] - base - rows, LANES), F32)
        near = held[b, pl.ds(base - q, total), :]
        far = held[b, pl.ds(base - q - 1, total), :]
        part = jnp.where(lane >= s, near, far)
        acc = part if acc is None else acc + part
    out[...] = acc


def delayed_sum(values, delays, step, held, out):
    bands = len(values)
    count, total = values[0].shape[0], out.shape[0]
    lane = lanes_of((total, LANES))
    acc = None
    for b in range(bands):
        delay = at(delays, step, b)
        q = lax.shift_right_logical(delay, 7)
        s = delay & (LANES - 1)
        held[b, 0:8, :] = jnp.zeros((8, LANES), F32)
        held[b, 8 : 8 + count, :] = pltpu.roll(values[b], s, 1)
        near = held[b, pl.ds(8 + REACH - q, total), :]
        far = held[b, pl.ds(8 + REACH - q - 1, total), :]
        part = jnp.where(lane >= s, near, far)
        acc = part if acc is None else acc + part
    out[...] = acc


def end_at_last(values, rows):
    row = lax.broadcasted_iota(jnp.int32, values.shape, 0)
    last = lax.axis_index("tm") == lax.axis_size("tm") - 1
    return jnp.where(row < jnp.where(last, PAD + rows, values.shape[0]), values, 0.0)


def gather_spread(own, even_in, odd_in, spread, rows):
    before, after = from_sides(even_in[...], odd_in[...])
    total = rows + REACH + 2 * PAD
    spread[0:PAD, :] = before[rows - PAD : rows]
    spread[PAD:total - PAD, :] = own[...]
    spread[total - PAD : total, :] = after[REACH : REACH + PAD]
    spread[PAD : PAD + REACH, :] += before[rows : rows + REACH]
    spread[PAD + rows : PAD + rows + REACH, :] += after[0:REACH]
    return end_at_last(spread[...], rows)


def read_spread(values, delay, held, b, rows):
    total = values.shape[0]
    q = lax.shift_right_logical(delay, 7)
    s = delay & (LANES - 1)
    held[b, 0:total, :] = pltpu.roll(values, (LANES - s) & (LANES - 1), 1)
    held[b, total:, :] = jnp.zeros((held.shape[1] - total, LANES), F32)
    count = rows + 2 * PAD
    near = held[b, pl.ds(q, count), :]
    far = held[b, pl.ds(q + 1, count), :]
    return jnp.where(lanes_of((count, LANES)) + s < LANES, near, far)


def k_begin(
    signal, cotangent, taps, delays, shifts, gains,
    even_out, odd_out, even_near, odd_near, sent, cot_rows,
    sig_held, cot_held, taps_held, delays_held, shifts_held, gains_held, done,
):
    steps, bands = taps.shape[:2]
    rows = cot_rows.shape[2]
    pairs = (
        (signal, sig_held), (cotangent, cot_held), (taps, taps_held),
        (delays, delays_held), (shifts, shifts_held), (gains, gains_held),
    )
    copies = [pltpu.make_async_copy(a, b, done.at[n]) for n, (a, b) in enumerate(pairs)]
    for copy in copies:
        copy.start()
    for copy in copies:
        copy.wait()
    even = is_even()
    length, wide, edge = rows * LANES, WIDE * LANES, EDGE * LANES
    for b in range(bands):
        for targets, held, first, width in (
            ((even_out, odd_out), sig_held, 0, wide),
            ((even_out, odd_out), cot_held, wide, edge),
            ((even_near, odd_near), sig_held, 0, edge),
            ((even_near, odd_near), cot_held, edge, edge),
        ):
            left = held[b, 0, :, 0:width]
            right = held[b, 0, :, length - width : length]
            targets[0][b, :, first : first + width] = jnp.where(even, right, left)
            targets[1][b, :, first : first + width] = jnp.where(even, left, right)
        for r in range(rows):
            lanes = slice(r * LANES, (r + 1) * LANES)
            pair = sig_held[b, 0, :, lanes]
            other = cot_held[b, 0, :, lanes]
            for c in range(2):
                row = (2 * b + c) * rows + r
                sent[row : row + 1, :] = pair[c : c + 1]
                cot_rows[b, c, r : r + 1, :] = other[c : c + 1]
    first = 2 * bands * rows
    for step in range(steps):
        for b in range(bands):
            row = first + 2 * (step * bands + b)
            sent[row : row + 2, :] = taps_held[step, b]
    first = first + 2 * steps * bands
    sent[first:, :] = jnp.zeros((sent.shape[0] - first, LANES), F32)
    for k, held in enumerate((delays_held, shifts_held, gains_held)):
        row = first + k * steps
        sent[row : row + steps, 0:bands] = held[...].astype(F32)


def k_setup(steps, rows, pack, delays, shifts, gains, *tables):
    bands = delays.shape[1]
    shape = (LANES, LANES)
    diagonal = lanes_of(shape) >= lax.broadcasted_iota(jnp.int32, shape, 0)
    base = 2 * bands * rows
    first = base + 2 * steps * bands
    for n, target in enumerate((delays, shifts, gains)):
        row = first + n * steps
        target[...] = pack[row : row + steps, 0:bands].astype(target.dtype)
    for b in range(bands):
        for step in range(steps):
            high, low = tables[2 * step : 2 * step + 2]
            for c in range(2):
                tap = base + 2 * (step * bands + b) + c
                row = jnp.broadcast_to(pack[tap : tap + 1, :], shape)
                ring = pltpu.roll(row, 0, 1, stride=1, stride_axis=0)
                near = jnp.where(diagonal, ring, 0.0)
                for place, half in ((0, near), (1, ring - near)):
                    for target, value in zip((high, low), split(half)):
                        a = place * LANES
                        d = (2 + place) * LANES
                        if c == 0:
                            target[b, 0:LANES, a : a + LANES] = value
                            target[b, LANES:, d : d + LANES] = value
                        else:
                            target[b, LANES:, a : a + LANES] = value
                            target[b, 0:LANES, d : d + LANES] = -value


def k_cotangent(cots, sides, first, out):
    own = cots[0].shape[0]
    rows = out.shape[2] - 2 * PAD
    for b in range(out.shape[0]):
        k = b // own
        extend(out, b, *sides[k], first[k], EDGE)
        for c in range(2):
            out[b, c, PAD : PAD + rows, :] = cots[k][b % own, c]


def widened(ext, pack, sides, edge, b):
    pad = edge + 4
    rows = ext.shape[2] - 2 * pad
    extend(ext, b, *sides, 0, edge)
    for c in range(2):
        row = (2 * b + c) * rows
        ext[b, c, pad : pad + rows, :] = pack[row : row + rows, :]


def k_first(delays, shifts, pack, sides, high, low, shifted, linear, out, ext, held):
    bands = linear.shape[0]
    rows = linear.shape[2] - 2 * PAD
    middle = slice(WIDE_PAD - PAD, WIDE_PAD + rows + PAD)
    powers = []
    for b in range(bands):
        widened(ext, pack, sides, WIDE, b)
        amount = LANES // 2 - at(shifts, 0, b)
        real = later(ext[b, 0], amount)
        imag = later(ext[b, 1], amount)
        shifted[b, 0] = real[middle]
        shifted[b, 1] = imag[middle]
        lr, li = fir(real, imag, high[b], low[b])
        linear[b, 0] = lr[middle]
        linear[b, 1] = li[middle]
        powers.append(keep_inside(lr * lr + li * li, rows, WIDE_PAD))
    delayed_sum(powers, delays, 0, held, out)


def k_beside(shifts, pack, sides, high, low, linear, ext):
    for b in range(linear.shape[0]):
        widened(ext, pack, sides, EDGE, b)
        amount = LANES // 2 - at(shifts, 0, b)
        real = later(ext[b, 0], amount)
        imag = later(ext[b, 1], amount)
        lr, li = fir(real, imag, high[b], low[b])
        linear[b, 0] = lr
        linear[b, 1] = li


def k_second(
    delays, shifts, gains, linear0, own, high, low,
    cosine0, sine0, field1, shifted, linear1, out, held, held_out,
):
    bands = linear1.shape[0]
    rows = linear1.shape[2] - 2 * PAD
    values = end_at_last(own[...], rows)
    powers = []
    for b in range(bands):
        spread = read_spread(values, at(delays, 0, b), held, b, rows)
        sine, cosine = sine_cosine(at(gains, 0, b) * spread)
        linear = of(linear0, b)
        lr, li = linear[0], linear[1]
        fr = keep_inside(lr * cosine - li * sine, rows)
        fi = keep_inside(lr * sine + li * cosine, rows)
        field1[b, 0] = fr
        field1[b, 1] = fi
        amount = LANES // 2 - at(shifts, 1, b)
        real = later(fr, amount)
        imag = later(fi, amount)
        if b < shifted.shape[0]:
            cosine0[b] = cosine
            sine0[b] = sine
            shifted[b, 0] = real
            shifted[b, 1] = imag
        lr, li = fir(real, imag, of(high, b)[...], of(low, b)[...])
        linear1[b, 0] = lr
        linear1[b, 1] = li
        lr, li = lr[PAD : PAD + rows], li[PAD : PAD + rows]
        powers.append(lr * lr + li * li)
    scatter_delayed(powers, delays, 1, held_out, out)


def k_third(
    delays, gains, linear1, own, even_in, odd_in, cotangent, turned1, out, spread, held, held_out
):
    bands = linear1.shape[0]
    rows = linear1.shape[2] - 2 * PAD
    values = gather_spread(own, even_in, odd_in, spread, rows)
    terms = []
    for b in range(bands):
        gain = at(gains, 1, b)
        phase = gain * read_spread(values, at(delays, 1, b), held, b, rows)
        sine, cosine = sine_cosine(phase)
        gr, gi = cotangent[b, 0], cotangent[b, 1]
        er = gr * cosine + gi * sine
        ei = gi * cosine - gr * sine
        turned1[b, 0] = er
        turned1[b, 1] = ei
        term = ei * linear1[b, 0] - er * linear1[b, 1]
        terms.append(gain * term[PAD : PAD + rows])
    scatter_delayed(terms, delays, 1, held_out, out)


def k_fourth(
    delays, shifts, gains, turned1, linear1, own, even_in, odd_in, high, low, cosine0, sine0, field1,
    grad1, turned0, out, spread, held, held_out,
):
    bands = linear1.shape[0]
    rows = linear1.shape[2] - 2 * PAD
    values = gather_spread(own, even_in, odd_in, spread, rows)
    terms = []
    for b in range(bands):
        twice = 2.0 * read_spread(values, at(delays, 1, b), held, b, rows)
        gr = keep_inside(turned1[b, 0] + linear1[b, 0] * twice, rows)
        gi = keep_inside(turned1[b, 1] + linear1[b, 1] * twice, rows)
        if b < grad1.shape[0]:
            grad1[b, 0] = gr
            grad1[b, 1] = gi
        gr, gi = fir_adjoint(gr, gi, of(high, b)[...], of(low, b)[...])
        amount = LANES // 2 - at(shifts, 1, b)
        gr = earlier(gr, amount)
        gi = earlier(gi, amount)
        if b < grad1.shape[0]:
            cosine, sine = cosine0[b], sine0[b]
            turned0[b, 0] = gr * cosine + gi * sine
            turned0[b, 1] = gi * cosine - gr * sine
        term = gi * field1[b, 0] - gr * field1[b, 1]
        terms.append(at(gains, 0, b) * term[PAD : PAD + rows])
    scatter_delayed(terms, delays, 0, held_out, out)


def correlate(real, imag, grad_real, grad_imag, rows):
    inside = slice(PAD, PAD + rows)
    following = slice(PAD + 1, PAD + rows + 1)
    a = jnp.concatenate(
        [
            jnp.concatenate([real[inside], real[following]], 1),
            jnp.concatenate([imag[inside], imag[following]], 1),
        ],
        0,
    )
    gr, gi = grad_real[inside], grad_imag[inside]
    d = jnp.concatenate([jnp.concatenate([gr, gi], 1), jnp.concatenate([gi, -gr], 1)], 0)
    ah, al = split(a)
    dh, dl = split(d)
    table = lax.dot_general(
        jnp.concatenate([dh, dh, dl], 0),
        jnp.concatenate([ah, al, ah], 0),
        (((0,), (0,)), ((), ())),
        preferred_element_type=F32,
    )
    width = 2 * LANES
    results = []
    for c in range(2):
        acc = table[c * LANES : c * LANES + 8]
        for g in range(1, LANES // 8):
            first = c * LANES + 8 * g
            acc = acc + pltpu.roll(table[first : first + 8], width - 8 * g, 1)
        total = acc[0:1]
        for s in range(1, 8):
            total = total + pltpu.roll(acc, width - s, 1)[s : s + 1]
        results.append(total[:, :LANES])
    return results


def k_taps(shifted, grad, out):
    bands = grad.shape[0]
    rows = grad.shape[2] - 2 * PAD
    for b in range(bands):
        parts = correlate(shifted[b, 0], shifted[b, 1], grad[b, 0], grad[b, 1], rows)
        for c in range(2):
            out[2 * b + c : 2 * b + c + 1, :] = parts[c]


def k_fifth(
    scale, delays, turned0, linear0, own, even_in, odd_in, shifted, taps1,
    grad0, out, spread, held,
):
    bands = turned0.shape[0]
    rows = turned0.shape[2] - 2 * PAD
    values = gather_spread(own, even_in, odd_in, spread, rows)
    for b in range(bands):
        twice = 2.0 * read_spread(values, at(delays, 0, b), held, b, rows)
        gr = keep_inside(turned0[b, 0] + linear0[b, 0] * twice, rows)
        gi = keep_inside(turned0[b, 1] + linear0[b, 1] * twice, rows)
        grad0[b, 0] = gr
        grad0[b, 1] = gi
        parts = correlate(shifted[b, 0], shifted[b, 1], gr, gi, rows)
        for c in range(2):
            out[2 * b + c : 2 * b + c + 1, :] = parts[c] * scale
    out[2 * bands :, :] = taps1[...] * scale


def k_last(shifts, grad0, high, low, result):
    bands = grad0.shape[0]
    rows = grad0.shape[2] - 2 * PAD
    for b in range(bands):
        gr, gi = fir_adjoint(grad0[b, 0], grad0[b, 1], high[b], low[b])
        amount = LANES // 2 - at(shifts, 0, b)
        gr = earlier(gr, amount)[PAD : PAD + rows]
        gi = earlier(gi, amount)[PAD : PAD + rows]
        for r in range(rows):
            result[b, 0, 0:1, r * LANES : (r + 1) * LANES] = gr[r : r + 1]
            result[b, 0, 1:2, r * LANES : (r + 1) * LANES] = gi[r : r + 1]


def call(kernel, arrays, shapes, scratch=(), micros=2.0):
    vmem = pl.BlockSpec(memory_space=pltpu.VMEM)
    return pl.pallas_call(
        kernel,
        out_shape=shapes,
        in_specs=jax.tree.map(lambda _: vmem, arrays),
        out_specs=[vmem] * len(shapes),
        scratch_shapes=[pltpu.VMEM(s, F32) for s in scratch],
        compiler_params=pltpu.CompilerParams(vmem_limit_bytes=24 * 1024 * 1024),
        cost_estimate=pl.CostEstimate(
            flops=int(micros * 1e8), bytes_accessed=int(micros * 3e6), transcendentals=0
        ),
    )(*arrays)


def swapped(x, axis, partner, cross):
    size, cores = lax.axis_size(axis), lax.axis_size("pol")
    pairs = []
    for i in range(size):
        for p in range(cores):
            j, q = partner(i), cores - 1 - p
            if 0 <= j < size:
                pairs.append((i * cores + p, j * cores + (q if cross else p)))
            else:
                pairs.append((i * cores + p, i * cores + q))
    return lax.ppermute(x, (axis, "pol"), pairs)


def summed(x, axis, cross=True):
    size = lax.axis_size(axis)
    if size & (size - 1):
        return lax.psum(x, axis)
    distance = 1
    while distance < size:
        x = x + swapped(x, axis, lambda i, d=distance: i ^ d, cross)
        distance *= 2
    return x


def over_cores(x):
    cores = lax.axis_size("pol")
    return x + lax.ppermute(x, "pol", [(p, cores - 1 - p) for p in range(cores)])


def evenly(i):
    return i ^ 1


def oddly(i):
    return ((i + 1) ^ 1) - 1


def neighbours(even_out, odd_out, cross):
    odd_in = swapped(odd_out, "tm", oddly, cross)
    even_in = swapped(even_out, "tm", evenly, cross)
    return even_in, odd_in


def aslant(x, partner):
    size, cores = lax.axis_size("tm"), lax.axis_size("pol")
    pairs = []
    for i in range(size):
        for b in range(2):
            for p in range(cores):
                here = (i * 2 + b) * cores
                j = partner(i)
                if 0 <= j < size:
                    pairs.append((here + p, (j * 2 + 1 - b) * cores + p))
                else:
                    pairs.append((here + p, here + cores - 1 - p))
    return lax.ppermute(x, ("tm", "band", "pol"), pairs)


def over_tm(x):
    if lax.axis_size("tm") != 4:
        return summed(x, "tm")
    others = [swapped(x, "tm", lambda i, d=d: i ^ d, True) for d in (1, 2, 3)]
    return (x + others[0]) + (others[1] + others[2])


def exchanged(part, doubled):
    part = over_cores(part)
    part = part if doubled else summed(part, "band")
    return (part,) + neighbours(part, part, True)


def on_device(signal, cotangent, taps, gains, walk_off, tap_shift):
    own, _, _, length = signal.shape
    steps = taps.shape[0]
    rows = length // LANES
    held_rows = rows + 2 * PAD
    doubled = lax.axis_size("band") == 2
    groups = 2 if doubled else 1
    bands = groups * own

    def shape(*dims, dtype=F32):
        return jax.ShapeDtypeStruct(dims, dtype)

    field = shape(bands, 2, held_rows, LANES)
    own_field = shape(own, 2, held_rows, LANES)
    angle = shape(own, held_rows, LANES)
    wide_part = shape(rows + REACH + 2 * PAD, LANES)
    part = shape(rows + REACH, LANES)
    table = shape(own, 2 * LANES, 4 * LANES, dtype=BF16)
    ext_wide = (own, 2, rows + 2 * WIDE_PAD, LANES)
    held_wide = (own, rows + 2 * WIDE_PAD + 8, LANES)
    spread = (rows + REACH + 2 * PAD, LANES)
    held_in = (bands, rows + REACH + 3 * PAD, LANES)
    held_out = (bands, rows + 3 * REACH, LANES)

    inputs = (signal, cotangent, taps, walk_off, tap_shift, gains)
    hbm, vmem = (pl.BlockSpec(memory_space=m) for m in (pltpu.HBM, pltpu.VMEM))
    cut = shape(own, 2, (WIDE + EDGE) * LANES)
    near = shape(own, 2, 2 * EDGE * LANES)
    pack_rows = 2 * own * rows + 2 * steps * own + 3 * steps
    pack = shape(pack_rows + -pack_rows % 8, LANES)
    even_out, odd_out, even_near, odd_near, pack_out, cot_out = pl.pallas_call(
        k_begin,
        out_shape=[cut, cut, near, near, pack, shape(own, 2, rows, LANES)],
        in_specs=[hbm] * len(inputs),
        out_specs=[vmem] * 6,
        scratch_shapes=[pltpu.VMEM(a.shape, a.dtype) for a in inputs]
        + [pltpu.SemaphoreType.DMA((len(inputs),))],
        compiler_params=pltpu.CompilerParams(vmem_limit_bytes=24 * 1024 * 1024),
        cost_estimate=pl.CostEstimate(flops=10**8, bytes_accessed=10**6, transcendentals=0),
    )(*(pltpu.with_memory_space_constraint(a, pltpu.HBM) for a in inputs))

    packs, cots, first_cot = [pack_out], [cot_out], [WIDE]
    sides = [neighbours(even_out, odd_out, False)]
    if doubled:
        packs.append(swapped(pack_out, "band", evenly, False))
        sides.append((aslant(even_near, evenly), aslant(odd_near, oddly)))
        cots.append(swapped(cot_out, "band", evenly, False))
        first_cot.append(EDGE)
    tiny = [shape(steps, own, dtype=d) for d in (jnp.int32, jnp.int32, F32)]
    setup = functools.partial(k_setup, steps, rows)
    made = [call(setup, (p,), tiny + [table] * (2 * steps)) for p in packs]
    delays, shifts, gains, high0, low0, high1, low1 = (list(m) for m in zip(*made))

    shifted0, linear, sent = call(
        k_first, (delays[:1], shifts[:1], pack_out, sides[0], high0[0], low0[0]),
        [own_field, own_field, wide_part], (ext_wide, held_wide),
    )
    spread0 = summed(over_cores(sent), "band")
    linear0 = [linear]
    if doubled:
        linear0 += call(
            k_beside, (shifts[1:], packs[1], sides[1], high0[1], low0[1]), [own_field],
            ((own, 2, held_rows, LANES),),
        )
    (cot_rows,) = call(
        lambda c, s, out: k_cotangent(c, s, first_cot, out), (cots, sides), [field]
    )
    cosine0, sine0, field1, shifted1, linear1, sent = call(
        k_second, (delays, shifts, gains, linear0, spread0, high1, low1),
        [angle, angle, field, own_field, field, part], (held_in, held_out),
    )
    turned1, sent = call(
        k_third, (delays, gains, linear1, *exchanged(sent, doubled), cot_rows),
        [field, part], (spread, held_in, held_out),
    )
    grad1, turned0, sent = call(
        k_fourth,
        (delays, shifts, gains, turned1, linear1, *exchanged(sent, doubled), high1, low1,
         cosine0, sine0, field1),
        [own_field, own_field, part], (spread, held_in, held_out),
    )
    (taps1,) = call(k_taps, (shifted1, grad1), [shape(2 * own, LANES)])
    scale = 1.0 / math.sqrt(2.0 * length * lax.axis_size("tm"))
    grad0, grad_taps = call(
        functools.partial(k_fifth, scale),
        (delays[:1], turned0, linear, *exchanged(sent, doubled), shifted0, taps1),
        [own_field, shape(steps * 2 * own, LANES)], (spread, held_in),
    )
    (grad_signal,) = call(
        k_last, (shifts[:1], grad0, high0[0], low0[0]), [shape(own, 1, 2, length)]
    )
    grad_taps = over_tm(over_cores(grad_taps))
    return grad_signal, grad_taps.reshape(steps, own, 2, LANES)


def solution(mesh):
    return jax.shard_map(
        on_device,
        mesh=mesh,
        in_specs=(
            P(("groups", "band"), "pol", None, "tm"),
            P(("groups", "band"), "pol", None, "tm"),
            P(None, "band", None, None),
            P(None, "band"),
            P(None, "band"),
            P(None, "band"),
        ),
        out_specs=(P(("groups", "band"), "pol", None, "tm"), P("groups", "band", None, None)),
        check_vma=False,
    )
```

```python
import functools
import math

import jax
import jax.numpy as jnp
from jax import lax
from jax.experimental import pallas as pl
from jax.experimental.pallas import tpu as pltpu
from jax.sharding import PartitionSpec as P

LANES = 128
REACH = 2048 // LANES
EDGE = 4
WIDE = REACH + 4
PAD = 8
WIDE_PAD = REACH + PAD
F32 = jnp.float32
BF16 = jnp.bfloat16

TWO_OVER_PI = 2.0 / math.pi
HALF_PI_1 = 1.5625
HALF_PI_2 = 67.0 / 8192.0
HALF_PI_3 = 123.0 / 1048576.0
HALF_PI_4 = math.pi / 2.0 - HALF_PI_1 - HALF_PI_2 - HALF_PI_3


def split(x):
    high = x.astype(BF16)
    return high, (x - high.astype(F32)).astype(BF16)


def sine_cosine(x):
    turns = jnp.floor(x * TWO_OVER_PI + 0.5)
    quadrant = turns.astype(jnp.int32)
    r = x - turns * HALF_PI_1
    r = r - turns * HALF_PI_2
    r = r - turns * HALF_PI_3
    r = r - turns * HALF_PI_4
    r2 = r * r
    s = r + r * r2 * (-1.6666654611e-1 + r2 * (8.3321608736e-3 + r2 * -1.9515295891e-4))
    c = 1.0 - 0.5 * r2 + r2 * r2 * (
        4.166664568298827e-2 + r2 * (-1.388731625493765e-3 + r2 * 2.443315711809948e-5)
    )
    odd = (quadrant & 1) == 1
    sine = jnp.where(odd, c, s)
    cosine = jnp.where(odd, s, c)
    sine = jnp.where((quadrant & 2) == 2, -sine, sine)
    cosine = jnp.where(((quadrant + 1) & 2) == 2, -cosine, cosine)
    return sine, cosine


def lanes_of(shape):
    return lax.broadcasted_iota(jnp.int32, shape, len(shape) - 1)


def later(x, amount):
    rolled = pltpu.roll(x, amount & (LANES - 1), 1)
    return jnp.where(lanes_of(x.shape) >= amount, rolled, pltpu.roll(rolled, 1, 0))


def earlier(x, amount):
    rows = x.shape[0]
    rolled = pltpu.roll(x, (LANES - amount) & (LANES - 1), 1)
    follow = pltpu.roll(rolled, rows - 1, 0)
    return jnp.where(lanes_of(x.shape) + amount < LANES, rolled, follow)


def at(table, step, b):
    own = table[0].shape[1]
    return table[b // own][step, b % own]


def of(groups, b):
    own = groups[0].shape[0]
    return groups[b // own].at[b % own]


def is_even():
    return lax.rem(lax.axis_index("tm"), 2) == 0


def keep_inside(values, rows, pad=PAD):
    z = lax.axis_index("tm")
    row = lax.broadcasted_iota(jnp.int32, values.shape, 0)
    low = jnp.where(z == 0, pad, 0)
    high = jnp.where(z == lax.axis_size("tm") - 1, pad + rows, 2 * pad + rows)
    return jnp.where((row >= low) & (row < high), values, 0.0)


def from_sides(even_value, odd_value):
    z = lax.axis_index("tm")
    even = is_even()
    before = jnp.where(even, odd_value, even_value)
    after = jnp.where(even, even_value, odd_value)
    before = jnp.where(z == 0, 0.0, before)
    after = jnp.where(z == lax.axis_size("tm") - 1, 0.0, after)
    return before, after


def extend(out, b, even_in, odd_in, first, edge):
    own = even_in.shape[0]
    rows = out.shape[2]
    pad = edge + 4
    for c in range(2):
        out[b, c, 0:8, :] = jnp.zeros((8, LANES), F32)
        out[b, c, rows - 8 :, :] = jnp.zeros((8, LANES), F32)
    for r in range(edge):
        lanes = slice((first + r) * LANES, (first + r + 1) * LANES)
        before, after = from_sides(even_in[b % own, :, lanes], odd_in[b % own, :, lanes])
        for c in range(2):
            above = pad - edge + r
            below = rows - pad + r
            out[b, c, above : above + 1, :] = before[c : c + 1]
            out[b, c, below : below + 1, :] = after[c : c + 1]


def fir(real, imag, high, low):
    rows = real.shape[0]
    x = jnp.concatenate(
        [real, pltpu.roll(real, rows - 1, 0), imag, pltpu.roll(imag, rows - 1, 0)], 1
    )
    xh, xl = split(x)
    contract = (((1,), (1,)), ((), ()))
    both = lax.dot_general(jnp.concatenate([xh, xl], 0), high, contract, preferred_element_type=F32)
    rest = lax.dot_general(xh, low, contract, preferred_element_type=F32)
    y = both[:rows] + both[rows:] + rest
    return y[:, :LANES], y[:, LANES:]


def fir_adjoint(real, imag, high, low):
    rows = real.shape[0]
    xh, xl = split(jnp.concatenate([real, imag], 1))
    both = jnp.dot(jnp.concatenate([xh, xl], 0), high, preferred_element_type=F32)
    rest = jnp.dot(xh, low, preferred_element_type=F32)
    g = both[:rows] + both[rows:] + rest
    out_real = g[:, :LANES] + pltpu.roll(g[:, LANES : 2 * LANES], 1, 0)
    out_imag = g[:, 2 * LANES : 3 * LANES] + pltpu.roll(g[:, 3 * LANES :], 1, 0)
    return out_real, out_imag


def scatter_delayed(values, delays, step, held, out):
    bands = len(values)
    rows = values[0].shape[0]
    total = rows + REACH
    base = REACH + 8
    lane = lanes_of((total, LANES))
    acc = None
    for b in range(bands):
        delay = at(delays, step, b)
        q = lax.shift_right_logical(delay, 7)
        s = delay & (LANES - 1)
        held[b, 0:base, :] = jnp.zeros((base, LANES), F32)
        held[b, base : base + rows, :] = pltpu.roll(values[b], s, 1)
        held[b, base + rows :, :] = jnp.zeros((held.shape[1] - base - rows, LANES), F32)
        near = held[b, pl.ds(base - q, total), :]
        far = held[b, pl.ds(base - q - 1, total), :]
        part = jnp.where(lane >= s, near, far)
        acc = part if acc is None else acc + part
    out[...] = acc


def delayed_sum(values, delays, step, held, out):
    bands = len(values)
    count, total = values[0].shape[0], out.shape[0]
    lane = lanes_of((total, LANES))
    acc = None
    for b in range(bands):
        delay = at(delays, step, b)
        q = lax.shift_right_logical(delay, 7)
        s = delay & (LANES - 1)
        held[b, 0:8, :] = jnp.zeros((8, LANES), F32)
        held[b, 8 : 8 + count, :] = pltpu.roll(values[b], s, 1)
        near = held[b, pl.ds(8 + REACH - q, total), :]
        far = held[b, pl.ds(8 + REACH - q - 1, total), :]
        part = jnp.where(lane >= s, near, far)
        acc = part if acc is None else acc + part
    out[...] = acc


def end_at_last(values, rows):
    row = lax.broadcasted_iota(jnp.int32, values.shape, 0)
    last = lax.axis_index("tm") == lax.axis_size("tm") - 1
    return jnp.where(row < jnp.where(last, PAD + rows, values.shape[0]), values, 0.0)


def gather_spread(own, even_in, odd_in, spread, rows):
    before, after = from_sides(even_in[...], odd_in[...])
    total = rows + REACH + 2 * PAD
    spread[0:PAD, :] = before[rows - PAD : rows]
    spread[PAD:total - PAD, :] = own[...]
    spread[total - PAD : total, :] = after[REACH : REACH + PAD]
    spread[PAD : PAD + REACH, :] += before[rows : rows + REACH]
    spread[PAD + rows : PAD + rows + REACH, :] += after[0:REACH]
    return end_at_last(spread[...], rows)


def read_spread(values, delay, held, b, rows):
    total = values.shape[0]
    q = lax.shift_right_logical(delay, 7)
    s = delay & (LANES - 1)
    held[b, 0:total, :] = pltpu.roll(values, (LANES - s) & (LANES - 1), 1)
    held[b, total:, :] = jnp.zeros((held.shape[1] - total, LANES), F32)
    count = rows + 2 * PAD
    near = held[b, pl.ds(q, count), :]
    far = held[b, pl.ds(q + 1, count), :]
    return jnp.where(lanes_of((count, LANES)) + s < LANES, near, far)


def k_begin(
    signal, cotangent, taps, delays, shifts, gains,
    even_out, odd_out, even_near, odd_near, sent, cot_rows,
    sig_held, cot_held, taps_held, delays_held, shifts_held, gains_held, done,
):
    steps, bands = taps.shape[:2]
    rows = cot_rows.shape[2]
    pairs = (
        (signal, sig_held), (cotangent, cot_held), (taps, taps_held),
        (delays, delays_held), (shifts, shifts_held), (gains, gains_held),
    )
    copies = [pltpu.make_async_copy(a, b, done.at[n]) for n, (a, b) in enumerate(pairs)]
    for copy in copies:
        copy.start()
    for copy in copies:
        copy.wait()
    even = is_even()
    length, wide, edge = rows * LANES, WIDE * LANES, EDGE * LANES
    for b in range(bands):
        for targets, held, first, width in (
            ((even_out, odd_out), sig_held, 0, wide),
            ((even_out, odd_out), cot_held, wide, edge),
            ((even_near, odd_near), sig_held, 0, edge),
            ((even_near, odd_near), cot_held, edge, edge),
        ):
            left = held[b, 0, :, 0:width]
            right = held[b, 0, :, length - width : length]
            targets[0][b, :, first : first + width] = jnp.where(even, right, left)
            targets[1][b, :, first : first + width] = jnp.where(even, left, right)
        for r in range(rows):
            lanes = slice(r * LANES, (r + 1) * LANES)
            pair = sig_held[b, 0, :, lanes]
            other = cot_held[b, 0, :, lanes]
            for c in range(2):
                row = (2 * b + c) * rows + r
                sent[row : row + 1, :] = pair[c : c + 1]
                cot_rows[b, c, r : r + 1, :] = other[c : c + 1]
    first = 2 * bands * rows
    for step in range(steps):
        for b in range(bands):
            row = first + 2 * (step * bands + b)
            sent[row : row + 2, :] = taps_held[step, b]
    first = first + 2 * steps * bands
    sent[first:, :] = jnp.zeros((sent.shape[0] - first, LANES), F32)
    for k, held in enumerate((delays_held, shifts_held, gains_held)):
        row = first + k * steps
        sent[row : row + steps, 0:bands] = held[...].astype(F32)


def k_setup(steps, rows, pack, delays, shifts, gains, *tables):
    bands = delays.shape[1]
    shape = (LANES, LANES)
    diagonal = lanes_of(shape) >= lax.broadcasted_iota(jnp.int32, shape, 0)
    base = 2 * bands * rows
    first = base + 2 * steps * bands
    for n, target in enumerate((delays, shifts, gains)):
        row = first + n * steps
        target[...] = pack[row : row + steps, 0:bands].astype(target.dtype)
    for b in range(bands):
        for step in range(steps):
            high, low = tables[2 * step : 2 * step + 2]
            for c in range(2):
                tap = base + 2 * (step * bands + b) + c
                row = jnp.broadcast_to(pack[tap : tap + 1, :], shape)
                ring = pltpu.roll(row, 0, 1, stride=1, stride_axis=0)
                near = jnp.where(diagonal, ring, 0.0)
                for place, half in ((0, near), (1, ring - near)):
                    for target, value in zip((high, low), split(half)):
                        a = place * LANES
                        d = (2 + place) * LANES
                        if c == 0:
                            target[b, 0:LANES, a : a + LANES] = value
                            target[b, LANES:, d : d + LANES] = value
                        else:
                            target[b, LANES:, a : a + LANES] = value
                            target[b, 0:LANES, d : d + LANES] = -value


def k_cotangent(cots, sides, first, out):
    own = cots[0].shape[0]
    rows = out.shape[2] - 2 * PAD
    for b in range(out.shape[0]):
        k = b // own
        extend(out, b, *sides[k], first[k], EDGE)
        for c in range(2):
            out[b, c, PAD : PAD + rows, :] = cots[k][b % own, c]


def widened(ext, pack, sides, edge, b):
    pad = edge + 4
    rows = ext.shape[2] - 2 * pad
    extend(ext, b, *sides, 0, edge)
    for c in range(2):
        row = (2 * b + c) * rows
        ext[b, c, pad : pad + rows, :] = pack[row : row + rows, :]


def k_first(delays, shifts, pack, sides, high, low, shifted, linear, out, ext, held):
    bands = linear.shape[0]
    rows = linear.shape[2] - 2 * PAD
    middle = slice(WIDE_PAD - PAD, WIDE_PAD + rows + PAD)
    powers = []
    for b in range(bands):
        widened(ext, pack, sides, WIDE, b)
        amount = LANES // 2 - at(shifts, 0, b)
        real = later(ext[b, 0], amount)
        imag = later(ext[b, 1], amount)
        shifted[b, 0] = real[middle]
        shifted[b, 1] = imag[middle]
        lr, li = fir(real, imag, high[b], low[b])
        linear[b, 0] = lr[middle]
        linear[b, 1] = li[middle]
        powers.append(keep_inside(lr * lr + li * li, rows, WIDE_PAD))
    delayed_sum(powers, delays, 0, held, out)


def k_beside(shifts, pack, sides, high, low, linear, ext):
    for b in range(linear.shape[0]):
        widened(ext, pack, sides, EDGE, b)
        amount = LANES // 2 - at(shifts, 0, b)
        real = later(ext[b, 0], amount)
        imag = later(ext[b, 1], amount)
        lr, li = fir(real, imag, high[b], low[b])
        linear[b, 0] = lr
        linear[b, 1] = li


def k_second(
    delays, shifts, gains, linear0, own, high, low,
    cosine0, sine0, field1, shifted, linear1, out, held, held_out,
):
    bands = linear1.shape[0]
    rows = linear1.shape[2] - 2 * PAD
    values = end_at_last(own[...], rows)
    powers = []
    for b in range(bands):
        spread = read_spread(values, at(delays, 0, b), held, b, rows)
        sine, cosine = sine_cosine(at(gains, 0, b) * spread)
        linear = of(linear0, b)
        lr, li = linear[0], linear[1]
        fr = keep_inside(lr * cosine - li * sine, rows)
        fi = keep_inside(lr * sine + li * cosine, rows)
        field1[b, 0] = fr
        field1[b, 1] = fi
        amount = LANES // 2 - at(shifts, 1, b)
        real = later(fr, amount)
        imag = later(fi, amount)
        if b < shifted.shape[0]:
            cosine0[b] = cosine
            sine0[b] = sine
            shifted[b, 0] = real
            shifted[b, 1] = imag
        lr, li = fir(real, imag, of(high, b)[...], of(low, b)[...])
        linear1[b, 0] = lr
        linear1[b, 1] = li
        lr, li = lr[PAD : PAD + rows], li[PAD : PAD + rows]
        powers.append(lr * lr + li * li)
    scatter_delayed(powers, delays, 1, held_out, out)


def k_third(
    delays, gains, linear1, own, even_in, odd_in, cotangent, turned1, out, spread, held, held_out
):
    bands = linear1.shape[0]
    rows = linear1.shape[2] - 2 * PAD
    values = gather_spread(own, even_in, odd_in, spread, rows)
    terms = []
    for b in range(bands):
        gain = at(gains, 1, b)
        phase = gain * read_spread(values, at(delays, 1, b), held, b, rows)
        sine, cosine = sine_cosine(phase)
        gr, gi = cotangent[b, 0], cotangent[b, 1]
        er = gr * cosine + gi * sine
        ei = gi * cosine - gr * sine
        turned1[b, 0] = er
        turned1[b, 1] = ei
        term = ei * linear1[b, 0] - er * linear1[b, 1]
        terms.append(gain * term[PAD : PAD + rows])
    scatter_delayed(terms, delays, 1, held_out, out)


def k_fourth(
    delays, shifts, gains, turned1, linear1, own, even_in, odd_in, high, low, cosine0, sine0, field1,
    grad1, turned0, out, spread, held, held_out,
):
    bands = linear1.shape[0]
    rows = linear1.shape[2] - 2 * PAD
    values = gather_spread(own, even_in, odd_in, spread, rows)
    terms = []
    for b in range(bands):
        twice = 2.0 * read_spread(values, at(delays, 1, b), held, b, rows)
        gr = keep_inside(turned1[b, 0] + linear1[b, 0] * twice, rows)
        gi = keep_inside(turned1[b, 1] + linear1[b, 1] * twice, rows)
        if b < grad1.shape[0]:
            grad1[b, 0] = gr
            grad1[b, 1] = gi
        gr, gi = fir_adjoint(gr, gi, of(high, b)[...], of(low, b)[...])
        amount = LANES // 2 - at(shifts, 1, b)
        gr = earlier(gr, amount)
        gi = earlier(gi, amount)
        if b < grad1.shape[0]:
            cosine, sine = cosine0[b], sine0[b]
            turned0[b, 0] = gr * cosine + gi * sine
            turned0[b, 1] = gi * cosine - gr * sine
        term = gi * field1[b, 0] - gr * field1[b, 1]
        terms.append(at(gains, 0, b) * term[PAD : PAD + rows])
    scatter_delayed(terms, delays, 0, held_out, out)


def correlate(real, imag, grad_real, grad_imag, rows):
    inside = slice(PAD, PAD + rows)
    following = slice(PAD + 1, PAD + rows + 1)
    a = jnp.concatenate(
        [
            jnp.concatenate([real[inside], real[following]], 1),
            jnp.concatenate([imag[inside], imag[following]], 1),
        ],
        0,
    )
    gr, gi = grad_real[inside], grad_imag[inside]
    d = jnp.concatenate([jnp.concatenate([gr, gi], 1), jnp.concatenate([gi, -gr], 1)], 0)
    ah, al = split(a)
    dh, dl = split(d)
    table = lax.dot_general(
        jnp.concatenate([dh, dh, dl], 0),
        jnp.concatenate([ah, al, ah], 0),
        (((0,), (0,)), ((), ())),
        preferred_element_type=F32,
    )
    width = 2 * LANES
    results = []
    for c in range(2):
        acc = table[c * LANES : c * LANES + 8]
        for g in range(1, LANES // 8):
            first = c * LANES + 8 * g
            acc = acc + pltpu.roll(table[first : first + 8], width - 8 * g, 1)
        total = acc[0:1]
        for s in range(1, 8):
            total = total + pltpu.roll(acc, width - s, 1)[s : s + 1]
        results.append(total[:, :LANES])
    return results


def k_taps(shifted, grad, out):
    bands = grad.shape[0]
    rows = grad.shape[2] - 2 * PAD
    for b in range(bands):
        parts = correlate(shifted[b, 0], shifted[b, 1], grad[b, 0], grad[b, 1], rows)
        for c in range(2):
            out[2 * b + c : 2 * b + c + 1, :] = parts[c]


def k_fifth(
    scale, delays, turned0, linear0, own, even_in, odd_in, shifted, taps1,
    grad0, out, spread, held,
):
    bands = turned0.shape[0]
    rows = turned0.shape[2] - 2 * PAD
    values = gather_spread(own, even_in, odd_in, spread, rows)
    for b in range(bands):
        twice = 2.0 * read_spread(values, at(delays, 0, b), held, b, rows)
        gr = keep_inside(turned0[b, 0] + linear0[b, 0] * twice, rows)
        gi = keep_inside(turned0[b, 1] + linear0[b, 1] * twice, rows)
        grad0[b, 0] = gr
        grad0[b, 1] = gi
        parts = correlate(shifted[b, 0], shifted[b, 1], gr, gi, rows)
        for c in range(2):
            out[2 * b + c : 2 * b + c + 1, :] = parts[c] * scale
    out[2 * bands :, :] = taps1[...] * scale


def k_last(shifts, grad0, high, low, result):
    bands = grad0.shape[0]
    rows = grad0.shape[2] - 2 * PAD
    for b in range(bands):
        gr, gi = fir_adjoint(grad0[b, 0], grad0[b, 1], high[b], low[b])
        amount = LANES // 2 - at(shifts, 0, b)
        gr = earlier(gr, amount)[PAD : PAD + rows]
        gi = earlier(gi, amount)[PAD : PAD + rows]
        for r in range(rows):
            result[b, 0, 0:1, r * LANES : (r + 1) * LANES] = gr[r : r + 1]
            result[b, 0, 1:2, r * LANES : (r + 1) * LANES] = gi[r : r + 1]


def call(kernel, arrays, shapes, scratch=(), micros=2.0):
    vmem = pl.BlockSpec(memory_space=pltpu.VMEM)
    return pl.pallas_call(
        kernel,
        out_shape=shapes,
        in_specs=jax.tree.map(lambda _: vmem, arrays),
        out_specs=[vmem] * len(shapes),
        scratch_shapes=[pltpu.VMEM(s, F32) for s in scratch],
        compiler_params=pltpu.CompilerParams(vmem_limit_bytes=24 * 1024 * 1024),
        cost_estimate=pl.CostEstimate(
            flops=int(micros * 1e8), bytes_accessed=int(micros * 3e6), transcendentals=0
        ),
    )(*arrays)


def swapped(x, axis, partner, cross):
    size, cores = lax.axis_size(axis), lax.axis_size("pol")
    pairs = []
    for i in range(size):
        for p in range(cores):
            j, q = partner(i), cores - 1 - p
            if 0 <= j < size:
                pairs.append((i * cores + p, j * cores + (q if cross else p)))
            else:
                pairs.append((i * cores + p, i * cores + q))
    return lax.ppermute(x, (axis, "pol"), pairs)


def summed(x, axis, cross=True):
    size = lax.axis_size(axis)
    if size & (size - 1):
        return lax.psum(x, axis)
    distance = 1
    while distance < size:
        x = x + swapped(x, axis, lambda i, d=distance: i ^ d, cross)
        distance *= 2
    return x


def over_cores(x):
    cores = lax.axis_size("pol")
    return x + lax.ppermute(x, "pol", [(p, cores - 1 - p) for p in range(cores)])


def evenly(i):
    return i ^ 1


def oddly(i):
    return ((i + 1) ^ 1) - 1


def neighbours(even_out, odd_out, cross):
    odd_in = swapped(odd_out, "tm", oddly, cross)
    even_in = swapped(even_out, "tm", evenly, cross)
    return even_in, odd_in


def aslant(x, partner):
    size, cores = lax.axis_size("tm"), lax.axis_size("pol")
    pairs = []
    for i in range(size):
        for b in range(2):
            for p in range(cores):
                here = (i * 2 + b) * cores
                j = partner(i)
                if 0 <= j < size:
                    pairs.append((here + p, (j * 2 + 1 - b) * cores + p))
                else:
                    pairs.append((here + p, here + cores - 1 - p))
    return lax.ppermute(x, ("tm", "band", "pol"), pairs)


def over_tm(x):
    if lax.axis_size("tm") != 4:
        return summed(x, "tm")
    others = [swapped(x, "tm", lambda i, d=d: i ^ d, True) for d in (1, 2, 3)]
    return (x + others[0]) + (others[1] + others[2])


def exchanged(part, doubled):
    part = over_cores(part)
    part = part if doubled else summed(part, "band")
    return (part,) + neighbours(part, part, True)


def on_device(signal, cotangent, taps, gains, walk_off, tap_shift):
    own, _, _, length = signal.shape
    steps = taps.shape[0]
    rows = length // LANES
    held_rows = rows + 2 * PAD
    doubled = lax.axis_size("band") == 2
    groups = 2 if doubled else 1
    bands = groups * own

    def shape(*dims, dtype=F32):
        return jax.ShapeDtypeStruct(dims, dtype)

    field = shape(bands, 2, held_rows, LANES)
    own_field = shape(own, 2, held_rows, LANES)
    angle = shape(own, held_rows, LANES)
    wide_part = shape(rows + REACH + 2 * PAD, LANES)
    part = shape(rows + REACH, LANES)
    table = shape(own, 2 * LANES, 4 * LANES, dtype=BF16)
    ext_wide = (own, 2, rows + 2 * WIDE_PAD, LANES)
    held_wide = (own, rows + 2 * WIDE_PAD + 8, LANES)
    spread = (rows + REACH + 2 * PAD, LANES)
    held_in = (bands, rows + REACH + 3 * PAD, LANES)
    held_out = (bands, rows + 3 * REACH, LANES)

    inputs = (signal, cotangent, taps, walk_off, tap_shift, gains)
    hbm, vmem = (pl.BlockSpec(memory_space=m) for m in (pltpu.HBM, pltpu.VMEM))
    cut = shape(own, 2, (WIDE + EDGE) * LANES)
    near = shape(own, 2, 2 * EDGE * LANES)
    pack_rows = 2 * own * rows + 2 * steps * own + 3 * steps
    pack = shape(pack_rows + -pack_rows % 8, LANES)
    even_out, odd_out, even_near, odd_near, pack_out, cot_out = pl.pallas_call(
        k_begin,
        out_shape=[cut, cut, near, near, pack, shape(own, 2, rows, LANES)],
        in_specs=[hbm] * len(inputs),
        out_specs=[vmem] * 6,
        scratch_shapes=[pltpu.VMEM(a.shape, a.dtype) for a in inputs]
        + [pltpu.SemaphoreType.DMA((len(inputs),))],
        compiler_params=pltpu.CompilerParams(vmem_limit_bytes=24 * 1024 * 1024),
        cost_estimate=pl.CostEstimate(flops=10**8, bytes_accessed=10**6, transcendentals=0),
    )(*(pltpu.with_memory_space_constraint(a, pltpu.HBM) for a in inputs))

    packs, cots, first_cot = [pack_out], [cot_out], [WIDE]
    sides = [neighbours(even_out, odd_out, False)]
    if doubled:
        packs.append(swapped(pack_out, "band", evenly, False))
        sides.append((aslant(even_near, evenly), aslant(odd_near, oddly)))
        cots.append(swapped(cot_out, "band", evenly, False))
        first_cot.append(EDGE)
    tiny = [shape(steps, own, dtype=d) for d in (jnp.int32, jnp.int32, F32)]
    setup = functools.partial(k_setup, steps, rows)
    made = [call(setup, (p,), tiny + [table] * (2 * steps)) for p in packs]
    delays, shifts, gains, high0, low0, high1, low1 = (list(m) for m in zip(*made))

    shifted0, linear, sent = call(
        k_first, (delays[:1], shifts[:1], pack_out, sides[0], high0[0], low0[0]),
        [own_field, own_field, wide_part], (ext_wide, held_wide),
    )
    sent, sides = lax.optimization_barrier((sent, sides))
    spread0 = summed(over_cores(sent), "band")
    linear0 = [linear]
    if doubled:
        linear0 += call(
            k_beside, (shifts[1:], packs[1], sides[1], high0[1], low0[1]), [own_field],
            ((own, 2, held_rows, LANES),),
        )
    (cot_rows,) = call(
        lambda c, s, out: k_cotangent(c, s, first_cot, out), (cots, sides), [field]
    )
    cosine0, sine0, field1, shifted1, linear1, sent = call(
        k_second, (delays, shifts, gains, linear0, spread0, high1, low1),
        [angle, angle, field, own_field, field, part], (held_in, held_out),
    )
    turned1, sent = call(
        k_third, (delays, gains, linear1, *exchanged(sent, doubled), cot_rows),
        [field, part], (spread, held_in, held_out),
    )
    grad1, turned0, sent = call(
        k_fourth,
        (delays, shifts, gains, turned1, linear1, *exchanged(sent, doubled), high1, low1,
         cosine0, sine0, field1),
        [own_field, own_field, part], (spread, held_in, held_out),
    )
    (taps1,) = call(k_taps, (shifted1, grad1), [shape(2 * own, LANES)])
    scale = 1.0 / math.sqrt(2.0 * length * lax.axis_size("tm"))
    grad0, grad_taps = call(
        functools.partial(k_fifth, scale),
        (delays[:1], turned0, linear, *exchanged(sent, doubled), shifted0, taps1),
        [own_field, shape(steps * 2 * own, LANES)], (spread, held_in),
    )
    (grad_signal,) = call(
        k_last, (shifts[:1], grad0, high0[0], low0[0]), [shape(own, 1, 2, length)]
    )
    grad_taps = over_tm(over_cores(grad_taps))
    return grad_signal, grad_taps.reshape(steps, own, 2, LANES)


def solution(mesh):
    return jax.shard_map(
        on_device,
        mesh=mesh,
        in_specs=(
            P(("groups", "band"), "pol", None, "tm"),
            P(("groups", "band"), "pol", None, "tm"),
            P(None, "band", None, None),
            P(None, "band"),
            P(None, "band"),
            P(None, "band"),
        ),
        out_specs=(P(("groups", "band"), "pol", None, "tm"), P("groups", "band", None, None)),
        check_vma=False,
    )
```

```python
import functools
import math

import jax
import jax.numpy as jnp
from jax import lax
from jax.experimental import pallas as pl
from jax.experimental.pallas import tpu as pltpu
from jax.sharding import PartitionSpec as P

LANES = 128
REACH = 2048 // LANES
EDGE = 4
WIDE = REACH + 4
PAD = 8
WIDE_PAD = REACH + PAD
F32 = jnp.float32
BF16 = jnp.bfloat16

TWO_OVER_PI = 2.0 / math.pi
HALF_PI_1 = 1.5625
HALF_PI_2 = 67.0 / 8192.0
HALF_PI_3 = 123.0 / 1048576.0
HALF_PI_4 = math.pi / 2.0 - HALF_PI_1 - HALF_PI_2 - HALF_PI_3


def split(x):
    high = x.astype(BF16)
    return high, (x - high.astype(F32)).astype(BF16)


def sine_cosine(x):
    turns = jnp.floor(x * TWO_OVER_PI + 0.5)
    quadrant = turns.astype(jnp.int32)
    r = x - turns * HALF_PI_1
    r = r - turns * HALF_PI_2
    r = r - turns * HALF_PI_3
    r = r - turns * HALF_PI_4
    r2 = r * r
    s = r + r * r2 * (-1.6666654611e-1 + r2 * (8.3321608736e-3 + r2 * -1.9515295891e-4))
    c = 1.0 - 0.5 * r2 + r2 * r2 * (
        4.166664568298827e-2 + r2 * (-1.388731625493765e-3 + r2 * 2.443315711809948e-5)
    )
    odd = (quadrant & 1) == 1
    sine = jnp.where(odd, c, s)
    cosine = jnp.where(odd, s, c)
    sine = jnp.where((quadrant & 2) == 2, -sine, sine)
    cosine = jnp.where(((quadrant + 1) & 2) == 2, -cosine, cosine)
    return sine, cosine


def lanes_of(shape):
    return lax.broadcasted_iota(jnp.int32, shape, len(shape) - 1)


def later(x, amount):
    rolled = pltpu.roll(x, amount & (LANES - 1), 1)
    return jnp.where(lanes_of(x.shape) >= amount, rolled, pltpu.roll(rolled, 1, 0))


def earlier(x, amount):
    rows = x.shape[0]
    rolled = pltpu.roll(x, (LANES - amount) & (LANES - 1), 1)
    follow = pltpu.roll(rolled, rows - 1, 0)
    return jnp.where(lanes_of(x.shape) + amount < LANES, rolled, follow)


def at(table, step, b):
    own = table[0].shape[1]
    return table[b // own][step, b % own]


def of(groups, b):
    own = groups[0].shape[0]
    return groups[b // own].at[b % own]


def is_even():
    return lax.rem(lax.axis_index("tm"), 2) == 0


def keep_inside(values, rows, pad=PAD):
    z = lax.axis_index("tm")
    row = lax.broadcasted_iota(jnp.int32, values.shape, 0)
    low = jnp.where(z == 0, pad, 0)
    high = jnp.where(z == lax.axis_size("tm") - 1, pad + rows, 2 * pad + rows)
    return jnp.where((row >= low) & (row < high), values, 0.0)


def from_sides(even_value, odd_value):
    z = lax.axis_index("tm")
    even = is_even()
    before = jnp.where(even, odd_value, even_value)
    after = jnp.where(even, even_value, odd_value)
    before = jnp.where(z == 0, 0.0, before)
    after = jnp.where(z == lax.axis_size("tm") - 1, 0.0, after)
    return before, after


def extend(out, b, even_in, odd_in, first, edge):
    own = even_in.shape[0]
    rows = out.shape[2]
    pad = edge + 4
    for c in range(2):
        out[b, c, 0:8, :] = jnp.zeros((8, LANES), F32)
        out[b, c, rows - 8 :, :] = jnp.zeros((8, LANES), F32)
    for r in range(edge):
        lanes = slice((first + r) * LANES, (first + r + 1) * LANES)
        before, after = from_sides(even_in[b % own, :, lanes], odd_in[b % own, :, lanes])
        for c in range(2):
            above = pad - edge + r
            below = rows - pad + r
            out[b, c, above : above + 1, :] = before[c : c + 1]
            out[b, c, below : below + 1, :] = after[c : c + 1]


def three_passes(x, high, low, transposed):
    rows = x.shape[0]
    xh, xl = split(x)
    contract = (((1,), (1 if transposed else 0,)), ((), ()))
    both = lax.dot_general(jnp.concatenate([xh, xl], 0), high, contract, preferred_element_type=F32)
    rest = lax.dot_general(xh, low, contract, preferred_element_type=F32)
    return both[:rows] + both[rows:] + rest


def fir(real, imag, high, low):
    rows = real.shape[0]
    x = [jnp.concatenate([part, pltpu.roll(part, rows - 1, 0)], 1) for part in (real, imag)]
    y = three_passes(jnp.concatenate(x, 0), high, low, True)
    first, second = y[:rows], y[rows:]
    return first[:, :LANES] - second[:, LANES:], first[:, LANES:] + second[:, :LANES]


def fir_adjoint(real, imag, high, low):
    rows = real.shape[0]
    x = [jnp.concatenate([real, imag], 1), jnp.concatenate([imag, -real], 1)]
    g = three_passes(jnp.concatenate(x, 0), high, low, False)
    parts = (g[:rows], g[rows:])
    return [part[:, :LANES] + pltpu.roll(part[:, LANES:], 1, 0) for part in parts]


def scatter_delayed(values, delays, step, held, out):
    bands = held.shape[0]
    base = REACH + 8
    total = out.shape[0]
    rows = total - REACH
    lane = lanes_of((total, LANES))
    parts = []
    for b, value in enumerate(values):
        delay = at(delays, step, b)
        parts.append((lax.shift_right_logical(delay, 7), delay & (LANES - 1)))
        held[b, 0:base, :] = jnp.zeros((base, LANES), F32)
        held[b, base : base + rows, :] = pltpu.roll(value, parts[b][1], 1)
        held[b, base + rows :, :] = jnp.zeros((held.shape[1] - base - rows, LANES), F32)
    acc = None
    for b, (q, s) in enumerate(parts):
        near = held[b, pl.ds(base - q, total), :]
        far = held[b, pl.ds(base - q - 1, total), :]
        part = jnp.where(lane >= s, near, far)
        acc = part if acc is None else acc + part
    out[...] = acc


def delayed_sum(values, delays, step, held, out):
    bands = len(values)
    count, total = values[0].shape[0], out.shape[0]
    lane = lanes_of((total, LANES))
    acc = None
    for b in range(bands):
        delay = at(delays, step, b)
        q = lax.shift_right_logical(delay, 7)
        s = delay & (LANES - 1)
        held[b, 0:8, :] = jnp.zeros((8, LANES), F32)
        held[b, 8 : 8 + count, :] = pltpu.roll(values[b], s, 1)
        near = held[b, pl.ds(8 + REACH - q, total), :]
        far = held[b, pl.ds(8 + REACH - q - 1, total), :]
        part = jnp.where(lane >= s, near, far)
        acc = part if acc is None else acc + part
    out[...] = acc


def end_at_last(values, rows):
    row = lax.broadcasted_iota(jnp.int32, values.shape, 0)
    last = lax.axis_index("tm") == lax.axis_size("tm") - 1
    return jnp.where(row < jnp.where(last, PAD + rows, values.shape[0]), values, 0.0)


def gather_spread(own, even_in, odd_in, spread, rows):
    before, after = from_sides(even_in[...], odd_in[...])
    total = rows + REACH + 2 * PAD
    spread[0:PAD, :] = before[rows - PAD : rows]
    spread[PAD:total - PAD, :] = own[...]
    spread[total - PAD : total, :] = after[REACH : REACH + PAD]
    spread[PAD : PAD + REACH, :] += before[rows : rows + REACH]
    spread[PAD + rows : PAD + rows + REACH, :] += after[0:REACH]
    return end_at_last(spread[...], rows)


def read_spread(values, delays, step, held, rows):
    bands, total = held.shape[0], values.shape[0]
    count = rows + 2 * PAD
    lane = lanes_of((count, LANES))
    parts = []
    for b in range(bands):
        delay = at(delays, step, b)
        parts.append((lax.shift_right_logical(delay, 7), delay & (LANES - 1)))
    for b, (_, s) in enumerate(parts):
        held[b, 0:total, :] = pltpu.roll(values, (LANES - s) & (LANES - 1), 1)
        held[b, total:, :] = jnp.zeros((held.shape[1] - total, LANES), F32)
    for b, (q, s) in enumerate(parts):
        near = held[b, pl.ds(q, count), :]
        far = held[b, pl.ds(q + 1, count), :]
        yield jnp.where(lane + s < LANES, near, far)


def k_begin(
    signal, cotangent, taps, delays, shifts, gains,
    even_out, odd_out, even_near, odd_near, sent, cot_rows,
    sig_held, cot_held, taps_held, delays_held, shifts_held, gains_held, done,
):
    steps, bands = taps.shape[:2]
    rows = cot_rows.shape[2]
    pairs = (
        (signal, sig_held), (cotangent, cot_held), (taps, taps_held),
        (delays, delays_held), (shifts, shifts_held), (gains, gains_held),
    )
    copies = [pltpu.make_async_copy(a, b, done.at[n]) for n, (a, b) in enumerate(pairs)]
    for copy in copies:
        copy.start()
    for copy in copies:
        copy.wait()
    even = is_even()
    length, wide, edge = rows * LANES, WIDE * LANES, EDGE * LANES
    for b in range(bands):
        for targets, held, first, width in (
            ((even_out, odd_out), sig_held, 0, wide),
            ((even_out, odd_out), cot_held, wide, edge),
            ((even_near, odd_near), sig_held, 0, edge),
            ((even_near, odd_near), cot_held, edge, edge),
        ):
            left = held[b, 0, :, 0:width]
            right = held[b, 0, :, length - width : length]
            targets[0][b, :, first : first + width] = jnp.where(even, right, left)
            targets[1][b, :, first : first + width] = jnp.where(even, left, right)
        for r in range(rows):
            lanes = slice(r * LANES, (r + 1) * LANES)
            pair = sig_held[b, 0, :, lanes]
            other = cot_held[b, 0, :, lanes]
            for c in range(2):
                row = (2 * b + c) * rows + r
                sent[row : row + 1, :] = pair[c : c + 1]
                cot_rows[b, c, r : r + 1, :] = other[c : c + 1]
    first = 2 * bands * rows
    for step in range(steps):
        for b in range(bands):
            row = first + 2 * (step * bands + b)
            sent[row : row + 2, :] = taps_held[step, b]
    first = first + 2 * steps * bands
    sent[first:, :] = jnp.zeros((sent.shape[0] - first, LANES), F32)
    for k, held in enumerate((delays_held, shifts_held, gains_held)):
        row = first + k * steps
        sent[row : row + steps, 0:bands] = held[...].astype(F32)


def k_setup(steps, rows, pack, delays, shifts, gains, *tables):
    bands = delays.shape[1]
    shape = (LANES, LANES)
    diagonal = lanes_of(shape) >= lax.broadcasted_iota(jnp.int32, shape, 0)
    base = 2 * bands * rows
    first = base + 2 * steps * bands
    for n, target in enumerate((delays, shifts, gains)):
        row = first + n * steps
        target[...] = pack[row : row + steps, 0:bands].astype(target.dtype)
    for b in range(bands):
        for step in range(steps):
            high, low = tables[2 * step : 2 * step + 2]
            for c in range(2):
                tap = base + 2 * (step * bands + b) + c
                row = jnp.broadcast_to(pack[tap : tap + 1, :], shape)
                ring = pltpu.roll(row, 0, 1, stride=1, stride_axis=0)
                near = jnp.where(diagonal, ring, 0.0)
                rows_of = slice(c * LANES, (c + 1) * LANES)
                for place, half in enumerate((near, ring - near)):
                    lanes = slice(place * LANES, (place + 1) * LANES)
                    high[b, rows_of, lanes], low[b, rows_of, lanes] = split(half)


def k_cotangent(cots, sides, first, out):
    own = cots[0].shape[0]
    rows = out.shape[2] - 2 * PAD
    for b in range(out.shape[0]):
        k = b // own
        extend(out, b, *sides[k], first[k], EDGE)
        for c in range(2):
            out[b, c, PAD : PAD + rows, :] = cots[k][b % own, c]


def widened(ext, pack, sides, edge, b):
    pad = edge + 4
    rows = ext.shape[2] - 2 * pad
    extend(ext, b, *sides, 0, edge)
    for c in range(2):
        row = (2 * b + c) * rows
        ext[b, c, pad : pad + rows, :] = pack[row : row + rows, :]


def k_first(delays, shifts, pack, sides, high, low, shifted, linear, out, ext, held):
    bands = linear.shape[0]
    rows = linear.shape[2] - 2 * PAD
    middle = slice(WIDE_PAD - PAD, WIDE_PAD + rows + PAD)
    powers = []
    for b in range(bands):
        widened(ext, pack, sides, WIDE, b)
        amount = LANES // 2 - at(shifts, 0, b)
        real = later(ext[b, 0], amount)
        imag = later(ext[b, 1], amount)
        shifted[b, 0] = real[middle]
        shifted[b, 1] = imag[middle]
        lr, li = fir(real, imag, high[b], low[b])
        linear[b, 0] = lr[middle]
        linear[b, 1] = li[middle]
        powers.append(keep_inside(lr * lr + li * li, rows, WIDE_PAD))
    delayed_sum(powers, delays, 0, held, out)


def k_beside(shifts, pack, sides, high, low, linear, ext):
    for b in range(linear.shape[0]):
        widened(ext, pack, sides, EDGE, b)
        amount = LANES // 2 - at(shifts, 0, b)
        real = later(ext[b, 0], amount)
        imag = later(ext[b, 1], amount)
        lr, li = fir(real, imag, high[b], low[b])
        linear[b, 0] = lr
        linear[b, 1] = li


def k_second(
    delays, shifts, gains, linear0, own, high, low,
    cosine0, sine0, field1, shifted, linear1, out, moved, held, held_out,
):
    bands = linear1.shape[0]
    rows = linear1.shape[2] - 2 * PAD
    values = end_at_last(own[...], rows)
    for b, spread in enumerate(read_spread(values, delays, 0, held, rows)):
        sine, cosine = sine_cosine(at(gains, 0, b) * spread)
        linear = of(linear0, b)
        lr, li = linear[0], linear[1]
        fr = keep_inside(lr * cosine - li * sine, rows)
        fi = keep_inside(lr * sine + li * cosine, rows)
        field1[b, 0] = fr
        field1[b, 1] = fi
        amount = LANES // 2 - at(shifts, 1, b)
        real = later(fr, amount)
        imag = later(fi, amount)
        moved[b, 0] = real
        moved[b, 1] = imag
        if b < shifted.shape[0]:
            cosine0[b] = cosine
            sine0[b] = sine
            shifted[b, 0] = real
            shifted[b, 1] = imag
    for b in range(bands):
        lr, li = fir(moved[b, 0], moved[b, 1], of(high, b)[...], of(low, b)[...])
        linear1[b, 0] = lr
        linear1[b, 1] = li
    inside = slice(PAD, PAD + rows)
    powers = (linear1[b, 0, inside] ** 2 + linear1[b, 1, inside] ** 2 for b in range(bands))
    scatter_delayed(powers, delays, 1, held_out, out)


def k_third(
    delays, gains, linear1, own, even_in, odd_in, cotangent, turned1, out, spread, held, held_out
):
    bands = linear1.shape[0]
    rows = linear1.shape[2] - 2 * PAD
    values = gather_spread(own, even_in, odd_in, spread, rows)
    terms = []
    for b, spread_b in enumerate(read_spread(values, delays, 1, held, rows)):
        gain = at(gains, 1, b)
        sine, cosine = sine_cosine(gain * spread_b)
        gr, gi = cotangent[b, 0], cotangent[b, 1]
        er = gr * cosine + gi * sine
        ei = gi * cosine - gr * sine
        turned1[b, 0] = er
        turned1[b, 1] = ei
        term = ei * linear1[b, 0] - er * linear1[b, 1]
        terms.append(gain * term[PAD : PAD + rows])
    scatter_delayed(terms, delays, 1, held_out, out)


def k_fourth(
    delays, shifts, gains, turned1, linear1, own, even_in, odd_in, high, low, cosine0, sine0, field1,
    grad1, turned0, out, spread, moved, held, held_out,
):
    bands = linear1.shape[0]
    rows = linear1.shape[2] - 2 * PAD
    values = gather_spread(own, even_in, odd_in, spread, rows)
    for b, spread_b in enumerate(read_spread(values, delays, 1, held, rows)):
        twice = 2.0 * spread_b
        gr = keep_inside(turned1[b, 0] + linear1[b, 0] * twice, rows)
        gi = keep_inside(turned1[b, 1] + linear1[b, 1] * twice, rows)
        moved[b, 0] = gr
        moved[b, 1] = gi
        if b < grad1.shape[0]:
            grad1[b, 0] = gr
            grad1[b, 1] = gi
    for b in range(bands):
        gr, gi = fir_adjoint(moved[b, 0], moved[b, 1], of(high, b)[...], of(low, b)[...])
        moved[b, 0] = gr
        moved[b, 1] = gi
    terms = []
    for b in range(bands):
        amount = LANES // 2 - at(shifts, 1, b)
        gr = earlier(moved[b, 0], amount)
        gi = earlier(moved[b, 1], amount)
        if b < grad1.shape[0]:
            cosine, sine = cosine0[b], sine0[b]
            turned0[b, 0] = gr * cosine + gi * sine
            turned0[b, 1] = gi * cosine - gr * sine
        term = gi * field1[b, 0] - gr * field1[b, 1]
        terms.append(at(gains, 0, b) * term[PAD : PAD + rows])
    scatter_delayed(terms, delays, 0, held_out, out)


def correlate(real, imag, grad_real, grad_imag, rows):
    inside = slice(PAD, PAD + rows)
    following = slice(PAD + 1, PAD + rows + 1)
    a = jnp.concatenate(
        [
            jnp.concatenate([real[inside], real[following]], 1),
            jnp.concatenate([imag[inside], imag[following]], 1),
        ],
        0,
    )
    gr, gi = grad_real[inside], grad_imag[inside]
    d = jnp.concatenate([jnp.concatenate([gr, gi], 1), jnp.concatenate([gi, -gr], 1)], 0)
    ah, al = split(a)
    dh, dl = split(d)
    table = lax.dot_general(
        jnp.concatenate([dh, dh, dl], 0),
        jnp.concatenate([ah, al, ah], 0),
        (((0,), (0,)), ((), ())),
        preferred_element_type=F32,
    )
    width = 2 * LANES
    results = []
    for c in range(2):
        acc = table[c * LANES : c * LANES + 8]
        for g in range(1, LANES // 8):
            first = c * LANES + 8 * g
            acc = acc + pltpu.roll(table[first : first + 8], width - 8 * g, 1)
        total = acc[0:1]
        for s in range(1, 8):
            total = total + pltpu.roll(acc, width - s, 1)[s : s + 1]
        results.append(total[:, :LANES])
    return results


def k_taps(shifted, grad, out):
    bands = grad.shape[0]
    rows = grad.shape[2] - 2 * PAD
    for b in range(bands):
        parts = correlate(shifted[b, 0], shifted[b, 1], grad[b, 0], grad[b, 1], rows)
        for c in range(2):
            out[2 * b + c : 2 * b + c + 1, :] = parts[c]


def k_fifth(
    scale, delays, turned0, linear0, own, even_in, odd_in, shifted, taps1,
    grad0, out, spread, held,
):
    bands = turned0.shape[0]
    rows = turned0.shape[2] - 2 * PAD
    values = gather_spread(own, even_in, odd_in, spread, rows)
    for b, spread_b in enumerate(read_spread(values, delays, 0, held, rows)):
        twice = 2.0 * spread_b
        gr = keep_inside(turned0[b, 0] + linear0[b, 0] * twice, rows)
        gi = keep_inside(turned0[b, 1] + linear0[b, 1] * twice, rows)
        grad0[b, 0] = gr
        grad0[b, 1] = gi
        parts = correlate(shifted[b, 0], shifted[b, 1], gr, gi, rows)
        for c in range(2):
            out[2 * b + c : 2 * b + c + 1, :] = parts[c] * scale
    out[2 * bands :, :] = taps1[...] * scale


def k_last(shifts, grad0, high, low, result):
    bands = grad0.shape[0]
    rows = grad0.shape[2] - 2 * PAD
    for b in range(bands):
        gr, gi = fir_adjoint(grad0[b, 0], grad0[b, 1], high[b], low[b])
        amount = LANES // 2 - at(shifts, 0, b)
        gr = earlier(gr, amount)[PAD : PAD + rows]
        gi = earlier(gi, amount)[PAD : PAD + rows]
        for r in range(rows):
            result[b, 0, 0:1, r * LANES : (r + 1) * LANES] = gr[r : r + 1]
            result[b, 0, 1:2, r * LANES : (r + 1) * LANES] = gi[r : r + 1]


def call(kernel, arrays, shapes, scratch=(), micros=2.0):
    vmem = pl.BlockSpec(memory_space=pltpu.VMEM)
    return pl.pallas_call(
        kernel,
        out_shape=shapes,
        in_specs=jax.tree.map(lambda _: vmem, arrays),
        out_specs=[vmem] * len(shapes),
        scratch_shapes=[pltpu.VMEM(s, F32) for s in scratch],
        compiler_params=pltpu.CompilerParams(vmem_limit_bytes=24 * 1024 * 1024),
        cost_estimate=pl.CostEstimate(
            flops=int(micros * 1e8), bytes_accessed=int(micros * 3e6), transcendentals=0
        ),
    )(*arrays)


def swapped(x, axis, partner, cross):
    size, cores = lax.axis_size(axis), lax.axis_size("pol")
    pairs = []
    for i in range(size):
        for p in range(cores):
            j, q = partner(i), cores - 1 - p
            if 0 <= j < size:
                pairs.append((i * cores + p, j * cores + (q if cross else p)))
            else:
                pairs.append((i * cores + p, i * cores + q))
    return lax.ppermute(x, (axis, "pol"), pairs)


def summed(x, axis, cross=True):
    size = lax.axis_size(axis)
    if size & (size - 1):
        return lax.psum(x, axis)
    distance = 1
    while distance < size:
        x = x + swapped(x, axis, lambda i, d=distance: i ^ d, cross)
        distance *= 2
    return x


def over_cores(x):
    cores = lax.axis_size("pol")
    return x + lax.ppermute(x, "pol", [(p, cores - 1 - p) for p in range(cores)])


def evenly(i):
    return i ^ 1


def oddly(i):
    return ((i + 1) ^ 1) - 1


def neighbours(even_out, odd_out, cross):
    odd_in = swapped(odd_out, "tm", oddly, cross)
    even_in = swapped(even_out, "tm", evenly, cross)
    return even_in, odd_in


def aslant(x, partner):
    size, cores = lax.axis_size("tm"), lax.axis_size("pol")
    pairs = []
    for i in range(size):
        for b in range(2):
            for p in range(cores):
                here = (i * 2 + b) * cores
                j = partner(i)
                if 0 <= j < size:
                    pairs.append((here + p, (j * 2 + 1 - b) * cores + p))
                else:
                    pairs.append((here + p, here + cores - 1 - p))
    return lax.ppermute(x, ("tm", "band", "pol"), pairs)


def over_tm(x):
    if lax.axis_size("tm") != 4:
        return summed(x, "tm")
    others = [swapped(x, "tm", lambda i, d=d: i ^ d, True) for d in (1, 2, 3)]
    return (x + others[0]) + (others[1] + others[2])


def exchanged(part, doubled):
    part = over_cores(part)
    part = part if doubled else summed(part, "band")
    return (part,) + neighbours(part, part, True)


def on_device(signal, cotangent, taps, gains, walk_off, tap_shift):
    own, _, _, length = signal.shape
    steps = taps.shape[0]
    rows = length // LANES
    held_rows = rows + 2 * PAD
    doubled = lax.axis_size("band") == 2
    groups = 2 if doubled else 1
    bands = groups * own

    def shape(*dims, dtype=F32):
        return jax.ShapeDtypeStruct(dims, dtype)

    field = shape(bands, 2, held_rows, LANES)
    own_field = shape(own, 2, held_rows, LANES)
    angle = shape(own, held_rows, LANES)
    wide_part = shape(rows + REACH + 2 * PAD, LANES)
    part = shape(rows + REACH, LANES)
    table = shape(own, 2 * LANES, 2 * LANES, dtype=BF16)
    ext_wide = (own, 2, rows + 2 * WIDE_PAD, LANES)
    held_wide = (own, rows + 2 * WIDE_PAD + 8, LANES)
    spread = (rows + REACH + 2 * PAD, LANES)
    moved = (bands, 2, held_rows, LANES)
    held_in = (bands, rows + REACH + 3 * PAD, LANES)
    held_own = (own, rows + REACH + 3 * PAD, LANES)
    held_out = (bands, rows + 3 * REACH, LANES)

    inputs = (signal, cotangent, taps, walk_off, tap_shift, gains)
    hbm, vmem = (pl.BlockSpec(memory_space=m) for m in (pltpu.HBM, pltpu.VMEM))
    cut = shape(own, 2, (WIDE + EDGE) * LANES)
    near = shape(own, 2, 2 * EDGE * LANES)
    pack_rows = 2 * own * rows + 2 * steps * own + 3 * steps
    pack = shape(pack_rows + -pack_rows % 8, LANES)
    even_out, odd_out, even_near, odd_near, pack_out, cot_out = pl.pallas_call(
        k_begin,
        out_shape=[cut, cut, near, near, pack, shape(own, 2, rows, LANES)],
        in_specs=[hbm] * len(inputs),
        out_specs=[vmem] * 6,
        scratch_shapes=[pltpu.VMEM(a.shape, a.dtype) for a in inputs]
        + [pltpu.SemaphoreType.DMA((len(inputs),))],
        compiler_params=pltpu.CompilerParams(vmem_limit_bytes=24 * 1024 * 1024),
        cost_estimate=pl.CostEstimate(flops=10**8, bytes_accessed=10**6, transcendentals=0),
    )(*(pltpu.with_memory_space_constraint(a, pltpu.HBM) for a in inputs))

    packs = [pack_out]
    sides = [neighbours(even_out, odd_out, False)]
    if doubled:
        packs.append(swapped(pack_out, "band", evenly, False))
        sides.append((aslant(even_near, evenly), aslant(odd_near, oddly)))
    tiny = [shape(steps, own, dtype=d) for d in (jnp.int32, jnp.int32, F32)]
    setup = functools.partial(k_setup, steps, rows)
    made = [call(setup, (p,), tiny + [table] * (2 * steps)) for p in packs]
    delays, shifts, gains, high0, low0, high1, low1 = (list(m) for m in zip(*made))

    shifted0, linear, sent = call(
        k_first, (delays[:1], shifts[:1], pack_out, sides[0], high0[0], low0[0]),
        [own_field, own_field, wide_part], (ext_wide, held_wide),
    )
    sent, sides = lax.optimization_barrier((sent, sides))
    sent = over_cores(sent)
    cots, first_cot = [cot_out], [WIDE]
    if doubled:
        delays[1], cot_sent = lax.optimization_barrier((delays[1], cot_out))
        cots.append(swapped(cot_sent, "band", evenly, False))
        first_cot.append(EDGE)
    spread0 = summed(sent, "band")
    linear0 = [linear]
    if doubled:
        linear0 += call(
            k_beside, (shifts[1:], packs[1], sides[1], high0[1], low0[1]), [own_field],
            ((own, 2, held_rows, LANES),),
        )
    (cot_rows,) = call(
        lambda c, s, out: k_cotangent(c, s, first_cot, out), (cots, sides), [field]
    )
    cosine0, sine0, field1, shifted1, linear1, sent = call(
        k_second, (delays, shifts, gains, linear0, spread0, high1, low1),
        [angle, angle, field, own_field, field, part], (moved, held_in, held_out),
    )
    turned1, sent = call(
        k_third, (delays, gains, linear1, *exchanged(sent, doubled), cot_rows),
        [field, part], (spread, held_in, held_out),
    )
    grad1, turned0, sent = call(
        k_fourth,
        (delays, shifts, gains, turned1, linear1, *exchanged(sent, doubled), high1, low1,
         cosine0, sine0, field1),
        [own_field, own_field, part], (spread, moved, held_in, held_out),
    )
    (taps1,) = call(k_taps, (shifted1, grad1), [shape(2 * own, LANES)])
    scale = 1.0 / math.sqrt(2.0 * length * lax.axis_size("tm"))
    grad0, grad_taps = call(
        functools.partial(k_fifth, scale),
        (delays[:1], turned0, linear, *exchanged(sent, doubled), shifted0, taps1),
        [own_field, shape(steps * 2 * own, LANES)], (spread, held_own),
    )
    (grad_signal,) = call(
        k_last, (shifts[:1], grad0, high0[0], low0[0]), [shape(own, 1, 2, length)]
    )
    grad_taps = over_tm(over_cores(grad_taps))
    return grad_signal, grad_taps.reshape(steps, own, 2, LANES)


def solution(mesh):
    return jax.shard_map(
        on_device,
        mesh=mesh,
        in_specs=(
            P(("groups", "band"), "pol", None, "tm"),
            P(("groups", "band"), "pol", None, "tm"),
            P(None, "band", None, None),
            P(None, "band"),
            P(None, "band"),
            P(None, "band"),
        ),
        out_specs=(P(("groups", "band"), "pol", None, "tm"), P("groups", "band", None, None)),
        check_vma=False,
    )
```

```python
import functools
import math

import jax
import jax.numpy as jnp
from jax import lax
from jax.experimental import pallas as pl
from jax.experimental.pallas import tpu as pltpu
from jax.sharding import PartitionSpec as P

LANES = 128
REACH = 2048 // LANES
EDGE = 4
WIDE = REACH + 4
PAD = 8
WIDE_PAD = REACH + PAD
F32 = jnp.float32
BF16 = jnp.bfloat16

TWO_OVER_PI = 2.0 / math.pi
HALF_PI_1 = 1.5625
HALF_PI_2 = 67.0 / 8192.0
HALF_PI_3 = 123.0 / 1048576.0
HALF_PI_4 = math.pi / 2.0 - HALF_PI_1 - HALF_PI_2 - HALF_PI_3


def split(x):
    high = x.astype(BF16)
    return high, (x - high.astype(F32)).astype(BF16)


def sine_cosine(x):
    turns = jnp.floor(x * TWO_OVER_PI + 0.5)
    quadrant = turns.astype(jnp.int32)
    r = x - turns * HALF_PI_1
    r = r - turns * HALF_PI_2
    r = r - turns * HALF_PI_3
    r = r - turns * HALF_PI_4
    r2 = r * r
    s = r + r * r2 * (-1.6666654611e-1 + r2 * (8.3321608736e-3 + r2 * -1.9515295891e-4))
    c = 1.0 - 0.5 * r2 + r2 * r2 * (
        4.166664568298827e-2 + r2 * (-1.388731625493765e-3 + r2 * 2.443315711809948e-5)
    )
    odd = (quadrant & 1) == 1
    sine = jnp.where(odd, c, s)
    cosine = jnp.where(odd, s, c)
    sine = jnp.where((quadrant & 2) == 2, -sine, sine)
    cosine = jnp.where(((quadrant + 1) & 2) == 2, -cosine, cosine)
    return sine, cosine


def lanes_of(shape):
    return lax.broadcasted_iota(jnp.int32, shape, len(shape) - 1)


def later(x, amount):
    rolled = pltpu.roll(x, amount & (LANES - 1), 1)
    return jnp.where(lanes_of(x.shape) >= amount, rolled, pltpu.roll(rolled, 1, 0))


def earlier(x, amount):
    rows = x.shape[0]
    rolled = pltpu.roll(x, (LANES - amount) & (LANES - 1), 1)
    follow = pltpu.roll(rolled, rows - 1, 0)
    return jnp.where(lanes_of(x.shape) + amount < LANES, rolled, follow)


def at(table, step, b):
    own = table[0].shape[1]
    return table[b // own][step, b % own]


def of(groups, b):
    own = groups[0].shape[0]
    return groups[b // own].at[b % own]


def is_even():
    return lax.rem(lax.axis_index("tm"), 2) == 0


def keep_inside(values, rows, pad=PAD):
    z = lax.axis_index("tm")
    row = lax.broadcasted_iota(jnp.int32, values.shape, 0)
    low = jnp.where(z == 0, pad, 0)
    high = jnp.where(z == lax.axis_size("tm") - 1, pad + rows, 2 * pad + rows)
    return jnp.where((row >= low) & (row < high), values, 0.0)


def from_sides(even_value, odd_value):
    z = lax.axis_index("tm")
    even = is_even()
    before = jnp.where(even, odd_value, even_value)
    after = jnp.where(even, even_value, odd_value)
    before = jnp.where(z == 0, 0.0, before)
    after = jnp.where(z == lax.axis_size("tm") - 1, 0.0, after)
    return before, after


def extend(out, b, even_in, odd_in, first, edge):
    own = even_in.shape[0]
    rows = out.shape[2]
    pad = edge + 4
    for c in range(2):
        out[b, c, 0:8, :] = jnp.zeros((8, LANES), F32)
        out[b, c, rows - 8 :, :] = jnp.zeros((8, LANES), F32)
    for r in range(edge):
        lanes = slice((first + r) * LANES, (first + r + 1) * LANES)
        before, after = from_sides(even_in[b % own, :, lanes], odd_in[b % own, :, lanes])
        for c in range(2):
            above = pad - edge + r
            below = rows - pad + r
            out[b, c, above : above + 1, :] = before[c : c + 1]
            out[b, c, below : below + 1, :] = after[c : c + 1]


def three_passes(x, high, low, transposed):
    rows = x.shape[0]
    xh, xl = split(x)
    contract = (((1,), (1 if transposed else 0,)), ((), ()))
    both = lax.dot_general(jnp.concatenate([xh, xl], 0), high, contract, preferred_element_type=F32)
    rest = lax.dot_general(xh, low, contract, preferred_element_type=F32)
    return both[:rows] + both[rows:] + rest


def fir(real, imag, high, low):
    rows = real.shape[0]
    x = [jnp.concatenate([part, pltpu.roll(part, rows - 1, 0)], 1) for part in (real, imag)]
    y = three_passes(jnp.concatenate(x, 0), high, low, True)
    first, second = y[:rows], y[rows:]
    return first[:, :LANES] - second[:, LANES:], first[:, LANES:] + second[:, :LANES]


def fir_adjoint(real, imag, high, low):
    rows = real.shape[0]
    x = [jnp.concatenate([real, imag], 1), jnp.concatenate([imag, -real], 1)]
    g = three_passes(jnp.concatenate(x, 0), high, low, False)
    parts = (g[:rows], g[rows:])
    return [part[:, :LANES] + pltpu.roll(part[:, LANES:], 1, 0) for part in parts]


def scatter_delayed(values, delays, step, held, out):
    bands = held.shape[0]
    base = REACH + 8
    total = out.shape[0]
    rows = total - REACH
    lane = lanes_of((total, LANES))
    parts = []
    for b, value in enumerate(values):
        delay = at(delays, step, b)
        parts.append((lax.shift_right_logical(delay, 7), delay & (LANES - 1)))
        held[b, 0:base, :] = jnp.zeros((base, LANES), F32)
        held[b, base : base + rows, :] = pltpu.roll(value, parts[b][1], 1)
        held[b, base + rows :, :] = jnp.zeros((held.shape[1] - base - rows, LANES), F32)
    acc = None
    for b, (q, s) in enumerate(parts):
        near = held[b, pl.ds(base - q, total), :]
        far = held[b, pl.ds(base - q - 1, total), :]
        part = jnp.where(lane >= s, near, far)
        acc = part if acc is None else acc + part
    out[...] = acc


def delayed_sum(values, delays, step, held, out):
    bands = len(values)
    count, total = values[0].shape[0], out.shape[0]
    lane = lanes_of((total, LANES))
    acc = None
    for b in range(bands):
        delay = at(delays, step, b)
        q = lax.shift_right_logical(delay, 7)
        s = delay & (LANES - 1)
        held[b, 0:8, :] = jnp.zeros((8, LANES), F32)
        held[b, 8 : 8 + count, :] = pltpu.roll(values[b], s, 1)
        near = held[b, pl.ds(8 + REACH - q, total), :]
        far = held[b, pl.ds(8 + REACH - q - 1, total), :]
        part = jnp.where(lane >= s, near, far)
        acc = part if acc is None else acc + part
    out[...] = acc


def end_at_last(values, rows):
    row = lax.broadcasted_iota(jnp.int32, values.shape, 0)
    last = lax.axis_index("tm") == lax.axis_size("tm") - 1
    return jnp.where(row < jnp.where(last, PAD + rows, values.shape[0]), values, 0.0)


def gather_spread(own, even_in, odd_in, spread, rows):
    before, after = from_sides(even_in[...], odd_in[...])
    total = rows + REACH + 2 * PAD
    spread[0:PAD, :] = before[rows - PAD : rows]
    spread[PAD:total - PAD, :] = own[...]
    spread[total - PAD : total, :] = after[REACH : REACH + PAD]
    spread[PAD : PAD + REACH, :] += before[rows : rows + REACH]
    spread[PAD + rows : PAD + rows + REACH, :] += after[0:REACH]
    return end_at_last(spread[...], rows)


def read_spread(values, delays, step, held, rows):
    bands, total = held.shape[0], values.shape[0]
    count = rows + 2 * PAD
    lane = lanes_of((count, LANES))
    parts = []
    for b in range(bands):
        delay = at(delays, step, b)
        parts.append((lax.shift_right_logical(delay, 7), delay & (LANES - 1)))
    for b, (_, s) in enumerate(parts):
        held[b, 0:total, :] = pltpu.roll(values, (LANES - s) & (LANES - 1), 1)
        held[b, total:, :] = jnp.zeros((held.shape[1] - total, LANES), F32)
    for b, (q, s) in enumerate(parts):
        near = held[b, pl.ds(q, count), :]
        far = held[b, pl.ds(q + 1, count), :]
        yield jnp.where(lane + s < LANES, near, far)


def k_begin(
    signal, cotangent, taps, delays, shifts, gains,
    even_out, odd_out, even_near, odd_near, sent,
    sig_held, cot_held, taps_held, delays_held, shifts_held, gains_held, done,
):
    steps, bands = taps.shape[:2]
    rows = signal.shape[3] // LANES
    pairs = (
        (signal, sig_held), (cotangent, cot_held), (taps, taps_held),
        (delays, delays_held), (shifts, shifts_held), (gains, gains_held),
    )
    copies = [pltpu.make_async_copy(a, b, done.at[n]) for n, (a, b) in enumerate(pairs)]
    for copy in copies:
        copy.start()
    for copy in copies:
        copy.wait()
    even = is_even()
    length, wide, edge = rows * LANES, WIDE * LANES, EDGE * LANES
    for b in range(bands):
        for targets, held, first, width in (
            ((even_out, odd_out), sig_held, 0, wide),
            ((even_out, odd_out), cot_held, wide, edge),
            ((even_near, odd_near), sig_held, 0, edge),
            ((even_near, odd_near), cot_held, edge, edge),
        ):
            left = held[b, 0, :, 0:width]
            right = held[b, 0, :, length - width : length]
            targets[0][b, :, first : first + width] = jnp.where(even, right, left)
            targets[1][b, :, first : first + width] = jnp.where(even, left, right)
        for r in range(rows):
            lanes = slice(r * LANES, (r + 1) * LANES)
            pair = sig_held[b, 0, :, lanes]
            other = cot_held[b, 0, :, lanes]
            for c in range(2):
                row = (2 * b + c) * rows + r
                sent[row : row + 1, :] = pair[c : c + 1]
                row = row + sent.shape[0] - 2 * bands * rows
                sent[row : row + 1, :] = other[c : c + 1]
    first = 2 * bands * rows
    for step in range(steps):
        for b in range(bands):
            row = first + 2 * (step * bands + b)
            sent[row : row + 2, :] = taps_held[step, b]
    first = first + 2 * steps * bands
    small = sent.shape[0] - 2 * bands * rows - first
    sent[first : first + small, :] = jnp.zeros((small, LANES), F32)
    for k, held in enumerate((delays_held, shifts_held, gains_held)):
        row = first + k * steps
        sent[row : row + steps, 0:bands] = held[...].astype(F32)


def k_setup(steps, rows, pack, delays, shifts, gains, *tables):
    bands = delays.shape[1]
    shape = (LANES, LANES)
    diagonal = lanes_of(shape) >= lax.broadcasted_iota(jnp.int32, shape, 0)
    base = 2 * bands * rows
    first = base + 2 * steps * bands
    for n, target in enumerate((delays, shifts, gains)):
        row = first + n * steps
        target[...] = pack[row : row + steps, 0:bands].astype(target.dtype)
    for b in range(bands):
        for step in range(steps):
            high, low = tables[2 * step : 2 * step + 2]
            for c in range(2):
                tap = base + 2 * (step * bands + b) + c
                row = jnp.broadcast_to(pack[tap : tap + 1, :], shape)
                ring = pltpu.roll(row, 0, 1, stride=1, stride_axis=0)
                near = jnp.where(diagonal, ring, 0.0)
                rows_of = slice(c * LANES, (c + 1) * LANES)
                for place, half in enumerate((near, ring - near)):
                    lanes = slice(place * LANES, (place + 1) * LANES)
                    high[b, rows_of, lanes], low[b, rows_of, lanes] = split(half)


def k_cotangent(packs, sides, first, out):
    own = sides[0][0].shape[0]
    rows = out.shape[2] - 2 * PAD
    base = packs[0].shape[0] - 2 * own * rows
    for b in range(out.shape[0]):
        k = b // own
        extend(out, b, *sides[k], first[k], EDGE)
        for c in range(2):
            row = base + (2 * (b % own) + c) * rows
            out[b, c, PAD : PAD + rows, :] = packs[k][row : row + rows, :]


def widened(ext, pack, sides, edge, b):
    pad = edge + 4
    rows = ext.shape[2] - 2 * pad
    extend(ext, b, *sides, 0, edge)
    for c in range(2):
        row = (2 * b + c) * rows
        ext[b, c, pad : pad + rows, :] = pack[row : row + rows, :]


def k_first(delays, shifts, pack, sides, high, low, shifted, linear, out, ext, held):
    bands = linear.shape[0]
    rows = linear.shape[2] - 2 * PAD
    middle = slice(WIDE_PAD - PAD, WIDE_PAD + rows + PAD)
    powers = []
    for b in range(bands):
        widened(ext, pack, sides, WIDE, b)
        amount = LANES // 2 - at(shifts, 0, b)
        real = later(ext[b, 0], amount)
        imag = later(ext[b, 1], amount)
        shifted[b, 0] = real[middle]
        shifted[b, 1] = imag[middle]
        lr, li = fir(real, imag, high[b], low[b])
        linear[b, 0] = lr[middle]
        linear[b, 1] = li[middle]
        powers.append(keep_inside(lr * lr + li * li, rows, WIDE_PAD))
    delayed_sum(powers, delays, 0, held, out)


def k_beside(shifts, pack, sides, high, low, linear, ext):
    for b in range(linear.shape[0]):
        widened(ext, pack, sides, EDGE, b)
        amount = LANES // 2 - at(shifts, 0, b)
        real = later(ext[b, 0], amount)
        imag = later(ext[b, 1], amount)
        lr, li = fir(real, imag, high[b], low[b])
        linear[b, 0] = lr
        linear[b, 1] = li


def k_second(
    delays, shifts, gains, linear0, own, high, low,
    cosine0, sine0, field1, shifted, linear1, out, moved, held, held_out,
):
    bands = linear1.shape[0]
    rows = linear1.shape[2] - 2 * PAD
    values = end_at_last(own[...], rows)
    for b, spread in enumerate(read_spread(values, delays, 0, held, rows)):
        sine, cosine = sine_cosine(at(gains, 0, b) * spread)
        linear = of(linear0, b)
        lr, li = linear[0], linear[1]
        fr = keep_inside(lr * cosine - li * sine, rows)
        fi = keep_inside(lr * sine + li * cosine, rows)
        field1[b, 0] = fr
        field1[b, 1] = fi
        amount = LANES // 2 - at(shifts, 1, b)
        real = later(fr, amount)
        imag = later(fi, amount)
        moved[b, 0] = real
        moved[b, 1] = imag
        if b < shifted.shape[0]:
            cosine0[b] = cosine
            sine0[b] = sine
            shifted[b, 0] = real
            shifted[b, 1] = imag
    for b in range(bands):
        lr, li = fir(moved[b, 0], moved[b, 1], of(high, b)[...], of(low, b)[...])
        linear1[b, 0] = lr
        linear1[b, 1] = li
    inside = slice(PAD, PAD + rows)
    powers = (linear1[b, 0, inside] ** 2 + linear1[b, 1, inside] ** 2 for b in range(bands))
    scatter_delayed(powers, delays, 1, held_out, out)


def k_third(
    delays, gains, linear1, own, even_in, odd_in, cotangent, turned1, out, spread, held, held_out
):
    bands = linear1.shape[0]
    rows = linear1.shape[2] - 2 * PAD
    values = gather_spread(own, even_in, odd_in, spread, rows)
    terms = []
    for b, spread_b in enumerate(read_spread(values, delays, 1, held, rows)):
        gain = at(gains, 1, b)
        sine, cosine = sine_cosine(gain * spread_b)
        gr, gi = cotangent[b, 0], cotangent[b, 1]
        er = gr * cosine + gi * sine
        ei = gi * cosine - gr * sine
        turned1[b, 0] = er
        turned1[b, 1] = ei
        term = ei * linear1[b, 0] - er * linear1[b, 1]
        terms.append(gain * term[PAD : PAD + rows])
    scatter_delayed(terms, delays, 1, held_out, out)


def k_fourth(
    delays, shifts, gains, turned1, linear1, own, even_in, odd_in, high, low, cosine0, sine0, field1,
    grad1, turned0, out, spread, moved, held, held_out,
):
    bands = linear1.shape[0]
    rows = linear1.shape[2] - 2 * PAD
    values = gather_spread(own, even_in, odd_in, spread, rows)
    for b, spread_b in enumerate(read_spread(values, delays, 1, held, rows)):
        twice = 2.0 * spread_b
        gr = keep_inside(turned1[b, 0] + linear1[b, 0] * twice, rows)
        gi = keep_inside(turned1[b, 1] + linear1[b, 1] * twice, rows)
        moved[b, 0] = gr
        moved[b, 1] = gi
        if b < grad1.shape[0]:
            grad1[b, 0] = gr
            grad1[b, 1] = gi
    for b in range(bands):
        gr, gi = fir_adjoint(moved[b, 0], moved[b, 1], of(high, b)[...], of(low, b)[...])
        moved[b, 0] = gr
        moved[b, 1] = gi
    terms = []
    for b in range(bands):
        amount = LANES // 2 - at(shifts, 1, b)
        gr = earlier(moved[b, 0], amount)
        gi = earlier(moved[b, 1], amount)
        if b < grad1.shape[0]:
            cosine, sine = cosine0[b], sine0[b]
            turned0[b, 0] = gr * cosine + gi * sine
            turned0[b, 1] = gi * cosine - gr * sine
        term = gi * field1[b, 0] - gr * field1[b, 1]
        terms.append(at(gains, 0, b) * term[PAD : PAD + rows])
    scatter_delayed(terms, delays, 0, held_out, out)


def correlate(real, imag, grad_real, grad_imag, rows):
    inside = slice(PAD, PAD + rows)
    following = slice(PAD + 1, PAD + rows + 1)
    a = jnp.concatenate(
        [
            jnp.concatenate([real[inside], real[following]], 1),
            jnp.concatenate([imag[inside], imag[following]], 1),
        ],
        0,
    )
    gr, gi = grad_real[inside], grad_imag[inside]
    d = jnp.concatenate([jnp.concatenate([gr, gi], 1), jnp.concatenate([gi, -gr], 1)], 0)
    ah, al = split(a)
    dh, dl = split(d)
    table = lax.dot_general(
        jnp.concatenate([dh, dh, dl], 0),
        jnp.concatenate([ah, al, ah], 0),
        (((0,), (0,)), ((), ())),
        preferred_element_type=F32,
    )
    width = 2 * LANES
    results = []
    for c in range(2):
        acc = table[c * LANES : c * LANES + 8]
        for g in range(1, LANES // 8):
            first = c * LANES + 8 * g
            acc = acc + pltpu.roll(table[first : first + 8], width - 8 * g, 1)
        total = acc[0:1]
        for s in range(1, 8):
            total = total + pltpu.roll(acc, width - s, 1)[s : s + 1]
        results.append(total[:, :LANES])
    return results


def k_taps(shifted, grad, out):
    bands = grad.shape[0]
    rows = grad.shape[2] - 2 * PAD
    for b in range(bands):
        parts = correlate(shifted[b, 0], shifted[b, 1], grad[b, 0], grad[b, 1], rows)
        for c in range(2):
            out[2 * b + c : 2 * b + c + 1, :] = parts[c]


def k_fifth(
    scale, delays, turned0, linear0, own, even_in, odd_in, shifted, taps1,
    grad0, out, spread, held,
):
    bands = turned0.shape[0]
    rows = turned0.shape[2] - 2 * PAD
    values = gather_spread(own, even_in, odd_in, spread, rows)
    for b, spread_b in enumerate(read_spread(values, delays, 0, held, rows)):
        twice = 2.0 * spread_b
        gr = keep_inside(turned0[b, 0] + linear0[b, 0] * twice, rows)
        gi = keep_inside(turned0[b, 1] + linear0[b, 1] * twice, rows)
        grad0[b, 0] = gr
        grad0[b, 1] = gi
        parts = correlate(shifted[b, 0], shifted[b, 1], gr, gi, rows)
        for c in range(2):
            out[2 * b + c : 2 * b + c + 1, :] = parts[c] * scale
    out[2 * bands :, :] = taps1[...] * scale


def k_last(shifts, grad0, high, low, result):
    bands = grad0.shape[0]
    rows = grad0.shape[2] - 2 * PAD
    for b in range(bands):
        gr, gi = fir_adjoint(grad0[b, 0], grad0[b, 1], high[b], low[b])
        amount = LANES // 2 - at(shifts, 0, b)
        gr = earlier(gr, amount)[PAD : PAD + rows]
        gi = earlier(gi, amount)[PAD : PAD + rows]
        for r in range(rows):
            result[b, 0, 0:1, r * LANES : (r + 1) * LANES] = gr[r : r + 1]
            result[b, 0, 1:2, r * LANES : (r + 1) * LANES] = gi[r : r + 1]


def call(kernel, arrays, shapes, scratch=(), micros=2.0):
    vmem = pl.BlockSpec(memory_space=pltpu.VMEM)
    return pl.pallas_call(
        kernel,
        out_shape=shapes,
        in_specs=jax.tree.map(lambda _: vmem, arrays),
        out_specs=[vmem] * len(shapes),
        scratch_shapes=[pltpu.VMEM(s, F32) for s in scratch],
        compiler_params=pltpu.CompilerParams(vmem_limit_bytes=24 * 1024 * 1024),
        cost_estimate=pl.CostEstimate(
            flops=int(micros * 1e8), bytes_accessed=int(micros * 3e6), transcendentals=0
        ),
    )(*arrays)


def swapped(x, axis, partner, cross):
    size, cores = lax.axis_size(axis), lax.axis_size("pol")
    pairs = []
    for i in range(size):
        for p in range(cores):
            j, q = partner(i), cores - 1 - p
            if 0 <= j < size:
                pairs.append((i * cores + p, j * cores + (q if cross else p)))
            else:
                pairs.append((i * cores + p, i * cores + q))
    return lax.ppermute(x, (axis, "pol"), pairs)


def summed(x, axis, cross=True):
    size = lax.axis_size(axis)
    if size & (size - 1):
        return lax.psum(x, axis)
    distance = 1
    while distance < size:
        x = x + swapped(x, axis, lambda i, d=distance: i ^ d, cross)
        distance *= 2
    return x


def over_cores(x):
    cores = lax.axis_size("pol")
    return x + lax.ppermute(x, "pol", [(p, cores - 1 - p) for p in range(cores)])


def evenly(i):
    return i ^ 1


def oddly(i):
    return ((i + 1) ^ 1) - 1


def neighbours(even_out, odd_out, cross):
    odd_in = swapped(odd_out, "tm", oddly, cross)
    even_in = swapped(even_out, "tm", evenly, cross)
    return even_in, odd_in


def aslant(x, partner):
    size, cores = lax.axis_size("tm"), lax.axis_size("pol")
    pairs = []
    for i in range(size):
        for b in range(2):
            for p in range(cores):
                here = (i * 2 + b) * cores
                j = partner(i)
                if 0 <= j < size:
                    pairs.append((here + p, (j * 2 + 1 - b) * cores + p))
                else:
                    pairs.append((here + p, here + cores - 1 - p))
    return lax.ppermute(x, ("tm", "band", "pol"), pairs)


def over_tm(x):
    if lax.axis_size("tm") != 4:
        return summed(x, "tm")
    others = [swapped(x, "tm", lambda i, d=d: i ^ d, True) for d in (1, 2, 3)]
    return (x + others[0]) + (others[1] + others[2])


def exchanged(part, doubled):
    part = over_cores(part)
    part = part if doubled else summed(part, "band")
    return (part,) + neighbours(part, part, True)


def on_device(signal, cotangent, taps, gains, walk_off, tap_shift):
    own, _, _, length = signal.shape
    steps = taps.shape[0]
    rows = length // LANES
    held_rows = rows + 2 * PAD
    doubled = lax.axis_size("band") == 2
    groups = 2 if doubled else 1
    bands = groups * own

    def shape(*dims, dtype=F32):
        return jax.ShapeDtypeStruct(dims, dtype)

    field = shape(bands, 2, held_rows, LANES)
    own_field = shape(own, 2, held_rows, LANES)
    angle = shape(own, held_rows, LANES)
    wide_part = shape(rows + REACH + 2 * PAD, LANES)
    part = shape(rows + REACH, LANES)
    table = shape(own, 2 * LANES, 2 * LANES, dtype=BF16)
    ext_wide = (own, 2, rows + 2 * WIDE_PAD, LANES)
    held_wide = (own, rows + 2 * WIDE_PAD + 8, LANES)
    spread = (rows + REACH + 2 * PAD, LANES)
    moved = (bands, 2, held_rows, LANES)
    held_in = (bands, rows + REACH + 3 * PAD, LANES)
    held_own = (own, rows + REACH + 3 * PAD, LANES)
    held_out = (bands, rows + 3 * REACH, LANES)

    inputs = (signal, cotangent, taps, walk_off, tap_shift, gains)
    hbm, vmem = (pl.BlockSpec(memory_space=m) for m in (pltpu.HBM, pltpu.VMEM))
    cut = shape(own, 2, (WIDE + EDGE) * LANES)
    near = shape(own, 2, 2 * EDGE * LANES)
    pack_rows = 2 * own * rows + 2 * steps * own + 3 * steps
    pack = shape(pack_rows + -pack_rows % 8 + 2 * own * rows, LANES)
    even_out, odd_out, even_near, odd_near, pack_out = pl.pallas_call(
        k_begin,
        out_shape=[cut, cut, near, near, pack],
        in_specs=[hbm] * len(inputs),
        out_specs=[vmem] * 5,
        scratch_shapes=[pltpu.VMEM(a.shape, a.dtype) for a in inputs]
        + [pltpu.SemaphoreType.DMA((len(inputs),))],
        compiler_params=pltpu.CompilerParams(vmem_limit_bytes=24 * 1024 * 1024),
        cost_estimate=pl.CostEstimate(flops=10**8, bytes_accessed=10**6, transcendentals=0),
    )(*(pltpu.with_memory_space_constraint(a, pltpu.HBM) for a in inputs))

    sides = [neighbours(even_out, odd_out, False)]
    if doubled:
        pack_in = swapped(pack_out, "band", evenly, False)
        sides.append((aslant(even_near, evenly), aslant(odd_near, oddly)))
    tiny = [shape(steps, own, dtype=d) for d in (jnp.int32, jnp.int32, F32)]
    setup = functools.partial(k_setup, steps, rows)
    made = [call(setup, (pack_out,), tiny + [table] * (2 * steps))]
    shifted0, linear, sent = call(
        k_first, (made[0][:1], made[0][1:2], pack_out, sides[0], *made[0][3:5]),
        [own_field, own_field, wide_part], (ext_wide, held_wide),
    )
    sent, sides = lax.optimization_barrier((sent, sides))
    sent = over_cores(sent)
    linear0, packs, first_cot = [linear], [pack_out], [WIDE]
    if doubled:
        sent, pack_in = lax.optimization_barrier((sent, pack_in))
        made.append(call(setup, (pack_in,), tiny + [table] * (2 * steps)))
        (other,) = call(
            k_beside, (made[1][1:2], pack_in, sides[1], *made[1][3:5]), [own_field],
            ((own, 2, held_rows, LANES),),
        )
        linear0.append(other)
        packs.append(pack_in)
        first_cot.append(EDGE)
    spread0 = summed(sent, "band")
    delays, shifts, gains, high0, low0, high1, low1 = (list(m) for m in zip(*made))
    (cot_rows,) = call(
        lambda c, s, out: k_cotangent(c, s, first_cot, out), (packs, sides), [field]
    )
    cosine0, sine0, field1, shifted1, linear1, sent = call(
        k_second, (delays, shifts, gains, linear0, spread0, high1, low1),
        [angle, angle, field, own_field, field, part], (moved, held_in, held_out),
    )
    turned1, sent = call(
        k_third, (delays, gains, linear1, *exchanged(sent, doubled), cot_rows),
        [field, part], (spread, held_in, held_out),
    )
    grad1, turned0, sent = call(
        k_fourth,
        (delays, shifts, gains, turned1, linear1, *exchanged(sent, doubled), high1, low1,
         cosine0, sine0, field1),
        [own_field, own_field, part], (spread, moved, held_in, held_out),
    )
    (taps1,) = call(k_taps, (shifted1, grad1), [shape(2 * own, LANES)])
    scale = 1.0 / math.sqrt(2.0 * length * lax.axis_size("tm"))
    grad0, grad_taps = call(
        functools.partial(k_fifth, scale),
        (delays[:1], turned0, linear, *exchanged(sent, doubled), shifted0, taps1),
        [own_field, shape(steps * 2 * own, LANES)], (spread, held_own),
    )
    (grad_signal,) = call(
        k_last, (shifts[:1], grad0, high0[0], low0[0]), [shape(own, 1, 2, length)]
    )
    grad_taps = over_tm(over_cores(grad_taps))
    return grad_signal, grad_taps.reshape(steps, own, 2, LANES)


def solution(mesh):
    return jax.shard_map(
        on_device,
        mesh=mesh,
        in_specs=(
            P(("groups", "band"), "pol", None, "tm"),
            P(("groups", "band"), "pol", None, "tm"),
            P(None, "band", None, None),
            P(None, "band"),
            P(None, "band"),
            P(None, "band"),
        ),
        out_specs=(P(("groups", "band"), "pol", None, "tm"), P("groups", "band", None, None)),
        check_vma=False,
    )
```

```python
import functools
import math

import jax
import jax.numpy as jnp
from jax import lax
from jax.experimental import pallas as pl
from jax.experimental.pallas import tpu as pltpu
from jax.sharding import PartitionSpec as P

LANES = 128
REACH = 2048 // LANES
EDGE = 4
WIDE = REACH + 4
PAD = 8
WIDE_PAD = REACH + PAD
F32 = jnp.float32
BF16 = jnp.bfloat16

TWO_OVER_PI = 2.0 / math.pi
HALF_PI_1 = 1.5625
HALF_PI_2 = 67.0 / 8192.0
HALF_PI_3 = 123.0 / 1048576.0
HALF_PI_4 = math.pi / 2.0 - HALF_PI_1 - HALF_PI_2 - HALF_PI_3


def split(x):
    high = x.astype(BF16)
    return high, (x - high.astype(F32)).astype(BF16)


def sine_cosine(x):
    turns = jnp.floor(x * TWO_OVER_PI + 0.5)
    quadrant = turns.astype(jnp.int32)
    r = x - turns * HALF_PI_1
    r = r - turns * HALF_PI_2
    r = r - turns * HALF_PI_3
    r = r - turns * HALF_PI_4
    r2 = r * r
    s = r + r * r2 * (-1.6666654611e-1 + r2 * (8.3321608736e-3 + r2 * -1.9515295891e-4))
    c = 1.0 - 0.5 * r2 + r2 * r2 * (
        4.166664568298827e-2 + r2 * (-1.388731625493765e-3 + r2 * 2.443315711809948e-5)
    )
    odd = (quadrant & 1) == 1
    sine = jnp.where(odd, c, s)
    cosine = jnp.where(odd, s, c)
    sine = jnp.where((quadrant & 2) == 2, -sine, sine)
    cosine = jnp.where(((quadrant + 1) & 2) == 2, -cosine, cosine)
    return sine, cosine


def lanes_of(shape):
    return lax.broadcasted_iota(jnp.int32, shape, len(shape) - 1)


def later(x, amount):
    rolled = pltpu.roll(x, amount & (LANES - 1), 1)
    return jnp.where(lanes_of(x.shape) >= amount, rolled, pltpu.roll(rolled, 1, 0))


def earlier(x, amount):
    rows = x.shape[0]
    rolled = pltpu.roll(x, (LANES - amount) & (LANES - 1), 1)
    follow = pltpu.roll(rolled, rows - 1, 0)
    return jnp.where(lanes_of(x.shape) + amount < LANES, rolled, follow)


def at(table, step, b):
    own = table[0].shape[1]
    return table[b // own][step, b % own]


def of(groups, b):
    own = groups[0].shape[0]
    return groups[b // own].at[b % own]


def is_even():
    return lax.rem(lax.axis_index("tm"), 2) == 0


def keep_inside(values, rows, pad=PAD):
    z = lax.axis_index("tm")
    row = lax.broadcasted_iota(jnp.int32, values.shape, 0)
    low = jnp.where(z == 0, pad, 0)
    high = jnp.where(z == lax.axis_size("tm") - 1, pad + rows, 2 * pad + rows)
    return jnp.where((row >= low) & (row < high), values, 0.0)


def from_sides(even_value, odd_value):
    z = lax.axis_index("tm")
    even = is_even()
    before = jnp.where(even, odd_value, even_value)
    after = jnp.where(even, even_value, odd_value)
    before = jnp.where(z == 0, 0.0, before)
    after = jnp.where(z == lax.axis_size("tm") - 1, 0.0, after)
    return before, after


def extend(out, b, even_in, odd_in, first, edge):
    own = even_in.shape[0]
    rows = out.shape[2]
    pad = edge + 4
    for c in range(2):
        out[b, c, 0:8, :] = jnp.zeros((8, LANES), F32)
        out[b, c, rows - 8 :, :] = jnp.zeros((8, LANES), F32)
    for r in range(edge):
        lanes = slice((first + r) * LANES, (first + r + 1) * LANES)
        before, after = from_sides(even_in[b % own, :, lanes], odd_in[b % own, :, lanes])
        for c in range(2):
            above = pad - edge + r
            below = rows - pad + r
            out[b, c, above : above + 1, :] = before[c : c + 1]
            out[b, c, below : below + 1, :] = after[c : c + 1]


def three_passes(x, high, low, transposed):
    rows = x.shape[0]
    xh, xl = split(x)
    contract = (((1,), (1 if transposed else 0,)), ((), ()))
    both = lax.dot_general(jnp.concatenate([xh, xl], 0), high, contract, preferred_element_type=F32)
    rest = lax.dot_general(xh, low, contract, preferred_element_type=F32)
    return both[:rows] + both[rows:] + rest


def fir(real, imag, high, low):
    rows = real.shape[0]
    x = [jnp.concatenate([part, pltpu.roll(part, rows - 1, 0)], 1) for part in (real, imag)]
    y = three_passes(jnp.concatenate(x, 0), high, low, True)
    first, second = y[:rows], y[rows:]
    return first[:, :LANES] - second[:, LANES:], first[:, LANES:] + second[:, :LANES]


def fir_adjoint(real, imag, high, low):
    rows = real.shape[0]
    x = [jnp.concatenate([real, imag], 1), jnp.concatenate([imag, -real], 1)]
    g = three_passes(jnp.concatenate(x, 0), high, low, False)
    parts = (g[:rows], g[rows:])
    return [part[:, :LANES] + pltpu.roll(part[:, LANES:], 1, 0) for part in parts]


def scatter_delayed(values, delays, step, held, out):
    bands = held.shape[0]
    base = REACH + 8
    total = out.shape[0]
    rows = total - REACH
    lane = lanes_of((total, LANES))
    parts = []
    for b, value in enumerate(values):
        delay = at(delays, step, b)
        parts.append((lax.shift_right_logical(delay, 7), delay & (LANES - 1)))
        held[b, 0:base, :] = jnp.zeros((base, LANES), F32)
        held[b, base : base + rows, :] = pltpu.roll(value, parts[b][1], 1)
        held[b, base + rows :, :] = jnp.zeros((held.shape[1] - base - rows, LANES), F32)
    acc = None
    for b, (q, s) in enumerate(parts):
        near = held[b, pl.ds(base - q, total), :]
        far = held[b, pl.ds(base - q - 1, total), :]
        part = jnp.where(lane >= s, near, far)
        acc = part if acc is None else acc + part
    out[...] = acc


def delayed_sum(values, delays, step, held, out):
    bands = len(values)
    count, total = values[0].shape[0], out.shape[0]
    lane = lanes_of((total, LANES))
    acc = None
    for b in range(bands):
        delay = at(delays, step, b)
        q = lax.shift_right_logical(delay, 7)
        s = delay & (LANES - 1)
        held[b, 0:8, :] = jnp.zeros((8, LANES), F32)
        held[b, 8 : 8 + count, :] = pltpu.roll(values[b], s, 1)
        near = held[b, pl.ds(8 + REACH - q, total), :]
        far = held[b, pl.ds(8 + REACH - q - 1, total), :]
        part = jnp.where(lane >= s, near, far)
        acc = part if acc is None else acc + part
    out[...] = acc


def end_at_last(values, rows):
    row = lax.broadcasted_iota(jnp.int32, values.shape, 0)
    last = lax.axis_index("tm") == lax.axis_size("tm") - 1
    return jnp.where(row < jnp.where(last, PAD + rows, values.shape[0]), values, 0.0)


def gather_spread(own, even_in, odd_in, spread, rows):
    before, after = from_sides(even_in[...], odd_in[...])
    total = rows + REACH + 2 * PAD
    spread[0:PAD, :] = before[rows - PAD : rows]
    spread[PAD:total - PAD, :] = own[...]
    spread[total - PAD : total, :] = after[REACH : REACH + PAD]
    spread[PAD : PAD + REACH, :] += before[rows : rows + REACH]
    spread[PAD + rows : PAD + rows + REACH, :] += after[0:REACH]
    return end_at_last(spread[...], rows)


def read_spread(values, delays, step, held, rows):
    bands, total = held.shape[0], values.shape[0]
    count = rows + 2 * PAD
    lane = lanes_of((count, LANES))
    parts = []
    for b in range(bands):
        delay = at(delays, step, b)
        parts.append((lax.shift_right_logical(delay, 7), delay & (LANES - 1)))
    for b, (_, s) in enumerate(parts):
        held[b, 0:total, :] = pltpu.roll(values, (LANES - s) & (LANES - 1), 1)
        held[b, total:, :] = jnp.zeros((held.shape[1] - total, LANES), F32)
    for b, (q, s) in enumerate(parts):
        near = held[b, pl.ds(q, count), :]
        far = held[b, pl.ds(q + 1, count), :]
        yield jnp.where(lane + s < LANES, near, far)


def k_begin(
    signal, cotangent, taps, delays, shifts, gains,
    even_out, odd_out, even_near, odd_near, sent, cot_rows,
    sig_held, cot_held, taps_held, delays_held, shifts_held, gains_held, done,
):
    steps, bands = taps.shape[:2]
    rows = cot_rows.shape[2]
    pairs = (
        (signal, sig_held), (cotangent, cot_held), (taps, taps_held),
        (delays, delays_held), (shifts, shifts_held), (gains, gains_held),
    )
    copies = [pltpu.make_async_copy(a, b, done.at[n]) for n, (a, b) in enumerate(pairs)]
    for copy in copies:
        copy.start()
    for copy in copies:
        copy.wait()
    even = is_even()
    length, wide, edge = rows * LANES, WIDE * LANES, EDGE * LANES
    for b in range(bands):
        for targets, held, first, width in (
            ((even_out, odd_out), sig_held, 0, wide),
            ((even_out, odd_out), cot_held, wide, edge),
            ((even_near, odd_near), sig_held, 0, edge),
            ((even_near, odd_near), cot_held, edge, edge),
        ):
            left = held[b, 0, :, 0:width]
            right = held[b, 0, :, length - width : length]
            targets[0][b, :, first : first + width] = jnp.where(even, right, left)
            targets[1][b, :, first : first + width] = jnp.where(even, left, right)
        for r in range(rows):
            lanes = slice(r * LANES, (r + 1) * LANES)
            pair = sig_held[b, 0, :, lanes]
            other = cot_held[b, 0, :, lanes]
            for c in range(2):
                row = (2 * b + c) * rows + r
                sent[row : row + 1, :] = pair[c : c + 1]
                cot_rows[b, c, r : r + 1, :] = other[c : c + 1]
    first = 2 * bands * rows
    for step in range(steps):
        for b in range(bands):
            row = first + 2 * (step * bands + b)
            sent[row : row + 2, :] = taps_held[step, b]
    first = first + 2 * steps * bands
    sent[first:, :] = jnp.zeros((sent.shape[0] - first, LANES), F32)
    for k, held in enumerate((delays_held, shifts_held, gains_held)):
        row = first + k * steps
        sent[row : row + steps, 0:bands] = held[...].astype(F32)


def k_setup(steps, rows, pack, delays, shifts, gains, *tables):
    bands = delays.shape[1]
    shape = (LANES, LANES)
    diagonal = lanes_of(shape) >= lax.broadcasted_iota(jnp.int32, shape, 0)
    base = 2 * bands * rows
    first = base + 2 * steps * bands
    for n, target in enumerate((delays, shifts, gains)):
        row = first + n * steps
        target[...] = pack[row : row + steps, 0:bands].astype(target.dtype)
    for b in range(bands):
        for step in range(steps):
            high, low = tables[2 * step : 2 * step + 2]
            for c in range(2):
                tap = base + 2 * (step * bands + b) + c
                row = jnp.broadcast_to(pack[tap : tap + 1, :], shape)
                ring = pltpu.roll(row, 0, 1, stride=1, stride_axis=0)
                near = jnp.where(diagonal, ring, 0.0)
                rows_of = slice(c * LANES, (c + 1) * LANES)
                for place, half in enumerate((near, ring - near)):
                    lanes = slice(place * LANES, (place + 1) * LANES)
                    high[b, rows_of, lanes], low[b, rows_of, lanes] = split(half)


def k_cotangent(cots, sides, first, out):
    own = cots[0].shape[0]
    rows = out.shape[2] - 2 * PAD
    for b in range(out.shape[0]):
        k = b // own
        extend(out, b, *sides[k], first[k], EDGE)
        for c in range(2):
            out[b, c, PAD : PAD + rows, :] = cots[k][b % own, c]


def widened(ext, pack, sides, edge, b):
    pad = edge + 4
    rows = ext.shape[2] - 2 * pad
    extend(ext, b, *sides, 0, edge)
    for c in range(2):
        row = (2 * b + c) * rows
        ext[b, c, pad : pad + rows, :] = pack[row : row + rows, :]


def k_first(delays, shifts, pack, sides, high, low, shifted, linear, out, ext, held):
    bands = linear.shape[0]
    rows = linear.shape[2] - 2 * PAD
    middle = slice(WIDE_PAD - PAD, WIDE_PAD + rows + PAD)
    powers = []
    for b in range(bands):
        widened(ext, pack, sides, WIDE, b)
        amount = LANES // 2 - at(shifts, 0, b)
        real = later(ext[b, 0], amount)
        imag = later(ext[b, 1], amount)
        shifted[b, 0] = real[middle]
        shifted[b, 1] = imag[middle]
        lr, li = fir(real, imag, high[b], low[b])
        linear[b, 0] = lr[middle]
        linear[b, 1] = li[middle]
        powers.append(keep_inside(lr * lr + li * li, rows, WIDE_PAD))
    delayed_sum(powers, delays, 0, held, out)


def k_beside(shifts, pack, sides, high, low, linear, ext):
    for b in range(linear.shape[0]):
        widened(ext, pack, sides, EDGE, b)
        amount = LANES // 2 - at(shifts, 0, b)
        real = later(ext[b, 0], amount)
        imag = later(ext[b, 1], amount)
        lr, li = fir(real, imag, high[b], low[b])
        linear[b, 0] = lr
        linear[b, 1] = li


def k_second(
    delays, shifts, gains, linear0, own, high, low,
    cosine0, sine0, field1, shifted, linear1, out, moved, held, held_out,
):
    bands = linear1.shape[0]
    rows = linear1.shape[2] - 2 * PAD
    values = end_at_last(own[...], rows)
    for b, spread in enumerate(read_spread(values, delays, 0, held, rows)):
        sine, cosine = sine_cosine(at(gains, 0, b) * spread)
        linear = of(linear0, b)
        lr, li = linear[0], linear[1]
        fr = keep_inside(lr * cosine - li * sine, rows)
        fi = keep_inside(lr * sine + li * cosine, rows)
        field1[b, 0] = fr
        field1[b, 1] = fi
        amount = LANES // 2 - at(shifts, 1, b)
        real = later(fr, amount)
        imag = later(fi, amount)
        moved[b, 0] = real
        moved[b, 1] = imag
        if b < shifted.shape[0]:
            cosine0[b] = cosine
            sine0[b] = sine
            shifted[b, 0] = real
            shifted[b, 1] = imag
    for b in range(bands):
        lr, li = fir(moved[b, 0], moved[b, 1], of(high, b)[...], of(low, b)[...])
        linear1[b, 0] = lr
        linear1[b, 1] = li
    inside = slice(PAD, PAD + rows)
    powers = (linear1[b, 0, inside] ** 2 + linear1[b, 1, inside] ** 2 for b in range(bands))
    scatter_delayed(powers, delays, 1, held_out, out)


def k_third(
    delays, gains, linear1, own, even_in, odd_in, cotangent, turned1, out, spread, held, held_out
):
    bands = linear1.shape[0]
    rows = linear1.shape[2] - 2 * PAD
    values = gather_spread(own, even_in, odd_in, spread, rows)
    terms = []
    for b, spread_b in enumerate(read_spread(values, delays, 1, held, rows)):
        gain = at(gains, 1, b)
        sine, cosine = sine_cosine(gain * spread_b)
        gr, gi = cotangent[b, 0], cotangent[b, 1]
        er = gr * cosine + gi * sine
        ei = gi * cosine - gr * sine
        turned1[b, 0] = er
        turned1[b, 1] = ei
        term = ei * linear1[b, 0] - er * linear1[b, 1]
        terms.append(gain * term[PAD : PAD + rows])
    scatter_delayed(terms, delays, 1, held_out, out)


def k_fourth(
    delays, shifts, gains, turned1, linear1, own, even_in, odd_in, high, low, cosine0, sine0, field1,
    grad1, turned0, out, spread, moved, held, held_out,
):
    bands = linear1.shape[0]
    rows = linear1.shape[2] - 2 * PAD
    values = gather_spread(own, even_in, odd_in, spread, rows)
    for b, spread_b in enumerate(read_spread(values, delays, 1, held, rows)):
        twice = 2.0 * spread_b
        gr = keep_inside(turned1[b, 0] + linear1[b, 0] * twice, rows)
        gi = keep_inside(turned1[b, 1] + linear1[b, 1] * twice, rows)
        moved[b, 0] = gr
        moved[b, 1] = gi
        if b < grad1.shape[0]:
            grad1[b, 0] = gr
            grad1[b, 1] = gi
    for b in range(bands):
        gr, gi = fir_adjoint(moved[b, 0], moved[b, 1], of(high, b)[...], of(low, b)[...])
        moved[b, 0] = gr
        moved[b, 1] = gi
    terms = []
    for b in range(bands):
        amount = LANES // 2 - at(shifts, 1, b)
        gr = earlier(moved[b, 0], amount)
        gi = earlier(moved[b, 1], amount)
        if b < grad1.shape[0]:
            cosine, sine = cosine0[b], sine0[b]
            turned0[b, 0] = gr * cosine + gi * sine
            turned0[b, 1] = gi * cosine - gr * sine
        term = gi * field1[b, 0] - gr * field1[b, 1]
        terms.append(at(gains, 0, b) * term[PAD : PAD + rows])
    scatter_delayed(terms, delays, 0, held_out, out)


def correlate(real, imag, grad_real, grad_imag, rows):
    inside = slice(PAD, PAD + rows)
    following = slice(PAD + 1, PAD + rows + 1)
    a = jnp.concatenate(
        [
            jnp.concatenate([real[inside], real[following]], 1),
            jnp.concatenate([imag[inside], imag[following]], 1),
        ],
        0,
    )
    gr, gi = grad_real[inside], grad_imag[inside]
    d = jnp.concatenate([jnp.concatenate([gr, gi], 1), jnp.concatenate([gi, -gr], 1)], 0)
    ah, al = split(a)
    dh, dl = split(d)
    table = lax.dot_general(
        jnp.concatenate([dh, dh, dl], 0),
        jnp.concatenate([ah, al, ah], 0),
        (((0,), (0,)), ((), ())),
        preferred_element_type=F32,
    )
    width = 2 * LANES
    results = []
    for c in range(2):
        acc = table[c * LANES : c * LANES + 8]
        for g in range(1, LANES // 8):
            first = c * LANES + 8 * g
            acc = acc + pltpu.roll(table[first : first + 8], width - 8 * g, 1)
        total = acc[0:1]
        for s in range(1, 8):
            total = total + pltpu.roll(acc, width - s, 1)[s : s + 1]
        results.append(total[:, :LANES])
    return results


def k_taps(shifted, grad, out):
    bands = grad.shape[0]
    rows = grad.shape[2] - 2 * PAD
    for b in range(bands):
        parts = correlate(shifted[b, 0], shifted[b, 1], grad[b, 0], grad[b, 1], rows)
        for c in range(2):
            out[2 * b + c : 2 * b + c + 1, :] = parts[c]


def k_fifth(
    scale, delays, turned0, linear0, own, even_in, odd_in, shifted, taps1,
    grad0, out, spread, held,
):
    bands = turned0.shape[0]
    rows = turned0.shape[2] - 2 * PAD
    values = gather_spread(own, even_in, odd_in, spread, rows)
    for b, spread_b in enumerate(read_spread(values, delays, 0, held, rows)):
        twice = 2.0 * spread_b
        gr = keep_inside(turned0[b, 0] + linear0[b, 0] * twice, rows)
        gi = keep_inside(turned0[b, 1] + linear0[b, 1] * twice, rows)
        grad0[b, 0] = gr
        grad0[b, 1] = gi
        parts = correlate(shifted[b, 0], shifted[b, 1], gr, gi, rows)
        for c in range(2):
            out[2 * b + c : 2 * b + c + 1, :] = parts[c] * scale
    out[2 * bands :, :] = taps1[...] * scale


def k_last(shifts, grad0, high, low, result):
    bands = grad0.shape[0]
    rows = grad0.shape[2] - 2 * PAD
    for b in range(bands):
        gr, gi = fir_adjoint(grad0[b, 0], grad0[b, 1], high[b], low[b])
        amount = LANES // 2 - at(shifts, 0, b)
        gr = earlier(gr, amount)[PAD : PAD + rows]
        gi = earlier(gi, amount)[PAD : PAD + rows]
        for r in range(rows):
            result[b, 0, 0:1, r * LANES : (r + 1) * LANES] = gr[r : r + 1]
            result[b, 0, 1:2, r * LANES : (r + 1) * LANES] = gi[r : r + 1]


def call(kernel, arrays, shapes, scratch=(), micros=2.0):
    vmem = pl.BlockSpec(memory_space=pltpu.VMEM)
    return pl.pallas_call(
        kernel,
        out_shape=shapes,
        in_specs=jax.tree.map(lambda _: vmem, arrays),
        out_specs=[vmem] * len(shapes),
        scratch_shapes=[pltpu.VMEM(s, F32) for s in scratch],
        compiler_params=pltpu.CompilerParams(vmem_limit_bytes=24 * 1024 * 1024),
        cost_estimate=pl.CostEstimate(
            flops=int(micros * 1e8), bytes_accessed=int(micros * 3e6), transcendentals=0
        ),
    )(*arrays)


def swapped(x, axis, partner, cross):
    size, cores = lax.axis_size(axis), lax.axis_size("pol")
    pairs = []
    for i in range(size):
        for p in range(cores):
            j, q = partner(i), cores - 1 - p
            if 0 <= j < size:
                pairs.append((i * cores + p, j * cores + (q if cross else p)))
            else:
                pairs.append((i * cores + p, i * cores + q))
    return lax.ppermute(x, (axis, "pol"), pairs)


def summed(x, axis, cross=True):
    size = lax.axis_size(axis)
    if size & (size - 1):
        return lax.psum(x, axis)
    distance = 1
    while distance < size:
        x = x + swapped(x, axis, lambda i, d=distance: i ^ d, cross)
        distance *= 2
    return x


def over_cores(x):
    cores = lax.axis_size("pol")
    return x + lax.ppermute(x, "pol", [(p, cores - 1 - p) for p in range(cores)])


def evenly(i):
    return i ^ 1


def oddly(i):
    return ((i + 1) ^ 1) - 1


def neighbours(even_out, odd_out, cross):
    odd_in = swapped(odd_out, "tm", oddly, cross)
    even_in = swapped(even_out, "tm", evenly, cross)
    return even_in, odd_in


def aslant(x, partner):
    size, cores = lax.axis_size("tm"), lax.axis_size("pol")
    pairs = []
    for i in range(size):
        for b in range(2):
            for p in range(cores):
                here = (i * 2 + b) * cores
                j = partner(i)
                if 0 <= j < size:
                    pairs.append((here + p, (j * 2 + 1 - b) * cores + p))
                else:
                    pairs.append((here + p, here + cores - 1 - p))
    return lax.ppermute(x, ("tm", "band", "pol"), pairs)


def over_tm(x):
    if lax.axis_size("tm") != 4:
        return summed(x, "tm")
    others = [swapped(x, "tm", lambda i, d=d: i ^ d, True) for d in (1, 2, 3)]
    return (x + others[0]) + (others[1] + others[2])


def exchanged(part, doubled):
    part = over_cores(part)
    part = part if doubled else summed(part, "band")
    return (part,) + neighbours(part, part, True)


def on_device(signal, cotangent, taps, gains, walk_off, tap_shift):
    own, _, _, length = signal.shape
    steps = taps.shape[0]
    rows = length // LANES
    held_rows = rows + 2 * PAD
    doubled = lax.axis_size("band") == 2
    groups = 2 if doubled else 1
    bands = groups * own

    def shape(*dims, dtype=F32):
        return jax.ShapeDtypeStruct(dims, dtype)

    field = shape(bands, 2, held_rows, LANES)
    own_field = shape(own, 2, held_rows, LANES)
    angle = shape(own, held_rows, LANES)
    wide_part = shape(rows + REACH + 2 * PAD, LANES)
    part = shape(rows + REACH, LANES)
    table = shape(own, 2 * LANES, 2 * LANES, dtype=BF16)
    ext_wide = (own, 2, rows + 2 * WIDE_PAD, LANES)
    held_wide = (own, rows + 2 * WIDE_PAD + 8, LANES)
    spread = (rows + REACH + 2 * PAD, LANES)
    moved = (bands, 2, held_rows, LANES)
    held_in = (bands, rows + REACH + 3 * PAD, LANES)
    held_own = (own, rows + REACH + 3 * PAD, LANES)
    held_out = (bands, rows + 3 * REACH, LANES)

    inputs = (signal, cotangent, taps, walk_off, tap_shift, gains)
    hbm, vmem = (pl.BlockSpec(memory_space=m) for m in (pltpu.HBM, pltpu.VMEM))
    cut = shape(own, 2, (WIDE + EDGE) * LANES)
    near = shape(own, 2, 2 * EDGE * LANES)
    pack_rows = 2 * own * rows + 2 * steps * own + 3 * steps
    pack = shape(pack_rows + -pack_rows % 8, LANES)
    even_out, odd_out, even_near, odd_near, pack_out, cot_out = pl.pallas_call(
        k_begin,
        out_shape=[cut, cut, near, near, pack, shape(own, 2, rows, LANES)],
        in_specs=[hbm] * len(inputs),
        out_specs=[vmem] * 6,
        scratch_shapes=[pltpu.VMEM(a.shape, a.dtype) for a in inputs]
        + [pltpu.SemaphoreType.DMA((len(inputs),))],
        compiler_params=pltpu.CompilerParams(vmem_limit_bytes=24 * 1024 * 1024),
        cost_estimate=pl.CostEstimate(flops=10**8, bytes_accessed=10**6, transcendentals=0),
    )(*(pltpu.with_memory_space_constraint(a, pltpu.HBM) for a in inputs))

    packs = [pack_out]
    sides = [neighbours(even_out, odd_out, False)]
    if doubled:
        packs.append(swapped(pack_out, "band", evenly, False))
        sides.append((aslant(even_near, evenly), aslant(odd_near, oddly)))
    tiny = [shape(steps, own, dtype=d) for d in (jnp.int32, jnp.int32, F32)]
    setup = functools.partial(k_setup, steps, rows)
    made = [call(setup, (p,), tiny + [table] * (2 * steps)) for p in packs]
    delays, shifts, gains, high0, low0, high1, low1 = (list(m) for m in zip(*made))

    shifted0, linear, sent = call(
        k_first, (delays[:1], shifts[:1], pack_out, sides[0], high0[0], low0[0]),
        [own_field, own_field, wide_part], (ext_wide, held_wide),
    )
    sent, sides = lax.optimization_barrier((sent, sides))
    sent = over_cores(sent)
    cots, first_cot = [cot_out], [WIDE]
    if doubled:
        cots.append(swapped(cot_out, "band", evenly, False))
        first_cot.append(EDGE)
    spread0 = summed(sent, "band")
    linear0 = [linear]
    if doubled:
        linear0 += call(
            k_beside, (shifts[1:], packs[1], sides[1], high0[1], low0[1]), [own_field],
            ((own, 2, held_rows, LANES),),
        )
    (cot_rows,) = call(
        lambda c, s, out: k_cotangent(c, s, first_cot, out), (cots, sides), [field]
    )
    cosine0, sine0, field1, shifted1, linear1, sent = call(
        k_second, (delays, shifts, gains, linear0, spread0, high1, low1),
        [angle, angle, field, own_field, field, part], (moved, held_in, held_out),
    )
    turned1, sent = call(
        k_third, (delays, gains, linear1, *exchanged(sent, doubled), cot_rows),
        [field, part], (spread, held_in, held_out),
    )
    grad1, turned0, sent = call(
        k_fourth,
        (delays, shifts, gains, turned1, linear1, *exchanged(sent, doubled), high1, low1,
         cosine0, sine0, field1),
        [own_field, own_field, part], (spread, moved, held_in, held_out),
    )
    (taps1,) = call(k_taps, (shifted1, grad1), [shape(2 * own, LANES)])
    scale = 1.0 / math.sqrt(2.0 * length * lax.axis_size("tm"))
    grad0, grad_taps = call(
        functools.partial(k_fifth, scale),
        (delays[:1], turned0, linear, *exchanged(sent, doubled), shifted0, taps1),
        [own_field, shape(steps * 2 * own, LANES)], (spread, held_own),
    )
    (grad_signal,) = call(
        k_last, (shifts[:1], grad0, high0[0], low0[0]), [shape(own, 1, 2, length)]
    )
    grad_taps = over_tm(over_cores(grad_taps))
    return grad_signal, grad_taps.reshape(steps, own, 2, LANES)


def solution(mesh):
    return jax.shard_map(
        on_device,
        mesh=mesh,
        in_specs=(
            P(("groups", "band"), "pol", None, "tm"),
            P(("groups", "band"), "pol", None, "tm"),
            P(None, "band", None, None),
            P(None, "band"),
            P(None, "band"),
            P(None, "band"),
        ),
        out_specs=(P(("groups", "band"), "pol", None, "tm"), P("groups", "band", None, None)),
        check_vma=False,
    )
```

```python
import functools
import math

import jax
import jax.numpy as jnp
from jax import lax
from jax.experimental import pallas as pl
from jax.experimental.pallas import tpu as pltpu
from jax.sharding import PartitionSpec as P

LANES = 128
REACH = 2048 // LANES
EDGE = 4
WIDE = REACH + 4
PAD = 8
WIDE_PAD = REACH + PAD
F32 = jnp.float32
BF16 = jnp.bfloat16

TWO_OVER_PI = 2.0 / math.pi
HALF_PI_1 = 1.5625
HALF_PI_2 = 67.0 / 8192.0
HALF_PI_3 = 123.0 / 1048576.0
HALF_PI_4 = math.pi / 2.0 - HALF_PI_1 - HALF_PI_2 - HALF_PI_3


def split(x):
    high = x.astype(BF16)
    return high, (x - high.astype(F32)).astype(BF16)


def sine_cosine(x):
    turns = jnp.floor(x * TWO_OVER_PI + 0.5)
    quadrant = turns.astype(jnp.int32)
    r = x - turns * HALF_PI_1
    r = r - turns * HALF_PI_2
    r = r - turns * HALF_PI_3
    r = r - turns * HALF_PI_4
    r2 = r * r
    s = r + r * r2 * (-1.6666654611e-1 + r2 * (8.3321608736e-3 + r2 * -1.9515295891e-4))
    c = 1.0 - 0.5 * r2 + r2 * r2 * (
        4.166664568298827e-2 + r2 * (-1.388731625493765e-3 + r2 * 2.443315711809948e-5)
    )
    odd = (quadrant & 1) == 1
    sine = jnp.where(odd, c, s)
    cosine = jnp.where(odd, s, c)
    sine = jnp.where((quadrant & 2) == 2, -sine, sine)
    cosine = jnp.where(((quadrant + 1) & 2) == 2, -cosine, cosine)
    return sine, cosine


def lanes_of(shape):
    return lax.broadcasted_iota(jnp.int32, shape, len(shape) - 1)


def later(x, amount):
    rolled = pltpu.roll(x, amount & (LANES - 1), 1)
    return jnp.where(lanes_of(x.shape) >= amount, rolled, pltpu.roll(rolled, 1, 0))


def earlier(x, amount):
    rows = x.shape[0]
    rolled = pltpu.roll(x, (LANES - amount) & (LANES - 1), 1)
    follow = pltpu.roll(rolled, rows - 1, 0)
    return jnp.where(lanes_of(x.shape) + amount < LANES, rolled, follow)


def at(table, step, b):
    own = table[0].shape[1]
    return table[b // own][step, b % own]


def of(groups, b):
    own = groups[0].shape[0]
    return groups[b // own].at[b % own]


def is_even():
    return lax.rem(lax.axis_index("tm"), 2) == 0


def keep_inside(values, rows, pad=PAD):
    z = lax.axis_index("tm")
    row = lax.broadcasted_iota(jnp.int32, values.shape, 0)
    low = jnp.where(z == 0, pad, 0)
    high = jnp.where(z == lax.axis_size("tm") - 1, pad + rows, 2 * pad + rows)
    return jnp.where((row >= low) & (row < high), values, 0.0)


def from_sides(even_value, odd_value):
    z = lax.axis_index("tm")
    even = is_even()
    before = jnp.where(even, odd_value, even_value)
    after = jnp.where(even, even_value, odd_value)
    before = jnp.where(z == 0, 0.0, before)
    after = jnp.where(z == lax.axis_size("tm") - 1, 0.0, after)
    return before, after


def extend(out, b, even_in, odd_in, first, edge):
    own = even_in.shape[0]
    rows = out.shape[2]
    pad = edge + 4
    for c in range(2):
        out[b, c, 0:8, :] = jnp.zeros((8, LANES), F32)
        out[b, c, rows - 8 :, :] = jnp.zeros((8, LANES), F32)
    for r in range(edge):
        lanes = slice((first + r) * LANES, (first + r + 1) * LANES)
        before, after = from_sides(even_in[b % own, :, lanes], odd_in[b % own, :, lanes])
        for c in range(2):
            above = pad - edge + r
            below = rows - pad + r
            out[b, c, above : above + 1, :] = before[c : c + 1]
            out[b, c, below : below + 1, :] = after[c : c + 1]


def three_passes(x, high, low, transposed):
    rows = x.shape[0]
    xh, xl = split(x)
    contract = (((1,), (1 if transposed else 0,)), ((), ()))
    both = lax.dot_general(jnp.concatenate([xh, xl], 0), high, contract, preferred_element_type=F32)
    rest = lax.dot_general(xh, low, contract, preferred_element_type=F32)
    return both[:rows] + both[rows:] + rest


def fir(real, imag, high, low):
    rows = real.shape[0]
    x = [jnp.concatenate([part, pltpu.roll(part, rows - 1, 0)], 1) for part in (real, imag)]
    y = three_passes(jnp.concatenate(x, 0), high, low, True)
    first, second = y[:rows], y[rows:]
    return first[:, :LANES] - second[:, LANES:], first[:, LANES:] + second[:, :LANES]


def fir_adjoint(real, imag, high, low):
    rows = real.shape[0]
    x = [jnp.concatenate([real, imag], 1), jnp.concatenate([imag, -real], 1)]
    g = three_passes(jnp.concatenate(x, 0), high, low, False)
    parts = (g[:rows], g[rows:])
    return [part[:, :LANES] + pltpu.roll(part[:, LANES:], 1, 0) for part in parts]


def scatter_delayed(values, delays, step, held, out):
    bands = held.shape[0]
    base = REACH + 8
    total = out.shape[0]
    rows = total - REACH
    lane = lanes_of((total, LANES))
    parts = []
    for b, value in enumerate(values):
        delay = at(delays, step, b)
        parts.append((lax.shift_right_logical(delay, 7), delay & (LANES - 1)))
        held[b, 0:base, :] = jnp.zeros((base, LANES), F32)
        held[b, base : base + rows, :] = pltpu.roll(value, parts[b][1], 1)
        held[b, base + rows :, :] = jnp.zeros((held.shape[1] - base - rows, LANES), F32)
    acc = None
    for b, (q, s) in enumerate(parts):
        near = held[b, pl.ds(base - q, total), :]
        far = held[b, pl.ds(base - q - 1, total), :]
        part = jnp.where(lane >= s, near, far)
        acc = part if acc is None else acc + part
    out[...] = acc


def delayed_sum(values, delays, step, held, out):
    bands = len(values)
    count, total = values[0].shape[0], out.shape[0]
    lane = lanes_of((total, LANES))
    acc = None
    for b in range(bands):
        delay = at(delays, step, b)
        q = lax.shift_right_logical(delay, 7)
        s = delay & (LANES - 1)
        held[b, 0:8, :] = jnp.zeros((8, LANES), F32)
        held[b, 8 : 8 + count, :] = pltpu.roll(values[b], s, 1)
        near = held[b, pl.ds(8 + REACH - q, total), :]
        far = held[b, pl.ds(8 + REACH - q - 1, total), :]
        part = jnp.where(lane >= s, near, far)
        acc = part if acc is None else acc + part
    out[...] = acc


def end_at_last(values, rows):
    row = lax.broadcasted_iota(jnp.int32, values.shape, 0)
    last = lax.axis_index("tm") == lax.axis_size("tm") - 1
    return jnp.where(row < jnp.where(last, PAD + rows, values.shape[0]), values, 0.0)


def gather_spread(own, even_in, odd_in, spread, rows):
    before, after = from_sides(even_in[...], odd_in[...])
    total = rows + REACH + 2 * PAD
    spread[0:PAD, :] = before[rows - PAD : rows]
    spread[PAD:total - PAD, :] = own[...]
    spread[total - PAD : total, :] = after[REACH : REACH + PAD]
    spread[PAD : PAD + REACH, :] += before[rows : rows + REACH]
    spread[PAD + rows : PAD + rows + REACH, :] += after[0:REACH]
    return end_at_last(spread[...], rows)


def read_spread(values, delays, step, held, rows):
    bands, total = held.shape[0], values.shape[0]
    count = rows + 2 * PAD
    lane = lanes_of((count, LANES))
    parts = []
    for b in range(bands):
        delay = at(delays, step, b)
        parts.append((lax.shift_right_logical(delay, 7), delay & (LANES - 1)))
    for b, (_, s) in enumerate(parts):
        held[b, 0:total, :] = pltpu.roll(values, (LANES - s) & (LANES - 1), 1)
        held[b, total:, :] = jnp.zeros((held.shape[1] - total, LANES), F32)
    for b, (q, s) in enumerate(parts):
        near = held[b, pl.ds(q, count), :]
        far = held[b, pl.ds(q + 1, count), :]
        yield jnp.where(lane + s < LANES, near, far)


def k_begin(
    signal, cotangent, taps, delays, shifts, gains,
    even_out, odd_out, even_near, odd_near, sent, cot_rows,
    sig_held, cot_held, taps_held, delays_held, shifts_held, gains_held, done,
):
    steps, bands = taps.shape[:2]
    rows = cot_rows.shape[2]
    pairs = (
        (signal, sig_held), (cotangent, cot_held), (taps, taps_held),
        (delays, delays_held), (shifts, shifts_held), (gains, gains_held),
    )
    copies = [pltpu.make_async_copy(a, b, done.at[n]) for n, (a, b) in enumerate(pairs)]
    for copy in copies:
        copy.start()
    for copy in copies:
        copy.wait()
    even = is_even()
    length, wide, edge = rows * LANES, WIDE * LANES, EDGE * LANES
    for b in range(bands):
        for targets, held, first, width in (
            ((even_out, odd_out), sig_held, 0, wide),
            ((even_out, odd_out), cot_held, wide, edge),
            ((even_near, odd_near), sig_held, 0, edge),
            ((even_near, odd_near), cot_held, edge, edge),
        ):
            left = held[b, 0, :, 0:width]
            right = held[b, 0, :, length - width : length]
            targets[0][b, :, first : first + width] = jnp.where(even, right, left)
            targets[1][b, :, first : first + width] = jnp.where(even, left, right)
        for r in range(rows):
            lanes = slice(r * LANES, (r + 1) * LANES)
            pair = sig_held[b, 0, :, lanes]
            other = cot_held[b, 0, :, lanes]
            for c in range(2):
                row = (2 * b + c) * rows + r
                sent[row : row + 1, :] = pair[c : c + 1]
                cot_rows[b, c, r : r + 1, :] = other[c : c + 1]
    first = 2 * bands * rows
    for step in range(steps):
        for b in range(bands):
            row = first + 2 * (step * bands + b)
            sent[row : row + 2, :] = taps_held[step, b]
    first = first + 2 * steps * bands
    sent[first:, :] = jnp.zeros((sent.shape[0] - first, LANES), F32)
    for k, held in enumerate((delays_held, shifts_held, gains_held)):
        row = first + k * steps
        sent[row : row + steps, 0:bands] = held[...].astype(F32)


def k_setup(steps, rows, pack, delays, shifts, gains, *tables):
    bands = delays.shape[1]
    shape = (LANES, LANES)
    diagonal = lanes_of(shape) >= lax.broadcasted_iota(jnp.int32, shape, 0)
    base = 2 * bands * rows
    first = base + 2 * steps * bands
    for n, target in enumerate((delays, shifts, gains)):
        row = first + n * steps
        target[...] = pack[row : row + steps, 0:bands].astype(target.dtype)
    for b in range(bands):
        for step in range(steps):
            high, low = tables[2 * step : 2 * step + 2]
            for c in range(2):
                tap = base + 2 * (step * bands + b) + c
                row = jnp.broadcast_to(pack[tap : tap + 1, :], shape)
                ring = pltpu.roll(row, 0, 1, stride=1, stride_axis=0)
                near = jnp.where(diagonal, ring, 0.0)
                rows_of = slice(c * LANES, (c + 1) * LANES)
                for place, half in enumerate((near, ring - near)):
                    lanes = slice(place * LANES, (place + 1) * LANES)
                    high[b, rows_of, lanes], low[b, rows_of, lanes] = split(half)


def k_cotangent(cots, sides, first, out):
    own = cots[0].shape[0]
    rows = out.shape[2] - 2 * PAD
    for b in range(out.shape[0]):
        k = b // own
        extend(out, b, *sides[k], first[k], EDGE)
        for c in range(2):
            out[b, c, PAD : PAD + rows, :] = cots[k][b % own, c]


def widened(ext, pack, sides, edge, b):
    pad = edge + 4
    rows = ext.shape[2] - 2 * pad
    extend(ext, b, *sides, 0, edge)
    for c in range(2):
        row = (2 * b + c) * rows
        ext[b, c, pad : pad + rows, :] = pack[row : row + rows, :]


def k_first(delays, shifts, pack, sides, high, low, shifted, linear, out, ext, held):
    bands = linear.shape[0]
    rows = linear.shape[2] - 2 * PAD
    middle = slice(WIDE_PAD - PAD, WIDE_PAD + rows + PAD)
    powers = []
    for b in range(bands):
        widened(ext, pack, sides, WIDE, b)
        amount = LANES // 2 - at(shifts, 0, b)
        real = later(ext[b, 0], amount)
        imag = later(ext[b, 1], amount)
        shifted[b, 0] = real[middle]
        shifted[b, 1] = imag[middle]
        lr, li = fir(real, imag, high[b], low[b])
        linear[b, 0] = lr[middle]
        linear[b, 1] = li[middle]
        powers.append(keep_inside(lr * lr + li * li, rows, WIDE_PAD))
    delayed_sum(powers, delays, 0, held, out)


def k_beside(shifts, pack, sides, high, low, linear, ext):
    for b in range(linear.shape[0]):
        widened(ext, pack, sides, EDGE, b)
        amount = LANES // 2 - at(shifts, 0, b)
        real = later(ext[b, 0], amount)
        imag = later(ext[b, 1], amount)
        lr, li = fir(real, imag, high[b], low[b])
        linear[b, 0] = lr
        linear[b, 1] = li


def k_second(
    delays, shifts, gains, linear0, own, high, low,
    cosine0, sine0, field1, shifted, linear1, out, moved, held, held_out,
):
    bands = linear1.shape[0]
    rows = linear1.shape[2] - 2 * PAD
    values = end_at_last(own[...], rows)
    for b, spread in enumerate(read_spread(values, delays, 0, held, rows)):
        sine, cosine = sine_cosine(at(gains, 0, b) * spread)
        linear = of(linear0, b)
        lr, li = linear[0], linear[1]
        fr = keep_inside(lr * cosine - li * sine, rows)
        fi = keep_inside(lr * sine + li * cosine, rows)
        field1[b, 0] = fr
        field1[b, 1] = fi
        amount = LANES // 2 - at(shifts, 1, b)
        real = later(fr, amount)
        imag = later(fi, amount)
        moved[b, 0] = real
        moved[b, 1] = imag
        if b < shifted.shape[0]:
            cosine0[b] = cosine
            sine0[b] = sine
            shifted[b, 0] = real
            shifted[b, 1] = imag
    for b in range(bands):
        lr, li = fir(moved[b, 0], moved[b, 1], of(high, b)[...], of(low, b)[...])
        linear1[b, 0] = lr
        linear1[b, 1] = li
    inside = slice(PAD, PAD + rows)
    powers = (linear1[b, 0, inside] ** 2 + linear1[b, 1, inside] ** 2 for b in range(bands))
    scatter_delayed(powers, delays, 1, held_out, out)


def k_third(
    delays, gains, linear1, own, odd_in, even_in, cotangent, turned1, out, spread, held, held_out
):
    bands = linear1.shape[0]
    rows = linear1.shape[2] - 2 * PAD
    values = gather_spread(own, even_in, odd_in, spread, rows)
    terms = []
    for b, spread_b in enumerate(read_spread(values, delays, 1, held, rows)):
        gain = at(gains, 1, b)
        sine, cosine = sine_cosine(gain * spread_b)
        gr, gi = cotangent[b, 0], cotangent[b, 1]
        er = gr * cosine + gi * sine
        ei = gi * cosine - gr * sine
        turned1[b, 0] = er
        turned1[b, 1] = ei
        term = ei * linear1[b, 0] - er * linear1[b, 1]
        terms.append(gain * term[PAD : PAD + rows])
    scatter_delayed(terms, delays, 1, held_out, out)


def k_fourth(
    delays, shifts, gains, turned1, linear1, own, odd_in, even_in, high, low, cosine0, sine0, field1,
    grad1, turned0, out, spread, moved, held, held_out,
):
    bands = linear1.shape[0]
    rows = linear1.shape[2] - 2 * PAD
    values = gather_spread(own, even_in, odd_in, spread, rows)
    for b, spread_b in enumerate(read_spread(values, delays, 1, held, rows)):
        twice = 2.0 * spread_b
        gr = keep_inside(turned1[b, 0] + linear1[b, 0] * twice, rows)
        gi = keep_inside(turned1[b, 1] + linear1[b, 1] * twice, rows)
        moved[b, 0] = gr
        moved[b, 1] = gi
        if b < grad1.shape[0]:
            grad1[b, 0] = gr
            grad1[b, 1] = gi
    for b in range(bands):
        gr, gi = fir_adjoint(moved[b, 0], moved[b, 1], of(high, b)[...], of(low, b)[...])
        moved[b, 0] = gr
        moved[b, 1] = gi
    terms = []
    for b in range(bands):
        amount = LANES // 2 - at(shifts, 1, b)
        gr = earlier(moved[b, 0], amount)
        gi = earlier(moved[b, 1], amount)
        if b < grad1.shape[0]:
            cosine, sine = cosine0[b], sine0[b]
            turned0[b, 0] = gr * cosine + gi * sine
            turned0[b, 1] = gi * cosine - gr * sine
        term = gi * field1[b, 0] - gr * field1[b, 1]
        terms.append(at(gains, 0, b) * term[PAD : PAD + rows])
    scatter_delayed(terms, delays, 0, held_out, out)


def correlate(real, imag, grad_real, grad_imag, rows):
    inside = slice(PAD, PAD + rows)
    following = slice(PAD + 1, PAD + rows + 1)
    a = jnp.concatenate(
        [
            jnp.concatenate([real[inside], real[following]], 1),
            jnp.concatenate([imag[inside], imag[following]], 1),
        ],
        0,
    )
    gr, gi = grad_real[inside], grad_imag[inside]
    d = jnp.concatenate([jnp.concatenate([gr, gi], 1), jnp.concatenate([gi, -gr], 1)], 0)
    ah, al = split(a)
    dh, dl = split(d)
    table = lax.dot_general(
        jnp.concatenate([dh, dh, dl], 0),
        jnp.concatenate([ah, al, ah], 0),
        (((0,), (0,)), ((), ())),
        preferred_element_type=F32,
    )
    width = 2 * LANES
    results = []
    for c in range(2):
        acc = table[c * LANES : c * LANES + 8]
        for g in range(1, LANES // 8):
            first = c * LANES + 8 * g
            acc = acc + pltpu.roll(table[first : first + 8], width - 8 * g, 1)
        total = acc[0:1]
        for s in range(1, 8):
            total = total + pltpu.roll(acc, width - s, 1)[s : s + 1]
        results.append(total[:, :LANES])
    return results


def k_taps(shifted, grad, out):
    bands = grad.shape[0]
    rows = grad.shape[2] - 2 * PAD
    for b in range(bands):
        parts = correlate(shifted[b, 0], shifted[b, 1], grad[b, 0], grad[b, 1], rows)
        for c in range(2):
            out[2 * b + c : 2 * b + c + 1, :] = parts[c]


def k_fifth(
    scale, delays, turned0, linear0, own, odd_in, even_in, shifted, taps1,
    grad0, out, spread, held,
):
    bands = turned0.shape[0]
    rows = turned0.shape[2] - 2 * PAD
    values = gather_spread(own, even_in, odd_in, spread, rows)
    for b, spread_b in enumerate(read_spread(values, delays, 0, held, rows)):
        twice = 2.0 * spread_b
        gr = keep_inside(turned0[b, 0] + linear0[b, 0] * twice, rows)
        gi = keep_inside(turned0[b, 1] + linear0[b, 1] * twice, rows)
        grad0[b, 0] = gr
        grad0[b, 1] = gi
        parts = correlate(shifted[b, 0], shifted[b, 1], gr, gi, rows)
        for c in range(2):
            out[2 * b + c : 2 * b + c + 1, :] = parts[c] * scale
    out[2 * bands :, :] = taps1[...] * scale


def k_last(shifts, grad0, high, low, result):
    bands = grad0.shape[0]
    rows = grad0.shape[2] - 2 * PAD
    for b in range(bands):
        gr, gi = fir_adjoint(grad0[b, 0], grad0[b, 1], high[b], low[b])
        amount = LANES // 2 - at(shifts, 0, b)
        gr = earlier(gr, amount)[PAD : PAD + rows]
        gi = earlier(gi, amount)[PAD : PAD + rows]
        for r in range(rows):
            result[b, 0, 0:1, r * LANES : (r + 1) * LANES] = gr[r : r + 1]
            result[b, 0, 1:2, r * LANES : (r + 1) * LANES] = gi[r : r + 1]


def call(kernel, arrays, shapes, scratch=(), micros=2.0):
    vmem = pl.BlockSpec(memory_space=pltpu.VMEM)
    return pl.pallas_call(
        kernel,
        out_shape=shapes,
        in_specs=jax.tree.map(lambda _: vmem, arrays),
        out_specs=[vmem] * len(shapes),
        scratch_shapes=[pltpu.VMEM(s, F32) for s in scratch],
        compiler_params=pltpu.CompilerParams(vmem_limit_bytes=24 * 1024 * 1024),
        cost_estimate=pl.CostEstimate(
            flops=int(micros * 1e8), bytes_accessed=int(micros * 3e6), transcendentals=0
        ),
    )(*arrays)


def swapped(x, axis, partner, cross):
    size, cores = lax.axis_size(axis), lax.axis_size("pol")
    pairs = []
    for i in range(size):
        for p in range(cores):
            j, q = partner(i), cores - 1 - p
            if 0 <= j < size:
                pairs.append((i * cores + p, j * cores + (q if cross else p)))
            else:
                pairs.append((i * cores + p, i * cores + q))
    return lax.ppermute(x, (axis, "pol"), pairs)


def summed(x, axis, cross=True):
    size = lax.axis_size(axis)
    if size & (size - 1):
        return lax.psum(x, axis)
    distance = 1
    while distance < size:
        x = x + swapped(x, axis, lambda i, d=distance: i ^ d, cross)
        distance *= 2
    return x


def over_cores(x):
    cores = lax.axis_size("pol")
    return x + lax.ppermute(x, "pol", [(p, cores - 1 - p) for p in range(cores)])


def evenly(i):
    return i ^ 1


def oddly(i):
    return ((i + 1) ^ 1) - 1


def neighbours(even_out, odd_out, cross):
    odd_in = swapped(odd_out, "tm", oddly, cross)
    even_in = swapped(even_out, "tm", evenly, cross)
    return even_in, odd_in


def aslant(x, partner):
    size, cores = lax.axis_size("tm"), lax.axis_size("pol")
    pairs = []
    for i in range(size):
        for b in range(2):
            for p in range(cores):
                here = (i * 2 + b) * cores
                j = partner(i)
                if 0 <= j < size:
                    pairs.append((here + p, (j * 2 + 1 - b) * cores + p))
                else:
                    pairs.append((here + p, here + cores - 1 - p))
    return lax.ppermute(x, ("tm", "band", "pol"), pairs)


def over_tm(x):
    if lax.axis_size("tm") != 4:
        return summed(x, "tm")
    others = [swapped(x, "tm", lambda i, d=d: i ^ d, True) for d in (1, 2, 3)]
    return (x + others[0]) + (others[1] + others[2])


def exchanged(part, doubled):
    part = over_cores(part)
    part = part if doubled else summed(part, "band")
    return (part,) + neighbours(part, part, True)[::-1]


def on_device(signal, cotangent, taps, gains, walk_off, tap_shift):
    own, _, _, length = signal.shape
    steps = taps.shape[0]
    rows = length // LANES
    held_rows = rows + 2 * PAD
    doubled = lax.axis_size("band") == 2
    groups = 2 if doubled else 1
    bands = groups * own

    def shape(*dims, dtype=F32):
        return jax.ShapeDtypeStruct(dims, dtype)

    field = shape(bands, 2, held_rows, LANES)
    own_field = shape(own, 2, held_rows, LANES)
    angle = shape(own, held_rows, LANES)
    wide_part = shape(rows + REACH + 2 * PAD, LANES)
    part = shape(rows + REACH, LANES)
    table = shape(own, 2 * LANES, 2 * LANES, dtype=BF16)
    ext_wide = (own, 2, rows + 2 * WIDE_PAD, LANES)
    held_wide = (own, rows + 2 * WIDE_PAD + 8, LANES)
    spread = (rows + REACH + 2 * PAD, LANES)
    moved = (bands, 2, held_rows, LANES)
    held_in = (bands, rows + REACH + 3 * PAD, LANES)
    held_own = (own, rows + REACH + 3 * PAD, LANES)
    held_out = (bands, rows + 3 * REACH, LANES)

    inputs = (signal, cotangent, taps, walk_off, tap_shift, gains)
    hbm, vmem = (pl.BlockSpec(memory_space=m) for m in (pltpu.HBM, pltpu.VMEM))
    cut = shape(own, 2, (WIDE + EDGE) * LANES)
    near = shape(own, 2, 2 * EDGE * LANES)
    pack_rows = 2 * own * rows + 2 * steps * own + 3 * steps
    pack = shape(pack_rows + -pack_rows % 8, LANES)
    even_out, odd_out, even_near, odd_near, pack_out, cot_out = pl.pallas_call(
        k_begin,
        out_shape=[cut, cut, near, near, pack, shape(own, 2, rows, LANES)],
        in_specs=[hbm] * len(inputs),
        out_specs=[vmem] * 6,
        scratch_shapes=[pltpu.VMEM(a.shape, a.dtype) for a in inputs]
        + [pltpu.SemaphoreType.DMA((len(inputs),))],
        compiler_params=pltpu.CompilerParams(vmem_limit_bytes=24 * 1024 * 1024),
        cost_estimate=pl.CostEstimate(flops=10**8, bytes_accessed=10**6, transcendentals=0),
    )(*(pltpu.with_memory_space_constraint(a, pltpu.HBM) for a in inputs))

    packs = [pack_out]
    sides = [neighbours(even_out, odd_out, False)]
    if doubled:
        packs.append(swapped(pack_out, "band", evenly, False))
        sides.append((aslant(even_near, evenly), aslant(odd_near, oddly)))
    tiny = [shape(steps, own, dtype=d) for d in (jnp.int32, jnp.int32, F32)]
    setup = functools.partial(k_setup, steps, rows)
    made = [call(setup, (p,), tiny + [table] * (2 * steps)) for p in packs]
    delays, shifts, gains, high0, low0, high1, low1 = (list(m) for m in zip(*made))

    shifted0, linear, sent = call(
        k_first, (delays[:1], shifts[:1], pack_out, sides[0], high0[0], low0[0]),
        [own_field, own_field, wide_part], (ext_wide, held_wide),
    )
    sent, sides = lax.optimization_barrier((sent, sides))
    sent = over_cores(sent)
    cots, first_cot = [cot_out], [WIDE]
    if doubled:
        cots.append(swapped(cot_out, "band", evenly, False))
        first_cot.append(EDGE)
    spread0 = summed(sent, "band")
    linear0 = [linear]
    if doubled:
        linear0 += call(
            k_beside, (shifts[1:], packs[1], sides[1], high0[1], low0[1]), [own_field],
            ((own, 2, held_rows, LANES),),
        )
    (cot_rows,) = call(
        lambda c, s, out: k_cotangent(c, s, first_cot, out), (cots, sides), [field]
    )
    cosine0, sine0, field1, shifted1, linear1, sent = call(
        k_second, (delays, shifts, gains, linear0, spread0, high1, low1),
        [angle, angle, field, own_field, field, part], (moved, held_in, held_out),
    )
    turned1, sent = call(
        k_third, (delays, gains, linear1, *exchanged(sent, doubled), cot_rows),
        [field, part], (spread, held_in, held_out),
    )
    grad1, turned0, sent = call(
        k_fourth,
        (delays, shifts, gains, turned1, linear1, *exchanged(sent, doubled), high1, low1,
         cosine0, sine0, field1),
        [own_field, own_field, part], (spread, moved, held_in, held_out),
    )
    (taps1,) = call(k_taps, (shifted1, grad1), [shape(2 * own, LANES)])
    scale = 1.0 / math.sqrt(2.0 * length * lax.axis_size("tm"))
    grad0, grad_taps = call(
        functools.partial(k_fifth, scale),
        (delays[:1], turned0, linear, *exchanged(sent, doubled), shifted0, taps1),
        [own_field, shape(steps * 2 * own, LANES)], (spread, held_own),
    )
    (grad_signal,) = call(
        k_last, (shifts[:1], grad0, high0[0], low0[0]), [shape(own, 1, 2, length)]
    )
    grad_taps = over_tm(over_cores(grad_taps))
    return grad_signal, grad_taps.reshape(steps, own, 2, LANES)


def solution(mesh):
    return jax.shard_map(
        on_device,
        mesh=mesh,
        in_specs=(
            P(("groups", "band"), "pol", None, "tm"),
            P(("groups", "band"), "pol", None, "tm"),
            P(None, "band", None, None),
            P(None, "band"),
            P(None, "band"),
            P(None, "band"),
        ),
        out_specs=(P(("groups", "band"), "pol", None, "tm"), P("groups", "band", None, None)),
        check_vma=False,
    )
```

```python
import functools
import math

import jax
import jax.numpy as jnp
from jax import lax
from jax.experimental import pallas as pl
from jax.experimental.pallas import tpu as pltpu
from jax.sharding import PartitionSpec as P

LANES = 128
REACH = 2048 // LANES
EDGE = 4
WIDE = REACH + 4
PAD = 8
WIDE_PAD = REACH + PAD
F32 = jnp.float32
BF16 = jnp.bfloat16

TWO_OVER_PI = 2.0 / math.pi
HALF_PI_1 = 1.5625
HALF_PI_2 = 67.0 / 8192.0
HALF_PI_3 = 123.0 / 1048576.0
HALF_PI_4 = math.pi / 2.0 - HALF_PI_1 - HALF_PI_2 - HALF_PI_3


def split(x):
    high = x.astype(BF16)
    return high, (x - high.astype(F32)).astype(BF16)


def sine_cosine(x):
    turns = jnp.floor(x * TWO_OVER_PI + 0.5)
    quadrant = turns.astype(jnp.int32)
    r = x - turns * HALF_PI_1
    r = r - turns * HALF_PI_2
    r = r - turns * HALF_PI_3
    r = r - turns * HALF_PI_4
    r2 = r * r
    s = r + r * r2 * (-1.6666654611e-1 + r2 * (8.3321608736e-3 + r2 * -1.9515295891e-4))
    c = 1.0 - 0.5 * r2 + r2 * r2 * (
        4.166664568298827e-2 + r2 * (-1.388731625493765e-3 + r2 * 2.443315711809948e-5)
    )
    odd = (quadrant & 1) == 1
    sine = jnp.where(odd, c, s)
    cosine = jnp.where(odd, s, c)
    sine = jnp.where((quadrant & 2) == 2, -sine, sine)
    cosine = jnp.where(((quadrant + 1) & 2) == 2, -cosine, cosine)
    return sine, cosine


def lanes_of(shape):
    return lax.broadcasted_iota(jnp.int32, shape, len(shape) - 1)


def later(x, amount):
    rolled = pltpu.roll(x, amount & (LANES - 1), 1)
    return jnp.where(lanes_of(x.shape) >= amount, rolled, pltpu.roll(rolled, 1, 0))


def earlier(x, amount):
    rows = x.shape[0]
    rolled = pltpu.roll(x, (LANES - amount) & (LANES - 1), 1)
    follow = pltpu.roll(rolled, rows - 1, 0)
    return jnp.where(lanes_of(x.shape) + amount < LANES, rolled, follow)


def at(table, step, b):
    own = table[0].shape[1]
    return table[b // own][step, b % own]


def of(groups, b):
    own = groups[0].shape[0]
    return groups[b // own].at[b % own]


def is_even():
    return lax.rem(lax.axis_index("tm"), 2) == 0


def keep_inside(values, rows, pad=PAD):
    z = lax.axis_index("tm")
    row = lax.broadcasted_iota(jnp.int32, values.shape, 0)
    low = jnp.where(z == 0, pad, 0)
    high = jnp.where(z == lax.axis_size("tm") - 1, pad + rows, 2 * pad + rows)
    return jnp.where((row >= low) & (row < high), values, 0.0)


def from_sides(even_value, odd_value):
    z = lax.axis_index("tm")
    even = is_even()
    before = jnp.where(even, odd_value, even_value)
    after = jnp.where(even, even_value, odd_value)
    before = jnp.where(z == 0, 0.0, before)
    after = jnp.where(z == lax.axis_size("tm") - 1, 0.0, after)
    return before, after


def extend(out, b, even_in, odd_in, first, edge):
    own = even_in.shape[0]
    rows = out.shape[2]
    pad = edge + 4
    for c in range(2):
        out[b, c, 0:8, :] = jnp.zeros((8, LANES), F32)
        out[b, c, rows - 8 :, :] = jnp.zeros((8, LANES), F32)
    for r in range(edge):
        lanes = slice((first + r) * LANES, (first + r + 1) * LANES)
        before, after = from_sides(even_in[b % own, :, lanes], odd_in[b % own, :, lanes])
        for c in range(2):
            above = pad - edge + r
            below = rows - pad + r
            out[b, c, above : above + 1, :] = before[c : c + 1]
            out[b, c, below : below + 1, :] = after[c : c + 1]


def three_passes(x, high, low, transposed):
    rows = x.shape[0]
    xh, xl = split(x)
    contract = (((1,), (1 if transposed else 0,)), ((), ()))
    both = lax.dot_general(jnp.concatenate([xh, xl], 0), high, contract, preferred_element_type=F32)
    rest = lax.dot_general(xh, low, contract, preferred_element_type=F32)
    return both[:rows] + both[rows:] + rest


def fir(real, imag, high, low):
    rows = real.shape[0]
    x = [jnp.concatenate([part, pltpu.roll(part, rows - 1, 0)], 1) for part in (real, imag)]
    y = three_passes(jnp.concatenate(x, 0), high, low, True)
    first, second = y[:rows], y[rows:]
    return first[:, :LANES] - second[:, LANES:], first[:, LANES:] + second[:, :LANES]


def fir_adjoint(real, imag, high, low):
    rows = real.shape[0]
    x = [jnp.concatenate([real, imag], 1), jnp.concatenate([imag, -real], 1)]
    g = three_passes(jnp.concatenate(x, 0), high, low, False)
    parts = (g[:rows], g[rows:])
    return [part[:, :LANES] + pltpu.roll(part[:, LANES:], 1, 0) for part in parts]


def scatter_delayed(values, delays, step, held, out):
    bands = held.shape[0]
    base = REACH + 8
    total = out.shape[0]
    rows = total - REACH
    lane = lanes_of((total, LANES))
    parts = []
    for b, value in enumerate(values):
        delay = at(delays, step, b)
        parts.append((lax.shift_right_logical(delay, 7), delay & (LANES - 1)))
        held[b, 0:base, :] = jnp.zeros((base, LANES), F32)
        held[b, base : base + rows, :] = pltpu.roll(value, parts[b][1], 1)
        held[b, base + rows :, :] = jnp.zeros((held.shape[1] - base - rows, LANES), F32)
    acc = None
    for b, (q, s) in enumerate(parts):
        near = held[b, pl.ds(base - q, total), :]
        far = held[b, pl.ds(base - q - 1, total), :]
        part = jnp.where(lane >= s, near, far)
        acc = part if acc is None else acc + part
    out[...] = acc


def delayed_sum(values, delays, step, held, out):
    bands = len(values)
    count, total = values[0].shape[0], out.shape[0]
    lane = lanes_of((total, LANES))
    acc = None
    for b in range(bands):
        delay = at(delays, step, b)
        q = lax.shift_right_logical(delay, 7)
        s = delay & (LANES - 1)
        held[b, 0:8, :] = jnp.zeros((8, LANES), F32)
        held[b, 8 : 8 + count, :] = pltpu.roll(values[b], s, 1)
        near = held[b, pl.ds(8 + REACH - q, total), :]
        far = held[b, pl.ds(8 + REACH - q - 1, total), :]
        part = jnp.where(lane >= s, near, far)
        acc = part if acc is None else acc + part
    out[...] = acc


def end_at_last(values, rows):
    row = lax.broadcasted_iota(jnp.int32, values.shape, 0)
    last = lax.axis_index("tm") == lax.axis_size("tm") - 1
    return jnp.where(row < jnp.where(last, PAD + rows, values.shape[0]), values, 0.0)


def gather_spread(own, even_in, odd_in, spread, rows):
    before, after = from_sides(even_in[...], odd_in[...])
    total = rows + REACH + 2 * PAD
    spread[0:PAD, :] = before[rows - PAD : rows]
    spread[PAD:total - PAD, :] = own[...]
    spread[total - PAD : total, :] = after[REACH : REACH + PAD]
    spread[PAD : PAD + REACH, :] += before[rows : rows + REACH]
    spread[PAD + rows : PAD + rows + REACH, :] += after[0:REACH]
    return end_at_last(spread[...], rows)


def read_spread(values, delays, step, held, rows):
    bands, total = held.shape[0], values.shape[0]
    count = rows + 2 * PAD
    lane = lanes_of((count, LANES))
    parts = []
    for b in range(bands):
        delay = at(delays, step, b)
        parts.append((lax.shift_right_logical(delay, 7), delay & (LANES - 1)))
    for b, (_, s) in enumerate(parts):
        held[b, 0:total, :] = pltpu.roll(values, (LANES - s) & (LANES - 1), 1)
        held[b, total:, :] = jnp.zeros((held.shape[1] - total, LANES), F32)
    for b, (q, s) in enumerate(parts):
        near = held[b, pl.ds(q, count), :]
        far = held[b, pl.ds(q + 1, count), :]
        yield jnp.where(lane + s < LANES, near, far)


def k_begin(
    signal, cotangent, taps, delays, shifts, gains,
    even_out, odd_out, even_near, odd_near, sent, cot_rows,
    sig_held, cot_held, taps_held, delays_held, shifts_held, gains_held, done,
):
    steps, bands = taps.shape[:2]
    rows = cot_rows.shape[2]
    pairs = (
        (signal, sig_held), (cotangent, cot_held), (taps, taps_held),
        (delays, delays_held), (shifts, shifts_held), (gains, gains_held),
    )
    copies = [pltpu.make_async_copy(a, b, done.at[n]) for n, (a, b) in enumerate(pairs)]
    for copy in copies:
        copy.start()
    for copy in copies:
        copy.wait()
    even = is_even()
    length, wide, edge = rows * LANES, WIDE * LANES, EDGE * LANES
    for b in range(bands):
        for targets, held, first, width in (
            ((even_out, odd_out), sig_held, 0, wide),
            ((even_out, odd_out), cot_held, wide, edge),
            ((even_near, odd_near), sig_held, 0, edge),
            ((even_near, odd_near), cot_held, edge, edge),
        ):
            left = held[b, 0, :, 0:width]
            right = held[b, 0, :, length - width : length]
            targets[0][b, :, first : first + width] = jnp.where(even, right, left)
            targets[1][b, :, first : first + width] = jnp.where(even, left, right)
        for r in range(rows):
            lanes = slice(r * LANES, (r + 1) * LANES)
            pair = sig_held[b, 0, :, lanes]
            other = cot_held[b, 0, :, lanes]
            for c in range(2):
                row = (2 * b + c) * rows + r
                sent[row : row + 1, :] = pair[c : c + 1]
                cot_rows[b, c, r : r + 1, :] = other[c : c + 1]
    first = 2 * bands * rows
    for step in range(steps):
        for b in range(bands):
            row = first + 2 * (step * bands + b)
            sent[row : row + 2, :] = taps_held[step, b]
    first = first + 2 * steps * bands
    sent[first:, :] = jnp.zeros((sent.shape[0] - first, LANES), F32)
    for k, held in enumerate((delays_held, shifts_held, gains_held)):
        row = first + k * steps
        sent[row : row + steps, 0:bands] = held[...].astype(F32)


def k_setup(steps, rows, pack, delays, shifts, gains, *tables):
    bands = delays.shape[1]
    shape = (LANES, LANES)
    diagonal = lanes_of(shape) >= lax.broadcasted_iota(jnp.int32, shape, 0)
    base = 2 * bands * rows
    first = base + 2 * steps * bands
    for n, target in enumerate((delays, shifts, gains)):
        row = first + n * steps
        target[...] = pack[row : row + steps, 0:bands].astype(target.dtype)
    for b in range(bands):
        for step in range(steps):
            high, low = tables[2 * step : 2 * step + 2]
            for c in range(2):
                tap = base + 2 * (step * bands + b) + c
                row = jnp.broadcast_to(pack[tap : tap + 1, :], shape)
                ring = pltpu.roll(row, 0, 1, stride=1, stride_axis=0)
                near = jnp.where(diagonal, ring, 0.0)
                rows_of = slice(c * LANES, (c + 1) * LANES)
                for place, half in enumerate((near, ring - near)):
                    lanes = slice(place * LANES, (place + 1) * LANES)
                    high[b, rows_of, lanes], low[b, rows_of, lanes] = split(half)


def k_cotangent(cots, sides, first, out):
    own = cots[0].shape[0]
    rows = out.shape[2] - 2 * PAD
    for b in range(out.shape[0]):
        k = b // own
        extend(out, b, *sides[k], first[k], EDGE)
        for c in range(2):
            out[b, c, PAD : PAD + rows, :] = cots[k][b % own, c]


def widened(ext, pack, sides, edge, b):
    pad = edge + 4
    rows = ext.shape[2] - 2 * pad
    extend(ext, b, *sides, 0, edge)
    for c in range(2):
        row = (2 * b + c) * rows
        ext[b, c, pad : pad + rows, :] = pack[row : row + rows, :]


def k_first(delays, shifts, pack, sides, high, low, shifted, linear, out, ext, held):
    bands = linear.shape[0]
    rows = linear.shape[2] - 2 * PAD
    middle = slice(WIDE_PAD - PAD, WIDE_PAD + rows + PAD)
    powers = []
    for b in range(bands):
        widened(ext, pack, sides, WIDE, b)
        amount = LANES // 2 - at(shifts, 0, b)
        real = later(ext[b, 0], amount)
        imag = later(ext[b, 1], amount)
        shifted[b, 0] = real[middle]
        shifted[b, 1] = imag[middle]
        lr, li = fir(real, imag, high[b], low[b])
        linear[b, 0] = lr[middle]
        linear[b, 1] = li[middle]
        powers.append(keep_inside(lr * lr + li * li, rows, WIDE_PAD))
    delayed_sum(powers, delays, 0, held, out)


def k_beside(shifts, pack, sides, high, low, linear, ext):
    for b in range(linear.shape[0]):
        widened(ext, pack, sides, EDGE, b)
        amount = LANES // 2 - at(shifts, 0, b)
        real = later(ext[b, 0], amount)
        imag = later(ext[b, 1], amount)
        lr, li = fir(real, imag, high[b], low[b])
        linear[b, 0] = lr
        linear[b, 1] = li


def k_second(
    delays, shifts, gains, linear0, own, high, low,
    cosine0, sine0, field1, shifted, linear1, out, moved, held, held_out,
):
    bands = linear1.shape[0]
    rows = linear1.shape[2] - 2 * PAD
    values = end_at_last(own[...], rows)
    for b, spread in enumerate(read_spread(values, delays, 0, held, rows)):
        sine, cosine = sine_cosine(at(gains, 0, b) * spread)
        linear = of(linear0, b)
        lr, li = linear[0], linear[1]
        fr = keep_inside(lr * cosine - li * sine, rows)
        fi = keep_inside(lr * sine + li * cosine, rows)
        field1[b, 0] = fr
        field1[b, 1] = fi
        amount = LANES // 2 - at(shifts, 1, b)
        real = later(fr, amount)
        imag = later(fi, amount)
        moved[b, 0] = real
        moved[b, 1] = imag
        if b < shifted.shape[0]:
            cosine0[b] = cosine
            sine0[b] = sine
            shifted[b, 0] = real
            shifted[b, 1] = imag
    for b in range(bands):
        lr, li = fir(moved[b, 0], moved[b, 1], of(high, b)[...], of(low, b)[...])
        linear1[b, 0] = lr
        linear1[b, 1] = li
    inside = slice(PAD, PAD + rows)
    powers = (linear1[b, 0, inside] ** 2 + linear1[b, 1, inside] ** 2 for b in range(bands))
    scatter_delayed(powers, delays, 1, held_out, out)


def k_third(
    delays, gains, linear1, own, odd_in, even_in, cotangent, turned1, out, spread, held, held_out
):
    bands = linear1.shape[0]
    rows = linear1.shape[2] - 2 * PAD
    values = gather_spread(own, even_in, odd_in, spread, rows)
    terms = []
    for b, spread_b in enumerate(read_spread(values, delays, 1, held, rows)):
        gain = at(gains, 1, b)
        sine, cosine = sine_cosine(gain * spread_b)
        gr, gi = cotangent[b, 0], cotangent[b, 1]
        er = gr * cosine + gi * sine
        ei = gi * cosine - gr * sine
        turned1[b, 0] = er
        turned1[b, 1] = ei
        term = ei * linear1[b, 0] - er * linear1[b, 1]
        terms.append(gain * term[PAD : PAD + rows])
    scatter_delayed(terms, delays, 1, held_out, out)


def k_fourth(
    delays, shifts, gains, turned1, linear1, own, odd_in, even_in, high, low, cosine0, sine0, field1,
    grad1, turned0, out, spread, moved, held, held_out,
):
    bands = linear1.shape[0]
    rows = linear1.shape[2] - 2 * PAD
    values = gather_spread(own, even_in, odd_in, spread, rows)
    for b, spread_b in enumerate(read_spread(values, delays, 1, held, rows)):
        twice = 2.0 * spread_b
        gr = keep_inside(turned1[b, 0] + linear1[b, 0] * twice, rows)
        gi = keep_inside(turned1[b, 1] + linear1[b, 1] * twice, rows)
        moved[b, 0] = gr
        moved[b, 1] = gi
        if b < grad1.shape[0]:
            grad1[b, 0] = gr
            grad1[b, 1] = gi
    for b in range(bands):
        gr, gi = fir_adjoint(moved[b, 0], moved[b, 1], of(high, b)[...], of(low, b)[...])
        moved[b, 0] = gr
        moved[b, 1] = gi
    terms = []
    for b in range(bands):
        amount = LANES // 2 - at(shifts, 1, b)
        gr = earlier(moved[b, 0], amount)
        gi = earlier(moved[b, 1], amount)
        if b < grad1.shape[0]:
            cosine, sine = cosine0[b], sine0[b]
            turned0[b, 0] = gr * cosine + gi * sine
            turned0[b, 1] = gi * cosine - gr * sine
        term = gi * field1[b, 0] - gr * field1[b, 1]
        terms.append(at(gains, 0, b) * term[PAD : PAD + rows])
    scatter_delayed(terms, delays, 0, held_out, out)


def correlate(real, imag, grad_real, grad_imag, rows):
    inside = slice(PAD, PAD + rows)
    following = slice(PAD + 1, PAD + rows + 1)
    a = jnp.concatenate(
        [
            jnp.concatenate([real[inside], real[following]], 1),
            jnp.concatenate([imag[inside], imag[following]], 1),
        ],
        0,
    )
    gr, gi = grad_real[inside], grad_imag[inside]
    d = jnp.concatenate([jnp.concatenate([gr, gi], 1), jnp.concatenate([gi, -gr], 1)], 0)
    ah, al = split(a)
    dh, dl = split(d)
    table = lax.dot_general(
        jnp.concatenate([dh, dh, dl], 0),
        jnp.concatenate([ah, al, ah], 0),
        (((0,), (0,)), ((), ())),
        preferred_element_type=F32,
    )
    width = 2 * LANES
    results = []
    for c in range(2):
        acc = table[c * LANES : c * LANES + 8]
        for g in range(1, LANES // 8):
            first = c * LANES + 8 * g
            acc = acc + pltpu.roll(table[first : first + 8], width - 8 * g, 1)
        total = acc[0:1]
        for s in range(1, 8):
            total = total + pltpu.roll(acc, width - s, 1)[s : s + 1]
        results.append(total[:, :LANES])
    return results


def k_taps(shifted, grad, out):
    bands = grad.shape[0]
    rows = grad.shape[2] - 2 * PAD
    for b in range(bands):
        parts = correlate(shifted[b, 0], shifted[b, 1], grad[b, 0], grad[b, 1], rows)
        for c in range(2):
            out[2 * b + c : 2 * b + c + 1, :] = parts[c]


def k_fifth(
    scale, delays, turned0, linear0, own, odd_in, even_in, shifted, taps1,
    grad0, out, spread, held,
):
    bands = turned0.shape[0]
    rows = turned0.shape[2] - 2 * PAD
    values = gather_spread(own, even_in, odd_in, spread, rows)
    for b, spread_b in enumerate(read_spread(values, delays, 0, held, rows)):
        twice = 2.0 * spread_b
        gr = keep_inside(turned0[b, 0] + linear0[b, 0] * twice, rows)
        gi = keep_inside(turned0[b, 1] + linear0[b, 1] * twice, rows)
        grad0[b, 0] = gr
        grad0[b, 1] = gi
        parts = correlate(shifted[b, 0], shifted[b, 1], gr, gi, rows)
        for c in range(2):
            out[2 * b + c : 2 * b + c + 1, :] = parts[c] * scale
    out[2 * bands :, :] = taps1[...] * scale


def k_last(shifts, grad0, high, low, result):
    bands = grad0.shape[0]
    rows = grad0.shape[2] - 2 * PAD
    for b in range(bands):
        gr, gi = fir_adjoint(grad0[b, 0], grad0[b, 1], high[b], low[b])
        amount = LANES // 2 - at(shifts, 0, b)
        gr = earlier(gr, amount)[PAD : PAD + rows]
        gi = earlier(gi, amount)[PAD : PAD + rows]
        for r in range(rows):
            result[b, 0, 0:1, r * LANES : (r + 1) * LANES] = gr[r : r + 1]
            result[b, 0, 1:2, r * LANES : (r + 1) * LANES] = gi[r : r + 1]


COST = {
    "k_setup": 0.01, "k_first": 0.75, "k_beside": 0.01, "k_cotangent": 0.1, "k_second": 6.0,
    "k_third": 0.7, "k_fourth": 1.0, "k_taps": 1.1, "k_fifth": 1.0, "k_last": 1.1,
}


def call(kernel, arrays, shapes, scratch=()):
    named = kernel.func if isinstance(kernel, functools.partial) else kernel
    micros = COST.get(named.__name__, 0.1)
    vmem = pl.BlockSpec(memory_space=pltpu.VMEM)
    return pl.pallas_call(
        kernel,
        out_shape=shapes,
        in_specs=jax.tree.map(lambda _: vmem, arrays),
        out_specs=[vmem] * len(shapes),
        scratch_shapes=[pltpu.VMEM(s, F32) for s in scratch],
        compiler_params=pltpu.CompilerParams(vmem_limit_bytes=24 * 1024 * 1024),
        cost_estimate=pl.CostEstimate(
            flops=int(micros * 1e8), bytes_accessed=int(micros * 3e6), transcendentals=0
        ),
    )(*arrays)


def swapped(x, axis, partner, cross):
    size, cores = lax.axis_size(axis), lax.axis_size("pol")
    pairs = []
    for i in range(size):
        for p in range(cores):
            j, q = partner(i), cores - 1 - p
            if 0 <= j < size:
                pairs.append((i * cores + p, j * cores + (q if cross else p)))
            else:
                pairs.append((i * cores + p, i * cores + q))
    return lax.ppermute(x, (axis, "pol"), pairs)


def summed(x, axis, cross=True):
    size = lax.axis_size(axis)
    if size & (size - 1):
        return lax.psum(x, axis)
    distance = 1
    while distance < size:
        x = x + swapped(x, axis, lambda i, d=distance: i ^ d, cross)
        distance *= 2
    return x


def over_cores(x):
    cores = lax.axis_size("pol")
    return x + lax.ppermute(x, "pol", [(p, cores - 1 - p) for p in range(cores)])


def evenly(i):
    return i ^ 1


def oddly(i):
    return ((i + 1) ^ 1) - 1


def neighbours(even_out, odd_out, cross):
    odd_in = swapped(odd_out, "tm", oddly, cross)
    even_in = swapped(even_out, "tm", evenly, cross)
    return even_in, odd_in


def aslant(x, partner):
    size, cores = lax.axis_size("tm"), lax.axis_size("pol")
    pairs = []
    for i in range(size):
        for b in range(2):
            for p in range(cores):
                here = (i * 2 + b) * cores
                j = partner(i)
                if 0 <= j < size:
                    pairs.append((here + p, (j * 2 + 1 - b) * cores + p))
                else:
                    pairs.append((here + p, here + cores - 1 - p))
    return lax.ppermute(x, ("tm", "band", "pol"), pairs)


def over_tm(x):
    if lax.axis_size("tm") != 4:
        return summed(x, "tm")
    others = [swapped(x, "tm", lambda i, d=d: i ^ d, True) for d in (1, 2, 3)]
    return (x + others[0]) + (others[1] + others[2])


def exchanged(part, doubled):
    part = over_cores(part)
    part = part if doubled else summed(part, "band")
    return (part,) + neighbours(part, part, True)[::-1]


def on_device(signal, cotangent, taps, gains, walk_off, tap_shift):
    own, _, _, length = signal.shape
    steps = taps.shape[0]
    rows = length // LANES
    held_rows = rows + 2 * PAD
    doubled = lax.axis_size("band") == 2
    groups = 2 if doubled else 1
    bands = groups * own

    def shape(*dims, dtype=F32):
        return jax.ShapeDtypeStruct(dims, dtype)

    field = shape(bands, 2, held_rows, LANES)
    own_field = shape(own, 2, held_rows, LANES)
    angle = shape(own, held_rows, LANES)
    wide_part = shape(rows + REACH + 2 * PAD, LANES)
    part = shape(rows + REACH, LANES)
    table = shape(own, 2 * LANES, 2 * LANES, dtype=BF16)
    ext_wide = (own, 2, rows + 2 * WIDE_PAD, LANES)
    held_wide = (own, rows + 2 * WIDE_PAD + 8, LANES)
    spread = (rows + REACH + 2 * PAD, LANES)
    moved = (bands, 2, held_rows, LANES)
    held_in = (bands, rows + REACH + 3 * PAD, LANES)
    held_own = (own, rows + REACH + 3 * PAD, LANES)
    held_out = (bands, rows + 3 * REACH, LANES)

    inputs = (signal, cotangent, taps, walk_off, tap_shift, gains)
    hbm, vmem = (pl.BlockSpec(memory_space=m) for m in (pltpu.HBM, pltpu.VMEM))
    cut = shape(own, 2, (WIDE + EDGE) * LANES)
    near = shape(own, 2, 2 * EDGE * LANES)
    pack_rows = 2 * own * rows + 2 * steps * own + 3 * steps
    pack = shape(pack_rows + -pack_rows % 8, LANES)
    even_out, odd_out, even_near, odd_near, pack_out, cot_out = pl.pallas_call(
        k_begin,
        out_shape=[cut, cut, near, near, pack, shape(own, 2, rows, LANES)],
        in_specs=[hbm] * len(inputs),
        out_specs=[vmem] * 6,
        scratch_shapes=[pltpu.VMEM(a.shape, a.dtype) for a in inputs]
        + [pltpu.SemaphoreType.DMA((len(inputs),))],
        compiler_params=pltpu.CompilerParams(vmem_limit_bytes=24 * 1024 * 1024),
        cost_estimate=pl.CostEstimate(flops=10**8, bytes_accessed=10**6, transcendentals=0),
    )(*(pltpu.with_memory_space_constraint(a, pltpu.HBM) for a in inputs))

    packs = [pack_out]
    sides = [neighbours(even_out, odd_out, False)]
    if doubled:
        packs.append(swapped(pack_out, "band", evenly, False))
        sides.append((aslant(even_near, evenly), aslant(odd_near, oddly)))
    tiny = [shape(steps, own, dtype=d) for d in (jnp.int32, jnp.int32, F32)]
    setup = functools.partial(k_setup, steps, rows)
    made = [call(setup, (p,), tiny + [table] * (2 * steps)) for p in packs]
    delays, shifts, gains, high0, low0, high1, low1 = (list(m) for m in zip(*made))

    shifted0, linear, sent = call(
        k_first, (delays[:1], shifts[:1], pack_out, sides[0], high0[0], low0[0]),
        [own_field, own_field, wide_part], (ext_wide, held_wide),
    )
    sent, sides = lax.optimization_barrier((sent, sides))
    sent = over_cores(sent)
    cots, first_cot = [cot_out], [WIDE]
    if doubled:
        cots.append(swapped(cot_out, "band", evenly, False))
        first_cot.append(EDGE)
    spread0 = summed(sent, "band")
    linear0 = [linear]
    if doubled:
        linear0 += call(
            k_beside, (shifts[1:], packs[1], sides[1], high0[1], low0[1]), [own_field],
            ((own, 2, held_rows, LANES),),
        )
    (cot_rows,) = call(
        lambda c, s, out: k_cotangent(c, s, first_cot, out), (cots, sides), [field]
    )
    cosine0, sine0, field1, shifted1, linear1, sent = call(
        k_second, (delays, shifts, gains, linear0, spread0, high1, low1),
        [angle, angle, field, own_field, field, part], (moved, held_in, held_out),
    )
    turned1, sent = call(
        k_third, (delays, gains, linear1, *exchanged(sent, doubled), cot_rows),
        [field, part], (spread, held_in, held_out),
    )
    grad1, turned0, sent = call(
        k_fourth,
        (delays, shifts, gains, turned1, linear1, *exchanged(sent, doubled), high1, low1,
         cosine0, sine0, field1),
        [own_field, own_field, part], (spread, moved, held_in, held_out),
    )
    (taps1,) = call(k_taps, (shifted1, grad1), [shape(2 * own, LANES)])
    scale = 1.0 / math.sqrt(2.0 * length * lax.axis_size("tm"))
    grad0, grad_taps = call(
        functools.partial(k_fifth, scale),
        (delays[:1], turned0, linear, *exchanged(sent, doubled), shifted0, taps1),
        [own_field, shape(steps * 2 * own, LANES)], (spread, held_own),
    )
    (grad_signal,) = call(
        k_last, (shifts[:1], grad0, high0[0], low0[0]), [shape(own, 1, 2, length)]
    )
    grad_taps = over_tm(over_cores(grad_taps))
    return grad_signal, grad_taps.reshape(steps, own, 2, LANES)


def solution(mesh):
    return jax.shard_map(
        on_device,
        mesh=mesh,
        in_specs=(
            P(("groups", "band"), "pol", None, "tm"),
            P(("groups", "band"), "pol", None, "tm"),
            P(None, "band", None, None),
            P(None, "band"),
            P(None, "band"),
            P(None, "band"),
        ),
        out_specs=(P(("groups", "band"), "pol", None, "tm"), P("groups", "band", None, None)),
        check_vma=False,
    )
```

```python
import functools
import math

import jax
import jax.numpy as jnp
from jax import lax
from jax.experimental import pallas as pl
from jax.experimental.pallas import tpu as pltpu
from jax.sharding import PartitionSpec as P

LANES = 128
REACH = 2048 // LANES
EDGE = 4
WIDE = REACH + 4
PAD = 8
WIDE_PAD = REACH + PAD
F32 = jnp.float32
BF16 = jnp.bfloat16

TWO_OVER_PI = 2.0 / math.pi
HALF_PI_1 = 1.5625
HALF_PI_2 = 67.0 / 8192.0
HALF_PI_3 = 123.0 / 1048576.0
HALF_PI_4 = math.pi / 2.0 - HALF_PI_1 - HALF_PI_2 - HALF_PI_3


def split(x):
    high = x.astype(BF16)
    return high, (x - high.astype(F32)).astype(BF16)


def sine_cosine(x):
    turns = jnp.floor(x * TWO_OVER_PI + 0.5)
    quadrant = turns.astype(jnp.int32)
    r = x - turns * HALF_PI_1
    r = r - turns * HALF_PI_2
    r = r - turns * HALF_PI_3
    r = r - turns * HALF_PI_4
    r2 = r * r
    s = r + r * r2 * (-1.6666654611e-1 + r2 * (8.3321608736e-3 + r2 * -1.9515295891e-4))
    c = 1.0 - 0.5 * r2 + r2 * r2 * (
        4.166664568298827e-2 + r2 * (-1.388731625493765e-3 + r2 * 2.443315711809948e-5)
    )
    odd = (quadrant & 1) == 1
    sine = jnp.where(odd, c, s)
    cosine = jnp.where(odd, s, c)
    sine = jnp.where((quadrant & 2) == 2, -sine, sine)
    cosine = jnp.where(((quadrant + 1) & 2) == 2, -cosine, cosine)
    return sine, cosine


def lanes_of(shape):
    return lax.broadcasted_iota(jnp.int32, shape, len(shape) - 1)


def later(x, amount):
    rolled = pltpu.roll(x, amount & (LANES - 1), 1)
    return jnp.where(lanes_of(x.shape) >= amount, rolled, pltpu.roll(rolled, 1, 0))


def earlier(x, amount):
    rows = x.shape[0]
    rolled = pltpu.roll(x, (LANES - amount) & (LANES - 1), 1)
    follow = pltpu.roll(rolled, rows - 1, 0)
    return jnp.where(lanes_of(x.shape) + amount < LANES, rolled, follow)


def at(table, step, b):
    own = table[0].shape[1]
    return table[b // own][step, b % own]


def of(groups, b):
    own = groups[0].shape[0]
    return groups[b // own].at[b % own]


def is_even():
    return lax.rem(lax.axis_index("tm"), 2) == 0


def keep_inside(values, rows, pad=PAD):
    z = lax.axis_index("tm")
    row = lax.broadcasted_iota(jnp.int32, values.shape, 0)
    low = jnp.where(z == 0, pad, 0)
    high = jnp.where(z == lax.axis_size("tm") - 1, pad + rows, 2 * pad + rows)
    return jnp.where((row >= low) & (row < high), values, 0.0)


def from_sides(even_value, odd_value):
    z = lax.axis_index("tm")
    even = is_even()
    before = jnp.where(even, odd_value, even_value)
    after = jnp.where(even, even_value, odd_value)
    before = jnp.where(z == 0, 0.0, before)
    after = jnp.where(z == lax.axis_size("tm") - 1, 0.0, after)
    return before, after


def extend(out, b, even_in, odd_in, first, edge):
    own = even_in.shape[0]
    rows = out.shape[2]
    pad = edge + 4
    for c in range(2):
        out[b, c, 0:8, :] = jnp.zeros((8, LANES), F32)
        out[b, c, rows - 8 :, :] = jnp.zeros((8, LANES), F32)
    for r in range(edge):
        lanes = slice((first + r) * LANES, (first + r + 1) * LANES)
        before, after = from_sides(even_in[b % own, :, lanes], odd_in[b % own, :, lanes])
        for c in range(2):
            above = pad - edge + r
            below = rows - pad + r
            out[b, c, above : above + 1, :] = before[c : c + 1]
            out[b, c, below : below + 1, :] = after[c : c + 1]


def three_passes(x, high, low, transposed):
    rows = x.shape[0]
    xh, xl = split(x)
    contract = (((1,), (1 if transposed else 0,)), ((), ()))
    both = lax.dot_general(jnp.concatenate([xh, xl], 0), high, contract, preferred_element_type=F32)
    rest = lax.dot_general(xh, low, contract, preferred_element_type=F32)
    return both[:rows] + both[rows:] + rest


def fir(real, imag, high, low):
    rows = real.shape[0]
    x = [jnp.concatenate([part, pltpu.roll(part, rows - 1, 0)], 1) for part in (real, imag)]
    y = three_passes(jnp.concatenate(x, 0), high, low, True)
    first, second = y[:rows], y[rows:]
    return first[:, :LANES] - second[:, LANES:], first[:, LANES:] + second[:, :LANES]


def fir_adjoint(real, imag, high, low):
    rows = real.shape[0]
    x = [jnp.concatenate([real, imag], 1), jnp.concatenate([imag, -real], 1)]
    g = three_passes(jnp.concatenate(x, 0), high, low, False)
    parts = (g[:rows], g[rows:])
    return [part[:, :LANES] + pltpu.roll(part[:, LANES:], 1, 0) for part in parts]


def scatter_delayed(values, delays, step, held, out):
    bands = held.shape[0]
    base = REACH + 8
    total = out.shape[0]
    rows = total - REACH
    lane = lanes_of((total, LANES))
    parts = []
    for b, value in enumerate(values):
        delay = at(delays, step, b)
        parts.append((lax.shift_right_logical(delay, 7), delay & (LANES - 1)))
        held[b, 0:base, :] = jnp.zeros((base, LANES), F32)
        held[b, base : base + rows, :] = pltpu.roll(value, parts[b][1], 1)
        held[b, base + rows :, :] = jnp.zeros((held.shape[1] - base - rows, LANES), F32)
    acc = None
    for b, (q, s) in enumerate(parts):
        near = held[b, pl.ds(base - q, total), :]
        far = held[b, pl.ds(base - q - 1, total), :]
        part = jnp.where(lane >= s, near, far)
        acc = part if acc is None else acc + part
    out[...] = acc


def delayed_sum(values, delays, step, held, out):
    bands = len(values)
    count, total = values[0].shape[0], out.shape[0]
    lane = lanes_of((total, LANES))
    acc = None
    for b in range(bands):
        delay = at(delays, step, b)
        q = lax.shift_right_logical(delay, 7)
        s = delay & (LANES - 1)
        held[b, 0:8, :] = jnp.zeros((8, LANES), F32)
        held[b, 8 : 8 + count, :] = pltpu.roll(values[b], s, 1)
        near = held[b, pl.ds(8 + REACH - q, total), :]
        far = held[b, pl.ds(8 + REACH - q - 1, total), :]
        part = jnp.where(lane >= s, near, far)
        acc = part if acc is None else acc + part
    out[...] = acc


def end_at_last(values, rows):
    row = lax.broadcasted_iota(jnp.int32, values.shape, 0)
    last = lax.axis_index("tm") == lax.axis_size("tm") - 1
    return jnp.where(row < jnp.where(last, PAD + rows, values.shape[0]), values, 0.0)


def gather_spread(own, even_in, odd_in, spread, rows):
    before, after = from_sides(even_in[...], odd_in[...])
    total = rows + REACH + 2 * PAD
    spread[0:PAD, :] = before[rows - PAD : rows]
    spread[PAD:total - PAD, :] = own[...]
    spread[total - PAD : total, :] = after[REACH : REACH + PAD]
    spread[PAD : PAD + REACH, :] += before[rows : rows + REACH]
    spread[PAD + rows : PAD + rows + REACH, :] += after[0:REACH]
    return end_at_last(spread[...], rows)


def read_spread(values, delays, step, held, rows):
    bands, total = held.shape[0], values.shape[0]
    count = rows + 2 * PAD
    lane = lanes_of((count, LANES))
    parts = []
    for b in range(bands):
        delay = at(delays, step, b)
        parts.append((lax.shift_right_logical(delay, 7), delay & (LANES - 1)))
    for b, (_, s) in enumerate(parts):
        held[b, 0:total, :] = pltpu.roll(values, (LANES - s) & (LANES - 1), 1)
        held[b, total:, :] = jnp.zeros((held.shape[1] - total, LANES), F32)
    for b, (q, s) in enumerate(parts):
        near = held[b, pl.ds(q, count), :]
        far = held[b, pl.ds(q + 1, count), :]
        yield jnp.where(lane + s < LANES, near, far)


def k_begin(
    signal, cotangent, taps, delays, shifts, gains,
    even_out, odd_out, even_near, odd_near, sent, cot_rows,
    sig_held, cot_held, taps_held, delays_held, shifts_held, gains_held, done,
):
    steps, bands = taps.shape[:2]
    rows = cot_rows.shape[2]
    pairs = (
        (signal, sig_held), (cotangent, cot_held), (taps, taps_held),
        (delays, delays_held), (shifts, shifts_held), (gains, gains_held),
    )
    copies = [pltpu.make_async_copy(a, b, done.at[n]) for n, (a, b) in enumerate(pairs)]
    for copy in copies:
        copy.start()
    for copy in copies[:2]:
        copy.wait()
    even = is_even()
    length, wide, edge = rows * LANES, WIDE * LANES, EDGE * LANES
    for b in range(bands):
        for targets, held, first, width in (
            ((even_out, odd_out), sig_held, 0, wide),
            ((even_out, odd_out), cot_held, wide, edge),
            ((even_near, odd_near), sig_held, 0, edge),
            ((even_near, odd_near), cot_held, edge, edge),
        ):
            left = held[b, 0, :, 0:width]
            right = held[b, 0, :, length - width : length]
            targets[0][b, :, first : first + width] = jnp.where(even, right, left)
            targets[1][b, :, first : first + width] = jnp.where(even, left, right)
        for r in range(rows):
            lanes = slice(r * LANES, (r + 1) * LANES)
            pair = sig_held[b, 0, :, lanes]
            other = cot_held[b, 0, :, lanes]
            for c in range(2):
                row = (2 * b + c) * rows + r
                sent[row : row + 1, :] = pair[c : c + 1]
                cot_rows[b, c, r : r + 1, :] = other[c : c + 1]
    for copy in copies[2:]:
        copy.wait()
    first = 2 * bands * rows
    for step in range(steps):
        for b in range(bands):
            row = first + 2 * (step * bands + b)
            sent[row : row + 2, :] = taps_held[step, b]
    first = first + 2 * steps * bands
    sent[first:, :] = jnp.zeros((sent.shape[0] - first, LANES), F32)
    for k, held in enumerate((delays_held, shifts_held, gains_held)):
        row = first + k * steps
        sent[row : row + steps, 0:bands] = held[...].astype(F32)


def k_setup(steps, rows, pack, delays, shifts, gains, *tables):
    bands = delays.shape[1]
    shape = (LANES, LANES)
    diagonal = lanes_of(shape) >= lax.broadcasted_iota(jnp.int32, shape, 0)
    base = 2 * bands * rows
    first = base + 2 * steps * bands
    for n, target in enumerate((delays, shifts, gains)):
        row = first + n * steps
        target[...] = pack[row : row + steps, 0:bands].astype(target.dtype)
    for b in range(bands):
        for step in range(steps):
            high, low = tables[2 * step : 2 * step + 2]
            for c in range(2):
                tap = base + 2 * (step * bands + b) + c
                row = jnp.broadcast_to(pack[tap : tap + 1, :], shape)
                ring = pltpu.roll(row, 0, 1, stride=1, stride_axis=0)
                near = jnp.where(diagonal, ring, 0.0)
                rows_of = slice(c * LANES, (c + 1) * LANES)
                for place, half in enumerate((near, ring - near)):
                    lanes = slice(place * LANES, (place + 1) * LANES)
                    high[b, rows_of, lanes], low[b, rows_of, lanes] = split(half)


def k_cotangent(cots, sides, first, out):
    own = cots[0].shape[0]
    rows = out.shape[2] - 2 * PAD
    for b in range(out.shape[0]):
        k = b // own
        extend(out, b, *sides[k], first[k], EDGE)
        for c in range(2):
            out[b, c, PAD : PAD + rows, :] = cots[k][b % own, c]


def widened(ext, pack, sides, edge, b):
    pad = edge + 4
    rows = ext.shape[2] - 2 * pad
    extend(ext, b, *sides, 0, edge)
    for c in range(2):
        row = (2 * b + c) * rows
        ext[b, c, pad : pad + rows, :] = pack[row : row + rows, :]


def k_first(delays, shifts, pack, sides, high, low, shifted, linear, out, ext, held):
    bands = linear.shape[0]
    rows = linear.shape[2] - 2 * PAD
    middle = slice(WIDE_PAD - PAD, WIDE_PAD + rows + PAD)
    powers = []
    for b in range(bands):
        widened(ext, pack, sides, WIDE, b)
        amount = LANES // 2 - at(shifts, 0, b)
        real = later(ext[b, 0], amount)
        imag = later(ext[b, 1], amount)
        shifted[b, 0] = real[middle]
        shifted[b, 1] = imag[middle]
        lr, li = fir(real, imag, high[b], low[b])
        linear[b, 0] = lr[middle]
        linear[b, 1] = li[middle]
        powers.append(keep_inside(lr * lr + li * li, rows, WIDE_PAD))
    delayed_sum(powers, delays, 0, held, out)


def k_beside(shifts, pack, sides, high, low, linear, ext):
    for b in range(linear.shape[0]):
        widened(ext, pack, sides, EDGE, b)
        amount = LANES // 2 - at(shifts, 0, b)
        real = later(ext[b, 0], amount)
        imag = later(ext[b, 1], amount)
        lr, li = fir(real, imag, high[b], low[b])
        linear[b, 0] = lr
        linear[b, 1] = li


def k_second(
    delays, shifts, gains, linear0, own, high, low,
    cosine0, sine0, field1, shifted, linear1, out, moved, held, held_out,
):
    bands = linear1.shape[0]
    rows = linear1.shape[2] - 2 * PAD
    values = end_at_last(own[...], rows)
    for b, spread in enumerate(read_spread(values, delays, 0, held, rows)):
        sine, cosine = sine_cosine(at(gains, 0, b) * spread)
        linear = of(linear0, b)
        lr, li = linear[0], linear[1]
        fr = keep_inside(lr * cosine - li * sine, rows)
        fi = keep_inside(lr * sine + li * cosine, rows)
        field1[b, 0] = fr
        field1[b, 1] = fi
        amount = LANES // 2 - at(shifts, 1, b)
        real = later(fr, amount)
        imag = later(fi, amount)
        moved[b, 0] = real
        moved[b, 1] = imag
        if b < shifted.shape[0]:
            cosine0[b] = cosine
            sine0[b] = sine
            shifted[b, 0] = real
            shifted[b, 1] = imag
    for b in range(bands):
        lr, li = fir(moved[b, 0], moved[b, 1], of(high, b)[...], of(low, b)[...])
        linear1[b, 0] = lr
        linear1[b, 1] = li
    inside = slice(PAD, PAD + rows)
    powers = (linear1[b, 0, inside] ** 2 + linear1[b, 1, inside] ** 2 for b in range(bands))
    scatter_delayed(powers, delays, 1, held_out, out)


def k_third(
    delays, gains, linear1, own, odd_in, even_in, cotangent, turned1, out, spread, held, held_out
):
    bands = linear1.shape[0]
    rows = linear1.shape[2] - 2 * PAD
    values = gather_spread(own, even_in, odd_in, spread, rows)
    terms = []
    for b, spread_b in enumerate(read_spread(values, delays, 1, held, rows)):
        gain = at(gains, 1, b)
        sine, cosine = sine_cosine(gain * spread_b)
        gr, gi = cotangent[b, 0], cotangent[b, 1]
        er = gr * cosine + gi * sine
        ei = gi * cosine - gr * sine
        turned1[b, 0] = er
        turned1[b, 1] = ei
        term = ei * linear1[b, 0] - er * linear1[b, 1]
        terms.append(gain * term[PAD : PAD + rows])
    scatter_delayed(terms, delays, 1, held_out, out)


def k_fourth(
    delays, shifts, gains, turned1, linear1, own, odd_in, even_in, high, low, cosine0, sine0, field1,
    grad1, turned0, out, spread, moved, held, held_out,
):
    bands = linear1.shape[0]
    rows = linear1.shape[2] - 2 * PAD
    values = gather_spread(own, even_in, odd_in, spread, rows)
    for b, spread_b in enumerate(read_spread(values, delays, 1, held, rows)):
        twice = 2.0 * spread_b
        gr = keep_inside(turned1[b, 0] + linear1[b, 0] * twice, rows)
        gi = keep_inside(turned1[b, 1] + linear1[b, 1] * twice, rows)
        moved[b, 0] = gr
        moved[b, 1] = gi
        if b < grad1.shape[0]:
            grad1[b, 0] = gr
            grad1[b, 1] = gi
    for b in range(bands):
        gr, gi = fir_adjoint(moved[b, 0], moved[b, 1], of(high, b)[...], of(low, b)[...])
        moved[b, 0] = gr
        moved[b, 1] = gi
    terms = []
    for b in range(bands):
        amount = LANES // 2 - at(shifts, 1, b)
        gr = earlier(moved[b, 0], amount)
        gi = earlier(moved[b, 1], amount)
        if b < grad1.shape[0]:
            cosine, sine = cosine0[b], sine0[b]
            turned0[b, 0] = gr * cosine + gi * sine
            turned0[b, 1] = gi * cosine - gr * sine
        term = gi * field1[b, 0] - gr * field1[b, 1]
        terms.append(at(gains, 0, b) * term[PAD : PAD + rows])
    scatter_delayed(terms, delays, 0, held_out, out)


def correlate(real, imag, grad_real, grad_imag, rows):
    inside = slice(PAD, PAD + rows)
    following = slice(PAD + 1, PAD + rows + 1)
    a = jnp.concatenate(
        [
            jnp.concatenate([real[inside], real[following]], 1),
            jnp.concatenate([imag[inside], imag[following]], 1),
        ],
        0,
    )
    gr, gi = grad_real[inside], grad_imag[inside]
    d = jnp.concatenate([jnp.concatenate([gr, gi], 1), jnp.concatenate([gi, -gr], 1)], 0)
    ah, al = split(a)
    dh, dl = split(d)
    table = lax.dot_general(
        jnp.concatenate([dh, dh, dl], 0),
        jnp.concatenate([ah, al, ah], 0),
        (((0,), (0,)), ((), ())),
        preferred_element_type=F32,
    )
    width = 2 * LANES
    results = []
    for c in range(2):
        acc = table[c * LANES : c * LANES + 8]
        for g in range(1, LANES // 8):
            first = c * LANES + 8 * g
            acc = acc + pltpu.roll(table[first : first + 8], width - 8 * g, 1)
        total = acc[0:1]
        for s in range(1, 8):
            total = total + pltpu.roll(acc, width - s, 1)[s : s + 1]
        results.append(total[:, :LANES])
    return results


def k_taps(shifted, grad, out):
    bands = grad.shape[0]
    rows = grad.shape[2] - 2 * PAD
    for b in range(bands):
        parts = correlate(shifted[b, 0], shifted[b, 1], grad[b, 0], grad[b, 1], rows)
        for c in range(2):
            out[2 * b + c : 2 * b + c + 1, :] = parts[c]


def k_fifth(
    scale, delays, turned0, linear0, own, odd_in, even_in, shifted, taps1,
    grad0, out, spread, held,
):
    bands = turned0.shape[0]
    rows = turned0.shape[2] - 2 * PAD
    values = gather_spread(own, even_in, odd_in, spread, rows)
    for b, spread_b in enumerate(read_spread(values, delays, 0, held, rows)):
        twice = 2.0 * spread_b
        gr = keep_inside(turned0[b, 0] + linear0[b, 0] * twice, rows)
        gi = keep_inside(turned0[b, 1] + linear0[b, 1] * twice, rows)
        grad0[b, 0] = gr
        grad0[b, 1] = gi
        parts = correlate(shifted[b, 0], shifted[b, 1], gr, gi, rows)
        for c in range(2):
            out[2 * b + c : 2 * b + c + 1, :] = parts[c] * scale
    out[2 * bands :, :] = taps1[...] * scale


def k_last(shifts, grad0, high, low, result):
    bands = grad0.shape[0]
    rows = grad0.shape[2] - 2 * PAD
    for b in range(bands):
        gr, gi = fir_adjoint(grad0[b, 0], grad0[b, 1], high[b], low[b])
        amount = LANES // 2 - at(shifts, 0, b)
        gr = earlier(gr, amount)[PAD : PAD + rows]
        gi = earlier(gi, amount)[PAD : PAD + rows]
        for r in range(rows):
            result[b, 0, 0:1, r * LANES : (r + 1) * LANES] = gr[r : r + 1]
            result[b, 0, 1:2, r * LANES : (r + 1) * LANES] = gi[r : r + 1]


def call(kernel, arrays, shapes, scratch=(), micros=2.0):
    vmem = pl.BlockSpec(memory_space=pltpu.VMEM)
    return pl.pallas_call(
        kernel,
        out_shape=shapes,
        in_specs=jax.tree.map(lambda _: vmem, arrays),
        out_specs=[vmem] * len(shapes),
        scratch_shapes=[pltpu.VMEM(s, F32) for s in scratch],
        compiler_params=pltpu.CompilerParams(vmem_limit_bytes=24 * 1024 * 1024),
        cost_estimate=pl.CostEstimate(
            flops=int(micros * 1e8), bytes_accessed=int(micros * 3e6), transcendentals=0
        ),
    )(*arrays)


def swapped(x, axis, partner, cross):
    size, cores = lax.axis_size(axis), lax.axis_size("pol")
    pairs = []
    for i in range(size):
        for p in range(cores):
            j, q = partner(i), cores - 1 - p
            if 0 <= j < size:
                pairs.append((i * cores + p, j * cores + (q if cross else p)))
            else:
                pairs.append((i * cores + p, i * cores + q))
    return lax.ppermute(x, (axis, "pol"), pairs)


def summed(x, axis, cross=True):
    size = lax.axis_size(axis)
    if size & (size - 1):
        return lax.psum(x, axis)
    distance = 1
    while distance < size:
        x = x + swapped(x, axis, lambda i, d=distance: i ^ d, cross)
        distance *= 2
    return x


def over_cores(x):
    cores = lax.axis_size("pol")
    return x + lax.ppermute(x, "pol", [(p, cores - 1 - p) for p in range(cores)])


def evenly(i):
    return i ^ 1


def oddly(i):
    return ((i + 1) ^ 1) - 1


def neighbours(even_out, odd_out, cross):
    odd_in = swapped(odd_out, "tm", oddly, cross)
    even_in = swapped(even_out, "tm", evenly, cross)
    return even_in, odd_in


def aslant(x, partner):
    size, cores = lax.axis_size("tm"), lax.axis_size("pol")
    pairs = []
    for i in range(size):
        for b in range(2):
            for p in range(cores):
                here = (i * 2 + b) * cores
                j = partner(i)
                if 0 <= j < size:
                    pairs.append((here + p, (j * 2 + 1 - b) * cores + p))
                else:
                    pairs.append((here + p, here + cores - 1 - p))
    return lax.ppermute(x, ("tm", "band", "pol"), pairs)


def over_tm(x):
    if lax.axis_size("tm") != 4:
        return summed(x, "tm")
    others = [swapped(x, "tm", lambda i, d=d: i ^ d, True) for d in (1, 2, 3)]
    return (x + others[0]) + (others[1] + others[2])


def exchanged(part, doubled):
    part = over_cores(part)
    part = part if doubled else summed(part, "band")
    return (part,) + neighbours(part, part, True)[::-1]


def on_device(signal, cotangent, taps, gains, walk_off, tap_shift):
    own, _, _, length = signal.shape
    steps = taps.shape[0]
    rows = length // LANES
    held_rows = rows + 2 * PAD
    doubled = lax.axis_size("band") == 2
    groups = 2 if doubled else 1
    bands = groups * own

    def shape(*dims, dtype=F32):
        return jax.ShapeDtypeStruct(dims, dtype)

    field = shape(bands, 2, held_rows, LANES)
    own_field = shape(own, 2, held_rows, LANES)
    angle = shape(own, held_rows, LANES)
    wide_part = shape(rows + REACH + 2 * PAD, LANES)
    part = shape(rows + REACH, LANES)
    table = shape(own, 2 * LANES, 2 * LANES, dtype=BF16)
    ext_wide = (own, 2, rows + 2 * WIDE_PAD, LANES)
    held_wide = (own, rows + 2 * WIDE_PAD + 8, LANES)
    spread = (rows + REACH + 2 * PAD, LANES)
    moved = (bands, 2, held_rows, LANES)
    held_in = (bands, rows + REACH + 3 * PAD, LANES)
    held_own = (own, rows + REACH + 3 * PAD, LANES)
    held_out = (bands, rows + 3 * REACH, LANES)

    inputs = (signal, cotangent, taps, walk_off, tap_shift, gains)
    hbm, vmem = (pl.BlockSpec(memory_space=m) for m in (pltpu.HBM, pltpu.VMEM))
    cut = shape(own, 2, (WIDE + EDGE) * LANES)
    near = shape(own, 2, 2 * EDGE * LANES)
    pack_rows = 2 * own * rows + 2 * steps * own + 3 * steps
    pack = shape(pack_rows + -pack_rows % 8, LANES)
    even_out, odd_out, even_near, odd_near, pack_out, cot_out = pl.pallas_call(
        k_begin,
        out_shape=[cut, cut, near, near, pack, shape(own, 2, rows, LANES)],
        in_specs=[hbm] * len(inputs),
        out_specs=[vmem] * 6,
        scratch_shapes=[pltpu.VMEM(a.shape, a.dtype) for a in inputs]
        + [pltpu.SemaphoreType.DMA((len(inputs),))],
        compiler_params=pltpu.CompilerParams(vmem_limit_bytes=24 * 1024 * 1024),
        cost_estimate=pl.CostEstimate(flops=10**8, bytes_accessed=10**6, transcendentals=0),
    )(*(pltpu.with_memory_space_constraint(a, pltpu.HBM) for a in inputs))

    packs = [pack_out]
    sides = [neighbours(even_out, odd_out, False)]
    if doubled:
        packs.append(swapped(pack_out, "band", evenly, False))
        sides.append((aslant(even_near, evenly), aslant(odd_near, oddly)))
    tiny = [shape(steps, own, dtype=d) for d in (jnp.int32, jnp.int32, F32)]
    setup = functools.partial(k_setup, steps, rows)
    made = [call(setup, (p,), tiny + [table] * (2 * steps)) for p in packs]
    delays, shifts, gains, high0, low0, high1, low1 = (list(m) for m in zip(*made))

    shifted0, linear, sent = call(
        k_first, (delays[:1], shifts[:1], pack_out, sides[0], high0[0], low0[0]),
        [own_field, own_field, wide_part], (ext_wide, held_wide),
    )
    sent, sides = lax.optimization_barrier((sent, sides))
    sent = over_cores(sent)
    cots, first_cot = [cot_out], [WIDE]
    if doubled:
        cots.append(swapped(cot_out, "band", evenly, False))
        first_cot.append(EDGE)
    spread0 = summed(sent, "band")
    linear0 = [linear]
    if doubled:
        linear0 += call(
            k_beside, (shifts[1:], packs[1], sides[1], high0[1], low0[1]), [own_field],
            ((own, 2, held_rows, LANES),),
        )
    (cot_rows,) = call(
        lambda c, s, out: k_cotangent(c, s, first_cot, out), (cots, sides), [field]
    )
    cosine0, sine0, field1, shifted1, linear1, sent = call(
        k_second, (delays, shifts, gains, linear0, spread0, high1, low1),
        [angle, angle, field, own_field, field, part], (moved, held_in, held_out),
    )
    turned1, sent = call(
        k_third, (delays, gains, linear1, *exchanged(sent, doubled), cot_rows),
        [field, part], (spread, held_in, held_out),
    )
    grad1, turned0, sent = call(
        k_fourth,
        (delays, shifts, gains, turned1, linear1, *exchanged(sent, doubled), high1, low1,
         cosine0, sine0, field1),
        [own_field, own_field, part], (spread, moved, held_in, held_out),
    )
    (taps1,) = call(k_taps, (shifted1, grad1), [shape(2 * own, LANES)])
    scale = 1.0 / math.sqrt(2.0 * length * lax.axis_size("tm"))
    grad0, grad_taps = call(
        functools.partial(k_fifth, scale),
        (delays[:1], turned0, linear, *exchanged(sent, doubled), shifted0, taps1),
        [own_field, shape(steps * 2 * own, LANES)], (spread, held_own),
    )
    (grad_signal,) = call(
        k_last, (shifts[:1], grad0, high0[0], low0[0]), [shape(own, 1, 2, length)]
    )
    grad_taps = over_tm(over_cores(grad_taps))
    return grad_signal, grad_taps.reshape(steps, own, 2, LANES)


def solution(mesh):
    return jax.shard_map(
        on_device,
        mesh=mesh,
        in_specs=(
            P(("groups", "band"), "pol", None, "tm"),
            P(("groups", "band"), "pol", None, "tm"),
            P(None, "band", None, None),
            P(None, "band"),
            P(None, "band"),
            P(None, "band"),
        ),
        out_specs=(P(("groups", "band"), "pol", None, "tm"), P("groups", "band", None, None)),
        check_vma=False,
    )
```
